32 devices in a mesh: tower: 2 (over core), rows: 16 (over z, y, x).
Axes of the slice: x: 2, y: 2, z: 4, core: 2. Of those that a mesh axis runs over, the one named last changes fastest.
Arguments:
- tokens: bfloat16 [2, 4096, 768], P('tower', 'rows'), may hold values from -6 to 6
- query_segments: int32 [16, 256], P('rows'), may hold values from 0 to 3, never falling along the last dimension, each value on 1 to 96 neighbouring positions
- doc_lengths: int32 [16], P('rows'), may hold values from 1 to 256, 2560 in all
- bucket_table: int32 [511], replicated, may hold values from 0 to 31, as said below
- positives: int32 [16, 4], replicated, may hold values from 0 to 15
- gain_attn: float32 [768], replicated, may hold values from 0.1 to 1.9
- w_query_key: bfloat16 [768, 1536], replicated, may hold values from -0.109375 to 0.109375
- w_value: bfloat16 [768, 768], replicated, may hold values from -0.21875 to 0.21875
- w_attn_out: bfloat16 [768, 768], replicated, may hold values from -0.625 to 0.625
- rel_bias: float32 [32, 12], replicated, may hold values from -4 to 4
- gain_ff: float32 [768], replicated, may hold values from 0.1 to 1.9
- w_in: bfloat16 [768, 3072], replicated, may hold values from -0.21875 to 0.21875
- w_out: bfloat16 [3072, 768], replicated, may hold values from -0.1875 to 0.1875
- gain_final: float32 [768], replicated, may hold values from 0.1 to 1.9
- w_proj: bfloat16 [768, 768], replicated, may hold values from -0.21875 to 0.21875
Outputs:
- loss: float32 [], replicated
- tokens_grad: float32 [2, 4096, 768], P('tower', 'rows')
- gain_attn_grad: float32 [768], replicated
- w_query_key_grad: float32 [768, 1536], P('rows', 'tower')
- w_value_grad: float32 [768, 768], P('rows', 'tower')
- w_attn_out_grad: float32 [768, 768], P('rows', 'tower')
- rel_bias_grad: float32 [32, 12], replicated
- gain_ff_grad: float32 [768], replicated
- w_in_grad: float32 [768, 3072], P('rows', 'tower')
- w_out_grad: float32 [3072, 768], P('rows', 'tower')
- gain_final_grad: float32 [768], replicated
- w_proj_grad: float32 [768, 768], P('rows', 'tower')
The draws below stay inside these ranges and needn't reach their ends.
Inputs may be any that keep to these rules, and one draw needn't show every extreme that they name: `query_segments`: each row's ids do not fall; each of the 4 ids names 1 to 96 slots of the row, one exactly 96. `doc_lengths`: one document has exactly 256 tokens. `bucket_table`: entry m holds the bucket of the offset m - (255) of key position minus query position: magnitudes under 8 have their own buckets 0 to 7, larger magnitudes buckets 8 to 15 not falling with the magnitude; positive offsets add 16.
All inputs are finite; a program needn't handle non-finite values. No bound on the sum of `doc_lengths` on one device may be relied on, other than what follows from the above.
Results may differ from the reference program's by a relative error of at most 0.018.
Values may be sent and summed in bfloat16 or wider, within the bound.
A program may use at most 192 MiB of HBM per device.

```python
import math
import jax
import jax.numpy as jnp
import numpy as np
from jax import lax

D = 768
FF = 3072
HEADS = 12
HEAD = 64
BUCKETS = 32
SLOT = 256
QMOST = 96
QPR = 4
ROWS = 16
TOKENS = 4096


def draw_bucket_table(key, part):
    key = jax.random.fold_in(key, 5)
    gaps = jax.random.randint(key, (7,), 2, 2 + SLOT // 32)
    limits = 8 + jnp.cumsum(gaps)
    offset = jnp.arange(2 * SLOT - 1) - (SLOT - 1)
    distance = jnp.abs(offset)
    far_bucket = 8 + jnp.sum((distance[:, None] >= limits[None, :]).astype(jnp.int32), axis=1)
    bucket = jnp.where(distance < 8, distance, far_bucket)
    return (bucket + jnp.where(offset > 0, 16, 0)).astype(jnp.int32)


def touch_ends(drawn, own_key, smallest, largest):
    spot = [jax.random.randint(jax.random.fold_in(own_key, axis), (), 0, length) for axis, length in enumerate(drawn.shape)]
    widest = drawn.shape.index(max(drawn.shape))
    beside = spot[:widest] + [(spot[widest] + 1) % drawn.shape[widest]] + spot[widest + 1:]
    return drawn.at[tuple(spot)].set(smallest).at[tuple(beside)].set(largest)


def levels(key, extent, pieces, least, top_value):
    def one(dim, shards_of):
        draws = jax.random.uniform(jax.random.fold_in(jax.random.fold_in(key, 6), dim), (shards_of,), jnp.float32, least / len(pieces), top_value / len(pieces))
        return jnp.repeat(jnp.exp(draws), extent[dim] // shards_of).reshape((-1,) + (1,) * (len(extent) - dim - 1))

    level = one(*pieces[0])
    for cut in pieces[1:]:
        level = level * one(*cut)
    return level


def profile(count, total, reach, skew):
    portions = [(1 << 20) // math.isqrt(standing ** skew) + 1 for standing in range(2, count + 1)]
    rest, holding = total - reach - (count - 1), [1] * (count - 1)
    while rest > 0:
        free = [i for i in range(count - 1) if holding[i] < reach]
        whole, left = sum([portions[i] for i in free]), rest
        for i in free:
            extra = min(reach - holding[i], max(1, left * portions[i] // whole), rest)
            holding[i] = holding[i] + extra
            rest = rest - extra
    return np.array([reach] + holding)


def ragged_sizes(stream_key, amount, total, most, lean):
    if amount == 2:
        one = jax.random.randint(stream_key, (), max(1, total - most), min(most, total - 1) + 1)
        return jnp.stack([one, total - one])
    lengths = jnp.asarray(profile(amount, total, most, lean), jnp.int32)
    pairs = (amount - 1) // 2
    donor, sink = lengths[1:1 + 2 * pairs:2], lengths[2:2 + 2 * pairs:2]
    slack = jnp.minimum(donor - 1, most - sink)
    passed = jax.random.randint(jax.random.fold_in(stream_key, 1), (pairs,), 0, 1 << 20) % (slack + 1)
    lengths = lengths.at[1:1 + 2 * pairs:2].set(donor - passed).at[2:2 + 2 * pairs:2].set(sink + passed)
    return lengths[jax.random.permutation(jax.random.fold_in(stream_key, 2), amount)]


def noise(rng, extent, deviation, bound, split=(), dtype=jnp.bfloat16):
    entries = deviation * jax.random.normal(rng, extent, jnp.float32)
    if split:
        entries = entries * levels(rng, extent, split, -0.22, 0.18)
    return jnp.clip(entries, -bound, bound).astype(dtype)


def setup_inputs(seed: int = 0) -> dict:
    key_of = jax.random.split(jax.random.key(seed), 16)
    tokens = noise(key_of[0], (2, TOKENS, D), 1.0, 6.0, ((0, 2), (1, 16)))
    query_segments = jax.vmap(lambda own: jnp.searchsorted(jnp.cumsum(ragged_sizes(own, QPR, SLOT, QMOST, 2)), jnp.arange(SLOT), side="right"))(jax.random.split(key_of[1], ROWS)).reshape((ROWS, SLOT)).astype(jnp.int32)
    doc_lengths = ragged_sizes(key_of[2], ROWS, ROWS * SLOT * 5 // 8, SLOT, 2).astype(jnp.int32)
    bucket_table = draw_bucket_table(jax.random.fold_in(key_of[15], 71), 0)
    positives = touch_ends(jax.random.randint(key_of[4], (ROWS, QPR), 0, ROWS), jax.random.fold_in(key_of[4], 1), 0, ROWS - 1).astype(jnp.int32)
    gain_attn = jnp.clip(1.0 + 0.18 * jax.random.normal(key_of[5], (D,), jnp.float32), 0.1, 1.9)
    w_query_key = noise(key_of[6], (D, 2 * D), (4 * D) ** -0.5, 0.109375)
    w_value = noise(key_of[7], (D, D), D ** -0.5, 0.21875)
    w_attn_out = noise(key_of[8], (D, D), (D // 8) ** -0.5, 0.625)
    rel_bias = noise(key_of[9], (BUCKETS, HEADS), 1.0, 4.0, (), jnp.float32)
    gain_ff = jnp.clip(1.0 + 0.18 * jax.random.normal(key_of[10], (D,), jnp.float32), 0.1, 1.9)
    w_in = noise(key_of[11], (D, FF), D ** -0.5, 0.21875)
    w_out = noise(key_of[12], (FF, D), (FF // 3) ** -0.5, 0.1875)
    gain_final = jnp.clip(1.0 + 0.18 * jax.random.normal(key_of[13], (D,), jnp.float32), 0.1, 1.9)
    w_proj = noise(key_of[14], (D, D), D ** -0.5, 0.21875)
    return dict(tokens=tokens, query_segments=query_segments, doc_lengths=doc_lengths, bucket_table=bucket_table, positives=positives, gain_attn=gain_attn, w_query_key=w_query_key, w_value=w_value, w_attn_out=w_attn_out, rel_bias=rel_bias, gain_ff=gain_ff, w_in=w_in, w_out=w_out, gain_final=gain_final, w_proj=w_proj)


EPSILON = 1e-06
LOGIT_SCALE = 50.0
MASKED = -1000000000.0
HIGHEST = lax.Precision.HIGHEST

@jax.custom_vjp
def low(v):
    return lax.optimization_barrier(v.astype(jnp.bfloat16)).astype(jnp.float32)

@jax.custom_vjp
def low_back(v):
    return v

def low_keep(v):
    return (low(v), None)

def low_pass(kept, grad):
    return (grad,)

def back_keep(v):
    return (v, None)

def back_low(kept, grad):
    return (low(grad),)
low.defvjp(low_keep, low_pass)
low_back.defvjp(back_keep, back_low)

def hdot(left, right):
    return jnp.dot(left, right, precision=HIGHEST, preferred_element_type=jnp.float32)

def rms_norm(values, gain):
    return values * lax.rsqrt(lax.optimization_barrier(jnp.mean(values * values, axis=-1, keepdims=True)) + EPSILON) * gain

def encode(row_tokens, segment, bias_full, weights):
    gain_attn, w_query_key, w_value, w_attn_out, gain_ff, w_in, w_out, gain_final, w_proj = weights
    width = row_tokens.shape[0]
    normed = low(rms_norm(row_tokens, gain_attn))
    query_key = low(low_back(hdot(normed, w_query_key)))
    values = low(low_back(hdot(normed, w_value)))
    query_heads = query_key[:, :D].reshape(width, HEADS, HEAD)
    key_heads = query_key[:, D:].reshape(width, HEADS, HEAD)
    value_heads = values.reshape(width, HEADS, HEAD)
    raw = low_back(jnp.einsum('ihd,jhd->hij', query_heads, key_heads, precision=HIGHEST))
    allowed = (segment[:, None] == segment[None, :])[None]
    scores = jnp.where(allowed, raw + bias_full, MASKED)
    probs = low(jax.nn.softmax(scores, axis=-1))
    mixed = jnp.einsum('hij,jhd->ihd', probs, value_heads, precision=HIGHEST).reshape(width, D)
    mixed = low(low_back(mixed))
    hidden_one = row_tokens + low_back(hdot(mixed, w_attn_out))
    normed_two = low(rms_norm(hidden_one, gain_ff))
    inner = low_back(hdot(normed_two, w_in))
    active = low(jax.nn.gelu(inner, approximate=True))
    hidden_two = hidden_one + low_back(hdot(active, w_out))
    normed_three = rms_norm(hidden_two, gain_final)
    member = (segment[None, :] == jnp.arange(QPR)[:, None]).astype(jnp.float32)
    pool = member / jnp.maximum(lax.optimization_barrier(jnp.sum(member, axis=-1, keepdims=True)), 1.0)
    pooled = low(hdot(pool, normed_three))
    projected = low_back(hdot(pooled, w_proj))
    scale = lax.rsqrt(lax.optimization_barrier(jnp.sum(projected * projected, axis=-1, keepdims=True)) + EPSILON)
    return low(projected * scale)

def reference(tokens, query_segments, doc_lengths, bucket_table, positives, gain_attn, w_query_key, w_value, w_attn_out, rel_bias, gain_ff, w_in, w_out, gain_final, w_proj):
    positions = jnp.arange(SLOT)
    doc_segments = jnp.where(positions[None, :] < doc_lengths[:, None], 0, 1).astype(jnp.int32)
    segments = jnp.concatenate([query_segments.astype(jnp.int32), doc_segments], axis=0)
    offsets = (positions[None, :] - positions[:, None] + SLOT - 1).astype(jnp.int32)

    def loss_fn(inputs, gain_attn, w_query_key, w_value, w_attn_out, rel_bias, gain_ff, w_in, w_out, gain_final, w_proj):
        weights = (gain_attn, w_query_key, w_value, w_attn_out, gain_ff, w_in, w_out, gain_final, w_proj)
        table_bias = rel_bias[bucket_table]
        bias_full = jnp.transpose(table_bias[offsets], (2, 0, 1))
        row_inputs = inputs.reshape(2 * ROWS, SLOT, D)

        def encode_one(row_tokens, segment):
            return encode(row_tokens, segment, bias_full, weights)
        checked = jax.checkpoint(encode_one)

        def step(carry, item):
            return (carry, checked(item[0], item[1]))
        unused, embeds = lax.scan(step, None, (row_inputs, segments))
        query_embeds = embeds[:ROWS]
        doc_embeds = embeds[ROWS:, 0]
        logits = LOGIT_SCALE * jnp.einsum('rqd,sd->rqs', query_embeds, doc_embeds, precision=HIGHEST)
        totals = jax.nn.logsumexp(logits, axis=-1)
        picked = jnp.take_along_axis(logits, positives[:, :, None], axis=-1)[..., 0]
        return jnp.mean(totals - picked)
    params = (gain_attn.astype(jnp.float32), w_query_key.astype(jnp.float32), w_value.astype(jnp.float32), w_attn_out.astype(jnp.float32), rel_bias.astype(jnp.float32), gain_ff.astype(jnp.float32), w_in.astype(jnp.float32), w_out.astype(jnp.float32), gain_final.astype(jnp.float32), w_proj.astype(jnp.float32))
    loss, pull = jax.vjp(loss_fn, tokens.astype(jnp.float32), *params)
    grads = pull(jnp.ones_like(loss))
    return (loss, grads[0], grads[1], grads[2], grads[3], grads[4], grads[5], grads[6], grads[7], grads[8], grads[9], grads[10])
```

```python
import math

import jax
import jax.numpy as jnp
from jax import lax
from jax.experimental import pallas as pl
from jax.experimental.pallas import tpu as pltpu
from jax.sharding import PartitionSpec as P

EPSILON = 1e-06
LOGIT_SCALE = 50.0
MASKED = -1000000000.0
MESH = pl.DeviceIdType.MESH
LOW = jnp.bfloat16
FULL = jnp.float32
LANES = 128
TILE = 512
UNIT_ROWS = 48
UNIT_COLUMNS = 384
VMEM_LIMIT = 60 * 2**20


def dot(left, right):
    return jnp.dot(left, right, preferred_element_type=FULL)


def dot_nt(left, right):
    return lax.dot_general(left, right, (((1,), (1,)), ((), ())), preferred_element_type=FULL)


def dot_tn(left, right):
    return lax.dot_general(left, right, (((0,), (0,)), ((), ())), preferred_element_type=FULL)


def split(values):
    upper = values.astype(LOW)
    return upper, (values - upper.astype(FULL)).astype(LOW)


def inverse_root(values):
    return lax.rsqrt(jnp.mean(values * values, axis=-1, keepdims=True) + EPSILON)


def norm_backward(values, inverse, gain, upstream):
    scaled = upstream * gain
    gain_grad = jnp.sum(upstream * (values * inverse), axis=0, keepdims=True)
    inner = jnp.mean(scaled * values, axis=-1, keepdims=True)
    return inverse * scaled - values * (inverse * inverse * inverse * inner), gain_grad


def tiles(total, size):
    def over(body):
        def step(index, carry):
            body(index, pl.ds(pl.multiple_of(index * size, size), size))
            return carry

        lax.fori_loop(0, total // size, step, 0)

    return over


class Refs:
    pass


def make_kernel(sizes, names):
    rows, width, model, ff, heads, buckets, per_row = sizes
    head_size = model // heads
    half = model // 2
    ff_half = ff // 2
    queries = rows * per_row
    parts = model // LANES
    query_message = parts * per_row
    row_bits = rows.bit_length() - 1

    def kernel(*args):
        r = Refs()
        for name, ref in zip(names, args):
            setattr(r, name, ref)
        tower = lax.axis_index("tower")
        row = lax.axis_index("rows")
        partner = (1 - tower, row)
        is_query = tower == 0

        barrier = pltpu.get_barrier_semaphore()
        pl.semaphore_signal(barrier, inc=1, device_id=partner, device_id_type=MESH)

        def greet(step, carry):
            peer = (tower, jnp.bitwise_xor(row, step))
            pl.semaphore_signal(barrier, inc=1, device_id=peer, device_id_type=MESH)
            return carry

        lax.fori_loop(1, rows, greet, 0)

        loads = {}
        for index, name in enumerate(("w_query_key", "w_value", "w_attn_out", "w_in", "w_out", "w_proj")):
            loads[name] = pltpu.make_async_copy(
                getattr(r, name), getattr(r, name + "_here"), r.load_sem.at[index]
            )
            loads[name].start()

        def weight(name):
            loads[name].wait()
            return getattr(r, name + "_here")

        def to_partner(src, dst, index):
            return pltpu.make_async_remote_copy(
                src_ref=src,
                dst_ref=dst,
                send_sem=r.core_send.at[index],
                recv_sem=r.core_recv.at[index],
                device_id=partner,
                device_id_type=MESH,
            )

        lane = lax.broadcasted_iota(jnp.int32, (8, width), 1)
        doc_row = jnp.where(lane < r.doc_lengths[0], 0, 1)
        seg_row = jnp.where(is_query, jnp.broadcast_to(r.query_segments[...], (8, width)), doc_row)
        eye = (
            lax.broadcasted_iota(jnp.int32, (width, width), 0)
            == lax.broadcasted_iota(jnp.int32, (width, width), 1)
        ).astype(FULL)
        seg_column = dot_nt(eye.astype(LOW), seg_row.astype(FULL).astype(LOW))[:, 0:1].astype(jnp.int32)
        member = (seg_row == lax.broadcasted_iota(jnp.int32, (8, width), 0)).astype(FULL)
        share = 1.0 / jnp.maximum(jnp.sum(member, axis=-1, keepdims=True), 1.0)

        wide = 2 * width
        table = jnp.concatenate(
            [r.bucket_table[...], jnp.zeros((1, 1), jnp.int32)], axis=1
        )
        turned = (
            lax.broadcasted_iota(jnp.int32, (wide, wide), 0)
            + lax.broadcasted_iota(jnp.int32, (wide, wide), 1)
            == wide - 2
        ).astype(FULL).astype(LOW)
        table_low = jnp.broadcast_to(table.astype(FULL), (8, wide)).astype(LOW)
        table_turned = dot(table_low, turned)[0:1]
        hot = (
            table_turned.astype(jnp.int32) == lax.broadcasted_iota(jnp.int32, (buckets, wide), 0)
        ).astype(FULL)
        r.hot[...] = hot.astype(LOW)
        bias_upper, bias_lower = split(r.rel_bias[...])
        bias_last = (r.rel_bias[...] - bias_upper.astype(FULL) - bias_lower.astype(FULL)).astype(LOW)
        hot_low = hot.astype(LOW)
        r.table[0:heads, :] = (
            dot_tn(bias_upper, hot_low) + dot_tn(bias_lower, hot_low) + dot_tn(bias_last, hot_low)
        )

        r.small[...] = jnp.zeros_like(r.small)
        r.diagonals[...] = jnp.zeros_like(r.diagonals)

        inputs = r.tokens[...].astype(FULL)
        normed = (inputs * inverse_root(inputs) * r.gain_attn[...]).astype(LOW)
        r.normed_one[0:width, :] = normed
        w_query_key = weight("w_query_key")

        @tiles(2 * model, TILE)
        def _(index, columns):
            r.qkv[:, columns] = dot(r.normed_one[0:width, :], w_query_key[:, columns]).astype(LOW)

        w_value = weight("w_value")
        r.qkv[:, 2 * model :] = dot(normed, w_value[...]).astype(LOW)

        pl.semaphore_wait(barrier, rows)
        send_one = to_partner(r.normed_one.at[0:width], r.normed_one.at[width : 2 * width], 0)
        send_one.start()

        r.keys_turned[...] = r.qkv[:, model : 2 * model].T
        r.values_turned[...] = r.qkv[:, 2 * model :].T

        allowed = seg_column == seg_row[0:1]
        r.allowed[...] = allowed.astype(FULL)

        @tiles(model, 2 * head_size)
        def _(pair, columns):
            query = r.qkv[:, columns]
            key = r.qkv[:, pl.ds(pl.multiple_of(model + pair * 2 * head_size, LANES), 2 * head_size)]
            place = lax.broadcasted_iota(jnp.int32, (width, 2 * head_size), 1)
            for side in range(2):
                head = 2 * pair + side
                own = (place >= head_size) if side else (place < head_size)
                score = dot_nt(jnp.where(own, key, jnp.zeros_like(key)), query)
                line = jnp.broadcast_to(r.table[pl.ds(head, 1), :], (width, wide))
                bias = pltpu.roll(line, width + 1, 1, stride=1, stride_axis=0)[:, :width]
                score = jnp.where(r.allowed[...] > 0.5, score + bias, MASKED)
                weights = jnp.exp(score - jnp.max(score, axis=0, keepdims=True))
                prob = (weights * (1.0 / jnp.sum(weights, axis=0, keepdims=True))).astype(LOW)
                r.probs[head] = prob
                here = pl.ds(pl.multiple_of(head * head_size, head_size), head_size)
                r.mixed_turned[here, :] = dot(r.values_turned[here, :], prob).astype(LOW)

        mixed = r.mixed_turned[...].T
        r.mixed[0:width, :] = mixed
        send_mixed = to_partner(r.mixed.at[0:width], r.mixed.at[width : 2 * width], 1)
        send_mixed.start()
        w_attn_out = weight("w_attn_out")
        hidden = r.tokens[...].astype(FULL) + dot(mixed, w_attn_out[...])
        r.hidden_one[...] = hidden
        r.normed_two[0:width, :] = (hidden * inverse_root(hidden) * r.gain_ff[...]).astype(LOW)
        send_two = to_partner(r.normed_two.at[0:width], r.normed_two.at[width : 2 * width], 2)
        send_two.start()

        w_in = weight("w_in")
        bend = math.sqrt(2.0 / math.pi)

        @tiles(ff, TILE)
        def _(index, columns):
            inner = dot(r.normed_two[0:width, :], w_in[:, columns])
            square = inner * inner
            curve = jnp.tanh(bend * (inner * (1.0 + 0.044715 * square)))
            lift = 0.5 * (1.0 + curve)
            r.active[0:width, columns] = (inner * lift).astype(LOW)
            slope = 0.5 * inner * (1.0 - curve * curve) * (bend * (1.0 + 3 * 0.044715 * square))
            r.slope[:, columns] = (lift + slope).astype(LOW)

        send_active = to_partner(r.active.at[0:width], r.active.at[width : 2 * width], 3)
        send_active.start()
        w_out = weight("w_out")

        @tiles(model, model // 3)
        def _(index, columns):
            r.hidden_two[:, columns] = r.hidden_one[:, columns] + dot(
                r.active[0:width, :], w_out[:, columns]
            )

        hidden = r.hidden_two[...]
        normed_upper, normed_lower = split(hidden * inverse_root(hidden) * r.gain_final[...])
        member_low = member.astype(LOW)
        pooled = (dot(member_low, normed_upper) + dot(member_low, normed_lower)) * share
        pooled = pooled.astype(LOW).astype(FULL)

        own_queries = r.pooled_queries.at[pl.ds(pl.multiple_of(row * query_message, 8), query_message)]
        own_doc = r.pooled_docs.at[pl.ds(pl.multiple_of(row * 8, 8), 8)]

        def spread(block, act):
            def step(index, carry):
                act(
                    pltpu.make_async_remote_copy(
                        src_ref=block,
                        dst_ref=block,
                        send_sem=r.spread_send.at[index],
                        recv_sem=r.spread_recv.at[index],
                        device_id=(tower, jnp.bitwise_xor(row, index)),
                        device_id_type=MESH,
                    )
                )
                return carry

            lax.fori_loop(1, rows, step, 0)

        relay_queries = to_partner(r.pooled_queries, r.pooled_queries, 4)
        relay_docs = to_partner(r.pooled_docs, r.pooled_docs, 5)

        @pl.when(is_query)
        def _():
            for part in range(parts):
                spot = pl.multiple_of(row * query_message, 8) + part * per_row
                r.pooled_queries[pl.ds(spot, per_row), :] = pooled[
                    0:per_row, part * LANES : (part + 1) * LANES
                ]
            spread(own_queries, lambda copy: copy.start())
            spread(own_queries, lambda copy: copy.wait())
            relay_queries.start()
            relay_docs.wait_recv()
            relay_queries.wait_send()

        @pl.when(jnp.logical_not(is_query))
        def _():
            own_doc[...] = jnp.zeros((8, LANES), FULL)
            for part in range(parts):
                spot = pl.multiple_of(row * 8, 8) + part
                r.pooled_docs[pl.ds(spot, 1), :] = pooled[0:1, part * LANES : (part + 1) * LANES]
            spread(own_doc, lambda copy: copy.start())
            spread(own_doc, lambda copy: copy.wait())
            relay_docs.start()
            relay_queries.wait_recv()
            relay_docs.wait_send()

        for part in range(parts):
            lanes = slice(part * LANES, (part + 1) * LANES)
            for query in range(per_row):
                r.pooled[query * rows : (query + 1) * rows, lanes] = r.pooled_queries[
                    pl.ds(part * per_row + query, rows, stride=query_message), :
                ]
            r.pooled[queries:, lanes] = r.pooled_docs[pl.ds(part, rows, stride=8), :]

        w_proj = weight("w_proj")
        pooled_low = r.pooled[...].astype(LOW)
        projected = dot(pooled_low, w_proj[...])
        scale = lax.rsqrt(jnp.sum(projected * projected, axis=-1, keepdims=True) + EPSILON)
        embed = (projected * scale).astype(LOW)
        query_embed, doc_embed = embed[:queries], embed[queries:]
        logits = LOGIT_SCALE * dot_nt(query_embed, doc_embed)
        target = jnp.concatenate(
            [
                (
                    r.positives[:, query : query + 1]
                    == lax.broadcasted_iota(jnp.int32, (rows, rows), 1)
                ).astype(FULL)
                for query in range(per_row)
            ],
            axis=0,
        )
        highest = jnp.max(logits, axis=-1, keepdims=True)
        log_sum = highest + jnp.log(jnp.sum(jnp.exp(logits - highest), axis=-1, keepdims=True))
        missed = log_sum - jnp.sum(logits * target, axis=-1, keepdims=True)
        r.loss[...] = jnp.sum(missed, axis=0, keepdims=True) / queries
        logits_grad = (jnp.exp(logits - log_sum) - target) * (LOGIT_SCALE / queries)
        grad_upper, grad_lower = split(logits_grad)
        embed_grad = jnp.concatenate(
            [
                dot(grad_upper, doc_embed) + dot(grad_lower, doc_embed),
                dot_tn(grad_upper, query_embed) + dot_tn(grad_lower, query_embed),
            ],
            axis=0,
        )
        along = jnp.sum(embed_grad * projected, axis=-1, keepdims=True)
        proj_grad = (scale * embed_grad - projected * (scale * scale * scale * along)).astype(LOW)
        r.proj_grad[...] = proj_grad.astype(FULL)
        r.own_grad[...] = jnp.zeros_like(r.own_grad)

        @pl.when(is_query)
        def _():
            for query in range(per_row):
                r.own_grad[query : query + 1, :] = r.proj_grad[pl.ds(query * rows + row, 1), :]

        @pl.when(jnp.logical_not(is_query))
        def _():
            r.own_grad[0:1, :] = r.proj_grad[pl.ds(queries + row, 1), :]

        pooled_grad = dot_nt(r.own_grad[...].astype(LOW), w_proj[...])[0:8] * share
        final_grad = jnp.zeros((width, model), FULL)
        for query in range(per_row):
            final_grad = jnp.where(seg_column == query, pooled_grad[query : query + 1, :], final_grad)

        hidden = r.hidden_two[...]
        hidden_grad, r.small[2:3, :] = norm_backward(
            hidden, inverse_root(hidden), r.gain_final[...], final_grad
        )
        r.hidden_grad[...] = hidden_grad
        r.branch[...] = hidden_grad.astype(LOW)
        own_half = pl.ds(pl.multiple_of(tower * half, LANES), half)
        other_half = pl.ds(pl.multiple_of((1 - tower) * half, LANES), half)
        send_branch = to_partner(r.branch.at[:, other_half], r.branch_half.at[width : 2 * width], 6)
        send_branch.start()
        r.branch_half[0:width, :] = r.branch[:, own_half]

        r.proj_grad_half[...] = r.proj_grad[:, own_half].astype(LOW)
        r.w_proj_whole[...] = dot_tn(r.pooled[...].astype(LOW), r.proj_grad_half[...])

        @tiles(ff, TILE)
        def _(index, columns):
            active_grad = dot_nt(r.branch[...], w_out[columns, :])
            r.inner_grad[:, columns] = (active_grad * r.slope[:, columns].astype(FULL)).astype(LOW)

        own_ff = pl.ds(pl.multiple_of(tower * ff_half, LANES), ff_half)
        other_ff = pl.ds(pl.multiple_of((1 - tower) * ff_half, LANES), ff_half)
        send_inner = to_partner(r.inner_grad.at[:, other_ff], r.inner_half.at[width : 2 * width], 7)
        send_inner.start()
        r.inner_half[0:width, :] = r.inner_grad[:, own_ff]

        send_active.wait()
        send_branch.wait()

        @tiles(ff, model)
        def _(index, columns):
            r.out_parts[index] = dot_tn(r.active[:, columns], r.branch_half[...]).astype(LOW)

        @tiles(model, model // 3)
        def _(index, columns):
            r.normed_grad[:, columns] = dot_nt(r.inner_grad[...], w_in[columns, :])

        hidden = r.hidden_one[...]
        through, r.small[1:2, :] = norm_backward(
            hidden, inverse_root(hidden), r.gain_ff[...], r.normed_grad[...]
        )
        hidden_grad = r.hidden_grad[...] + through
        r.hidden_grad[...] = hidden_grad
        r.attn[...] = hidden_grad.astype(LOW)
        send_attn = to_partner(r.attn.at[:, other_half], r.attn_half.at[width : 2 * width], 8)
        send_attn.start()
        r.attn_half[0:width, :] = r.attn[:, own_half]

        send_two.wait()
        send_inner.wait()

        @tiles(ff_half, TILE)
        def _(index, columns):
            r.in_parts[index] = dot_tn(r.normed_two[...], r.inner_half[:, columns]).astype(LOW)

        r.mixed_grad[...] = dot_nt(r.attn[...], w_attn_out[...]).astype(LOW)
        send_mixed.wait()
        send_attn.wait()
        r.attn_parts[...] = dot_tn(r.mixed[...], r.attn_half[...]).astype(LOW)

        @tiles(model, 2 * head_size)
        def _(pair, columns):
            query = r.qkv[:, columns]
            value = r.qkv[:, pl.ds(pl.multiple_of(2 * model + pair * 2 * head_size, LANES), 2 * head_size)]
            mixed_grad = r.mixed_grad[:, columns]
            place = lax.broadcasted_iota(jnp.int32, (width, 2 * head_size), 1)
            key_sides, value_sides = [], []
            for side in range(2):
                head = 2 * pair + side
                own = (place >= head_size) if side else (place < head_size)
                prob_low = r.probs[head]
                prob = prob_low.astype(FULL)
                prob_grad = dot_nt(jnp.where(own, value, jnp.zeros_like(value)), mixed_grad)
                weighted = prob * prob_grad
                score_grad = weighted - prob * jnp.sum(weighted, axis=0, keepdims=True)
                score_low = score_grad.astype(LOW)
                key_sides.append(dot(score_low, query))
                value_sides.append(dot(prob_low, mixed_grad))
                here = pl.ds(pl.multiple_of(head * head_size, head_size), head_size)
                r.queries_turned[here, :] = dot(r.keys_turned[here, :], score_low).astype(LOW)
                r.score_grad[...] = score_grad
                total = jnp.zeros((8, wide), FULL)
                blank = jnp.zeros((8, wide - width), FULL)
                for block in range(width // 8):
                    line = jnp.concatenate([r.score_grad[8 * block : 8 * block + 8, :], blank], axis=1)
                    total = total + pltpu.roll(line, (wide + width - 1 - 8 * block) % wide, 1)
                for line in range(8):
                    r.diagonals[line, pl.ds(head, 1), :] = total[line : line + 1, :]
            after = place >= head_size
            r.qkv_grad[:, pl.ds(pl.multiple_of(model + pair * 2 * head_size, LANES), 2 * head_size)] = (
                jnp.where(after, key_sides[1], key_sides[0]).astype(LOW)
            )
            r.qkv_grad[:, pl.ds(pl.multiple_of(2 * model + pair * 2 * head_size, LANES), 2 * head_size)] = (
                jnp.where(after, value_sides[1], value_sides[0]).astype(LOW)
            )

        r.qkv_grad[:, 0:model] = r.queries_turned[...].T

        own_whole = pl.ds(pl.multiple_of(tower * model, LANES), model)
        other_whole = pl.ds(pl.multiple_of((1 - tower) * model, LANES), model)
        own_value = pl.ds(pl.multiple_of(2 * model + tower * half, LANES), half)
        other_value = pl.ds(pl.multiple_of(2 * model + (1 - tower) * half, LANES), half)
        send_qk = to_partner(
            r.qkv_grad.at[:, other_whole], r.qkv_half.at[width : 2 * width, 0:model], 9
        )
        send_value = to_partner(
            r.qkv_grad.at[:, other_value], r.qkv_half.at[width : 2 * width, model:], 10
        )
        send_qk.start()
        send_value.start()
        r.qkv_half[0:width, 0:model] = r.qkv_grad[:, own_whole]
        r.qkv_half[0:width, model:] = r.qkv_grad[:, own_value]

        normed_grad = dot_nt(r.qkv_grad[:, 0 : 2 * model], w_query_key[...])
        r.normed_grad[...] = normed_grad + dot_nt(r.qkv_grad[:, 2 * model :], w_value[...])
        inputs = r.tokens[...].astype(FULL)
        through, r.small[0:1, :] = norm_backward(
            inputs, inverse_root(inputs), r.gain_attn[...], r.normed_grad[...]
        )
        r.tokens_grad[...] = r.hidden_grad[...] + through

        offsets = jnp.zeros((16, wide), FULL)
        for line in range(8):
            row_lines = r.diagonals[line]
            offsets = offsets + (pltpu.roll(row_lines, wide - line, 1) if line else row_lines)
        offset_upper, offset_lower = split(offsets)
        hot_low = r.hot[...]
        r.small[8 : 8 + buckets, 0:16] = dot_nt(hot_low, offset_upper) + dot_nt(hot_low, offset_lower)

        send_one.wait()
        send_qk.wait()
        send_value.wait()
        r.qkv_parts[...] = dot_tn(r.normed_one[...], r.qkv_half[...]).astype(LOW)

        small_rows = 8 + buckets
        for bit in range(row_bits + 1):
            peer = partner if bit == row_bits else (tower, jnp.bitwise_xor(row, 1 << bit))
            copy = pltpu.make_async_remote_copy(
                src_ref=r.small,
                dst_ref=r.small_in.at[bit],
                send_sem=r.small_send.at[bit],
                recv_sem=r.small_recv.at[bit],
                device_id=peer,
                device_id_type=MESH,
            )
            copy.start()
            copy.wait()
            r.small[...] = r.small[...] + r.small_in[bit]
        r.gain_attn_grad[...] = r.small[0:1, :]
        r.gain_ff_grad[...] = r.small[1:2, :]
        r.gain_final_grad[...] = r.small[2:3, :]
        r.rel_bias_grad[...] = r.small[8 : 8 + buckets, 0:heads]

    return kernel


def on_device(rows):
    def step(
        tokens,
        query_segments,
        doc_lengths,
        bucket_table,
        positives,
        gain_attn,
        w_query_key,
        w_value,
        w_attn_out,
        rel_bias,
        gain_ff,
        w_in,
        w_out,
        gain_final,
        w_proj,
    ):
        width, model = tokens.shape[1:]
        ff = w_in.shape[1]
        buckets, heads = rel_bias.shape
        per_row = positives.shape[1]
        half = model // 2
        wide = 2 * width
        queries = rows * per_row
        row_bits = rows.bit_length() - 1
        own_rows = model // rows
        vmem = pl.BlockSpec(memory_space=pltpu.VMEM)
        smem = pl.BlockSpec(memory_space=pltpu.SMEM)
        hbm = pl.BlockSpec(memory_space=pl.ANY)
        inputs = [
            ("tokens", tokens[0], vmem),
            ("query_segments", query_segments, vmem),
            ("doc_lengths", doc_lengths, smem),
            ("bucket_table", bucket_table[None], vmem),
            ("positives", positives, vmem),
            ("gain_attn", gain_attn[None], vmem),
            ("w_query_key", w_query_key, hbm),
            ("w_value", w_value, hbm),
            ("w_attn_out", w_attn_out, hbm),
            ("rel_bias", rel_bias, vmem),
            ("gain_ff", gain_ff[None], vmem),
            ("w_in", w_in, hbm),
            ("w_out", w_out, hbm),
            ("gain_final", gain_final[None], vmem),
            ("w_proj", w_proj, hbm),
        ]
        outputs = [
            ("loss", (1, 1), FULL),
            ("tokens_grad", (width, model), FULL),
            ("gain_attn_grad", (1, model), FULL),
            ("gain_ff_grad", (1, model), FULL),
            ("gain_final_grad", (1, model), FULL),
            ("rel_bias_grad", (buckets, heads), FULL),
            ("w_proj_whole", (model, half), FULL),
            ("out_parts", (ff // model, model, half), LOW),
            ("in_parts", (ff // 2 // TILE, model, TILE), LOW),
            ("attn_parts", (model, half), LOW),
            ("qkv_parts", (model, model + half), LOW),
        ]
        scratch = [
            ("w_query_key_here", w_query_key.shape, LOW),
            ("w_value_here", w_value.shape, LOW),
            ("w_attn_out_here", w_attn_out.shape, LOW),
            ("w_in_here", w_in.shape, LOW),
            ("w_out_here", w_out.shape, LOW),
            ("w_proj_here", w_proj.shape, LOW),
            ("hot", (buckets, wide), LOW),
            ("table", (16, wide), FULL),
            ("allowed", (width, width), FULL),
            ("normed_one", (2 * width, model), LOW),
            ("qkv", (width, 3 * model), LOW),
            ("keys_turned", (model, width), LOW),
            ("values_turned", (model, width), LOW),
            ("probs", (heads, width, width), LOW),
            ("mixed_turned", (model, width), LOW),
            ("mixed", (2 * width, model), LOW),
            ("hidden_one", (width, model), FULL),
            ("normed_two", (2 * width, model), LOW),
            ("active", (2 * width, ff), LOW),
            ("slope", (width, ff), LOW),
            ("hidden_two", (width, model), FULL),
            ("pooled_queries", (rows * per_row * model // LANES, LANES), FULL),
            ("pooled_docs", (rows * 8, LANES), FULL),
            ("pooled", (queries + rows, model), FULL),
            ("proj_grad", (queries + rows, model), FULL),
            ("proj_grad_half", (queries + rows, half), LOW),
            ("own_grad", (16, model), FULL),
            ("hidden_grad", (width, model), FULL),
            ("branch", (width, model), LOW),
            ("branch_half", (2 * width, half), LOW),
            ("inner_grad", (width, ff), LOW),
            ("inner_half", (2 * width, ff // 2), LOW),
            ("normed_grad", (width, model), FULL),
            ("attn", (width, model), LOW),
            ("attn_half", (2 * width, half), LOW),
            ("mixed_grad", (width, model), LOW),
            ("score_grad", (width, width), FULL),
            ("diagonals", (8, 16, wide), FULL),
            ("queries_turned", (model, width), LOW),
            ("qkv_grad", (width, 3 * model), LOW),
            ("qkv_half", (2 * width, model + half), LOW),
            ("small", (8 + buckets, model), FULL),
            ("small_in", (row_bits + 1, 8 + buckets, model), FULL),
        ]
        semaphores = [
            ("load_sem", 6),
            ("core_send", 11),
            ("core_recv", 11),
            ("spread_send", rows),
            ("spread_recv", rows),
            ("small_send", row_bits + 1),
            ("small_recv", row_bits + 1),
        ]
        names = [name for group in (inputs, outputs, scratch, semaphores) for name, *_ in group]
        sizes = (rows, width, model, ff, heads, buckets, per_row)
        results = pl.pallas_call(
            make_kernel(sizes, names),
            out_shape=[jax.ShapeDtypeStruct(shape, kind) for _, shape, kind in outputs],
            in_specs=[spec for _, _, spec in inputs],
            out_specs=[vmem] * len(outputs),
            scratch_shapes=[pltpu.VMEM(shape, kind) for _, shape, kind in scratch]
            + [pltpu.SemaphoreType.DMA((count,)) for _, count in semaphores],
            compiler_params=pltpu.CompilerParams(
                collective_id=0, has_side_effects=True, vmem_limit_bytes=VMEM_LIMIT
            ),
        )(*[array for _, array, _ in inputs])
        r = dict(zip([name for name, *_ in outputs], results))

        def over_rows(parts, axis):
            return lax.psum_scatter(parts, "rows", scatter_dimension=axis, tiled=True).astype(FULL)

        out_grad = over_rows(r["out_parts"].reshape(ff, half), 0)
        in_grad = over_rows(r["in_parts"], 1).transpose(1, 0, 2).reshape(own_rows, ff // 2)
        attn_grad = over_rows(r["attn_parts"], 0)
        qkv_grad = over_rows(r["qkv_parts"], 0)
        return (
            r["loss"][0, 0],
            r["tokens_grad"][None],
            r["gain_attn_grad"][0],
            qkv_grad[:, :model],
            qkv_grad[:, model:],
            attn_grad,
            r["rel_bias_grad"],
            r["gain_ff_grad"][0],
            in_grad,
            out_grad,
            r["gain_final_grad"][0],
            lax.dynamic_slice_in_dim(
                r["w_proj_whole"], lax.axis_index("rows") * own_rows, own_rows, 0
            ),
        )

    return step


def solution(mesh):
    return jax.shard_map(
        on_device(mesh.shape["rows"]),
        mesh=mesh,
        in_specs=(P("tower", "rows", None), P("rows", None), P("rows")) + (P(),) * 12,
        out_specs=(
            P(),
            P("tower", "rows", None),
            P(),
            P("rows", "tower"),
            P("rows", "tower"),
            P("rows", "tower"),
            P(),
            P(),
            P("rows", "tower"),
            P("rows", "tower"),
            P(),
            P("rows", "tower"),
        ),
        check_vma=False,
    )
```

```python
import math
from types import SimpleNamespace

import jax
import jax.numpy as jnp
from jax import lax
from jax.experimental import pallas as pl
from jax.experimental.pallas import tpu as pltpu
from jax.sharding import PartitionSpec as P

EPSILON = 1e-06
LOGIT_SCALE = 50.0
MASKED = -1000000000.0
MESH = pl.DeviceIdType.MESH
LOW = jnp.bfloat16
FULL = jnp.float32
LANES = 128
TILE = 512
VMEM_LIMIT = 60 * 2**20

Z_HALF, Z_PAIR, Y, X = range(4)
X_FIRST = (X, Y, Z_PAIR, Z_HALF)
Y_FIRST = (Y, X, Z_PAIR, Z_HALF)
Z_THEN_X = (Z_PAIR, X, Y, Z_HALF)
Z_THEN_Y = (Z_PAIR, Y, X, Z_HALF)
ORDERS = (
    X_FIRST, Y_FIRST, Z_THEN_X, X_FIRST, Y_FIRST, Z_THEN_Y,
    X_FIRST, Y_FIRST, Z_THEN_X, X_FIRST, Y_FIRST, Z_THEN_Y,
)
AFTER_STAGE = (0, 0, 3, 3, 3, 3)
OUT_UNIT, IN_UNIT, ATTN_UNIT, QKV_UNIT, UNITS = 0, 4, 8, 9, 12


def dot(left, right):
    return jnp.dot(left, right, preferred_element_type=FULL)


def dot_nt(left, right):
    return lax.dot_general(left, right, (((1,), (1,)), ((), ())), preferred_element_type=FULL)


def dot_tn(left, right):
    return lax.dot_general(left, right, (((0,), (0,)), ((), ())), preferred_element_type=FULL)


def split(values):
    upper = values.astype(LOW)
    return upper, (values - upper.astype(FULL)).astype(LOW)


def inverse_root(values):
    return lax.rsqrt(jnp.mean(values * values, axis=-1, keepdims=True) + EPSILON)


def norm_backward(values, inverse, gain, upstream):
    scaled = upstream * gain
    gain_grad = jnp.sum(upstream * (values * inverse), axis=0, keepdims=True)
    inner = jnp.mean(scaled * values, axis=-1, keepdims=True)
    return inverse * scaled - values * (inverse * inverse * inverse * inner), gain_grad


def tiles(total, size):
    def over(body):
        def step(index, carry):
            body(index, pl.ds(pl.multiple_of(index * size, size), size))
            return carry

        lax.fori_loop(0, total // size, step, 0)

    return over


def in_kernel_sums(rows, model):
    return rows == 2 ** len(ORDERS[0]) and model % (16 * rows) == 0


def make_kernel(sizes, names):
    rows, width, model, ff, heads, buckets, per_row = sizes
    head_size = model // heads
    half = model // 2
    ff_half = ff // 2
    queries = rows * per_row
    parts = model // LANES
    query_message = parts * per_row
    row_bits = rows.bit_length() - 1
    direct = in_kernel_sums(rows, model)

    def kernel(*args):
        r = SimpleNamespace(**dict(zip(names, args)))
        arrived = args[len(names) :]
        tower = lax.axis_index("tower")
        row = lax.axis_index("rows")
        partner = (1 - tower, row)
        is_query = tower == 0
        own_rows = model // rows

        barrier = pltpu.get_barrier_semaphore()
        pl.semaphore_signal(barrier, inc=1, device_id=partner, device_id_type=MESH)

        def greet(step, carry):
            peer = (tower, jnp.bitwise_xor(row, step))
            pl.semaphore_signal(barrier, inc=1, device_id=peer, device_id_type=MESH)
            return carry

        lax.fori_loop(1, rows, greet, 0)

        loads = [
            pltpu.make_async_copy(far, near, r.load_sem.at[index])
            for index, (far, near) in enumerate(
                (
                    (r.w_query_key, r.w_query_key_here),
                    (r.w_value, r.w_value_here),
                    (r.w_attn_out, r.w_attn_out_here),
                    (r.w_in, r.w_in_here),
                    (r.w_out, r.w_out_here),
                    (r.w_proj, r.w_proj_here),
                )
            )
        ]
        for load in loads:
            load.start()

        def to_partner(src, dst, index):
            return pltpu.make_async_remote_copy(
                src_ref=src,
                dst_ref=dst,
                send_sem=r.core_send.at[index],
                recv_sem=r.core_recv.at[index],
                device_id=partner,
                device_id_type=MESH,
            )

        coordinate = [jnp.bitwise_and(lax.shift_right_logical(row, 3 - bit), 1) for bit in range(4)]

        def piece(unit, phase, kept):
            order = ORDERS[unit]
            place = [slice(None)] * 4
            for bit in order[:phase]:
                place[bit] = coordinate[bit]
            last = order[phase]
            place[last] = coordinate[last] if kept else 1 - coordinate[last]
            return (unit, *place)

        def exchange(unit, phase):
            return pltpu.make_async_remote_copy(
                src_ref=r.grads.at[piece(unit, phase, False)],
                dst_ref=arrived[phase].at[unit],
                send_sem=r.sum_send.at[unit, phase],
                recv_sem=r.sum_recv.at[unit, phase],
                device_id=(tower, jnp.bitwise_xor(row, 1 << (3 - ORDERS[unit][phase]))),
                device_id_type=MESH,
            )

        def begin(unit):
            if direct:
                exchange(unit, 0).start()

        def finish(unit, phase):
            exchange(unit, phase).wait_recv()
            kept = piece(unit, phase, True)
            come = arrived[phase][unit]
            if phase + 1 < row_bits:
                r.grads[kept] = r.grads[kept] + come
                exchange(unit, phase + 1).start()
                return
            total = r.grads[kept].astype(FULL) + come.astype(FULL)
            if unit < IN_UNIT:
                spot = unit - OUT_UNIT
                r.w_out_grad[spot * own_rows : (spot + 1) * own_rows, :] = total
            elif unit < ATTN_UNIT:
                spot = unit - IN_UNIT
                r.w_in_grad[:, spot * half : (spot + 1) * half] = total
            elif unit < QKV_UNIT:
                r.w_attn_out_grad[...] = total
            elif unit < UNITS - 1:
                spot = unit - QKV_UNIT
                r.w_query_key_grad[:, spot * half : (spot + 1) * half] = total
            else:
                r.w_value_grad[...] = total

        events = sorted(
            ((unit, phase) for unit in range(UNITS) for phase in range(4)),
            key=lambda event: (event[0] // 3 + event[1], -event[1], event[0]),
        )

        def after_stage(stage):
            if direct:
                first = sum(AFTER_STAGE[:stage])
                for event in events[first : first + AFTER_STAGE[stage]]:
                    finish(*event)

        def keep(unit, value):
            value = value.astype(LOW)
            r.grads[unit] = value.reshape(r.grads.shape[1:]) if direct else value

        lane = lax.broadcasted_iota(jnp.int32, (8, width), 1)
        doc_row = jnp.where(lane < r.doc_lengths[0], 0, 1)
        seg_row = jnp.where(is_query, jnp.broadcast_to(r.query_segments[...], (8, width)), doc_row)
        eye = (
            lax.broadcasted_iota(jnp.int32, (width, width), 0)
            == lax.broadcasted_iota(jnp.int32, (width, width), 1)
        ).astype(FULL)
        seg_column = dot_nt(eye.astype(LOW), seg_row.astype(FULL).astype(LOW))[:, 0:1].astype(jnp.int32)
        member = (seg_row == lax.broadcasted_iota(jnp.int32, (8, width), 0)).astype(FULL)
        share = 1.0 / jnp.maximum(jnp.sum(member, axis=-1, keepdims=True), 1.0)

        wide = 2 * width
        table = jnp.concatenate(
            [r.bucket_table[...], jnp.zeros((1, 1), jnp.int32)], axis=1
        )
        turned = (
            lax.broadcasted_iota(jnp.int32, (wide, wide), 0)
            + lax.broadcasted_iota(jnp.int32, (wide, wide), 1)
            == wide - 2
        ).astype(FULL).astype(LOW)
        table_low = jnp.broadcast_to(table.astype(FULL), (8, wide)).astype(LOW)
        table_turned = dot(table_low, turned)[0:1]
        hot = (
            table_turned.astype(jnp.int32) == lax.broadcasted_iota(jnp.int32, (buckets, wide), 0)
        ).astype(FULL)
        r.hot[...] = hot.astype(LOW)
        bias_upper, bias_lower = split(r.rel_bias[...])
        bias_last = (r.rel_bias[...] - bias_upper.astype(FULL) - bias_lower.astype(FULL)).astype(LOW)
        hot_low = hot.astype(LOW)
        r.table[0:heads, :] = dot(bias_upper, hot_low) + dot(bias_lower, hot_low) + dot(bias_last, hot_low)

        r.small[0] = jnp.zeros((8, model + 2 * LANES), FULL)
        r.diagonals[...] = jnp.zeros_like(r.diagonals)

        inputs = r.tokens[...].astype(FULL)
        normed = (inputs * inverse_root(inputs) * r.gain_attn[...][None]).astype(LOW)
        r.normed_one[0:width, :] = normed
        loads[0].wait()
        w_query_key = r.w_query_key_here

        @tiles(2 * model, TILE)
        def _(index, columns):
            r.qkv[:, columns] = dot(r.normed_one[0:width, :], w_query_key[:, columns]).astype(LOW)

        loads[1].wait()
        w_value = r.w_value_here
        r.qkv[:, 2 * model :] = dot(normed, w_value[...]).astype(LOW)

        pl.semaphore_wait(barrier, rows)
        send_one = to_partner(r.normed_one.at[0:width], r.normed_one.at[width : 2 * width], 0)
        send_one.start()

        r.keys_turned[...] = r.qkv[:, model : 2 * model].T
        r.values_turned[...] = r.qkv[:, 2 * model :].T

        allowed = seg_column == seg_row[0:1]
        r.allowed[...] = allowed.astype(FULL)

        @tiles(model, 2 * head_size)
        def _(pair, columns):
            query = r.qkv[:, columns]
            key = r.qkv[:, pl.ds(pl.multiple_of(model + pair * 2 * head_size, LANES), 2 * head_size)]
            place = lax.broadcasted_iota(jnp.int32, (width, 2 * head_size), 1)
            for side in range(2):
                head = 2 * pair + side
                own = (place >= head_size) if side else (place < head_size)
                score = dot_nt(jnp.where(own, key, jnp.zeros_like(key)), query)
                line = jnp.broadcast_to(r.table[pl.ds(head, 1), :], (width, wide))
                bias = pltpu.roll(line, width + 1, 1, stride=1, stride_axis=0)[:, :width]
                score = jnp.where(r.allowed[...] > 0.5, score + bias, MASKED)
                weights = jnp.exp(score - jnp.max(score, axis=0, keepdims=True))
                prob = (weights * (1.0 / jnp.sum(weights, axis=0, keepdims=True))).astype(LOW)
                r.probs[head] = prob
                here = pl.ds(pl.multiple_of(head * head_size, head_size), head_size)
                r.mixed_turned[here, :] = dot(r.values_turned[here, :], prob).astype(LOW)

        mixed = r.mixed_turned[...].T
        r.mixed[0:width, :] = mixed
        send_mixed = to_partner(r.mixed.at[0:width], r.mixed.at[width : 2 * width], 1)
        send_mixed.start()
        loads[2].wait()
        w_attn_out = r.w_attn_out_here
        hidden = r.tokens[...].astype(FULL) + dot(mixed, w_attn_out[...])
        r.hidden_one[...] = hidden
        r.normed_two[0:width, :] = (hidden * inverse_root(hidden) * r.gain_ff[...][None]).astype(LOW)
        send_two = to_partner(r.normed_two.at[0:width], r.normed_two.at[width : 2 * width], 2)
        send_two.start()

        loads[3].wait()
        w_in = r.w_in_here
        bend = math.sqrt(2.0 / math.pi)

        @tiles(ff, TILE)
        def _(index, columns):
            inner = dot(r.normed_two[0:width, :], w_in[:, columns])
            square = inner * inner
            curve = jnp.tanh(bend * (inner * (1.0 + 0.044715 * square)))
            lift = 0.5 * (1.0 + curve)
            r.active[0:width, columns] = (inner * lift).astype(LOW)
            slope = 0.5 * inner * (1.0 - curve * curve) * (bend * (1.0 + 3 * 0.044715 * square))
            r.slope[:, columns] = (lift + slope).astype(LOW)

        send_active = to_partner(r.active.at[0:width], r.active.at[width : 2 * width], 3)
        send_active.start()
        loads[4].wait()
        w_out = r.w_out_here

        @tiles(model, model // 3)
        def _(index, columns):
            r.hidden_two[:, columns] = r.hidden_one[:, columns] + dot(
                r.active[0:width, :], w_out[:, columns]
            )

        hidden = r.hidden_two[...]
        normed_upper, normed_lower = split(hidden * inverse_root(hidden) * r.gain_final[...][None])
        member_low = member.astype(LOW)
        pooled = (dot(member_low, normed_upper) + dot(member_low, normed_lower)) * share
        pooled = pooled.astype(LOW).astype(FULL)

        own_queries = r.pooled_queries.at[pl.ds(pl.multiple_of(row * query_message, 8), query_message)]
        own_doc = r.pooled_docs.at[pl.ds(pl.multiple_of(row * 8, 8), 8)]

        def spread(block, act):
            def step(index, carry):
                act(
                    pltpu.make_async_remote_copy(
                        src_ref=block,
                        dst_ref=block,
                        send_sem=r.spread_send.at[index],
                        recv_sem=r.spread_recv.at[index],
                        device_id=(tower, jnp.bitwise_xor(row, index)),
                        device_id_type=MESH,
                    )
                )
                return carry

            lax.fori_loop(1, rows, step, 0)

        relay_queries = to_partner(r.pooled_queries, r.pooled_queries, 4)
        relay_docs = to_partner(r.pooled_docs, r.pooled_docs, 5)

        @pl.when(is_query)
        def _():
            for part in range(parts):
                spot = pl.multiple_of(row * query_message, 8) + part * per_row
                r.pooled_queries[pl.ds(spot, per_row), :] = pooled[
                    0:per_row, part * LANES : (part + 1) * LANES
                ]
            spread(own_queries, lambda copy: copy.start())
            spread(own_queries, lambda copy: copy.wait())
            relay_queries.start()
            relay_docs.wait_recv()
            relay_queries.wait_send()

        @pl.when(jnp.logical_not(is_query))
        def _():
            own_doc[...] = jnp.zeros((8, LANES), FULL)
            for part in range(parts):
                spot = pl.multiple_of(row * 8, 8) + part
                r.pooled_docs[pl.ds(spot, 1), :] = pooled[0:1, part * LANES : (part + 1) * LANES]
            spread(own_doc, lambda copy: copy.start())
            spread(own_doc, lambda copy: copy.wait())
            relay_docs.start()
            relay_queries.wait_recv()
            relay_docs.wait_send()

        for part in range(parts):
            lanes = slice(part * LANES, (part + 1) * LANES)
            for query in range(per_row):
                r.pooled[query * rows : (query + 1) * rows, lanes] = r.pooled_queries[
                    pl.ds(part * per_row + query, rows, stride=query_message), :
                ]
            r.pooled[queries:, lanes] = r.pooled_docs[pl.ds(part, rows, stride=8), :]

        loads[5].wait()
        w_proj = r.w_proj_here
        pooled_low = r.pooled[...].astype(LOW)
        projected = dot(pooled_low, w_proj[...])
        scale = lax.rsqrt(jnp.sum(projected * projected, axis=-1, keepdims=True) + EPSILON)
        embed = (projected * scale).astype(LOW)
        query_embed, doc_embed = embed[:queries], embed[queries:]
        logits = LOGIT_SCALE * dot_nt(query_embed, doc_embed)
        target = jnp.concatenate(
            [
                (
                    jnp.broadcast_to(r.positives[query : query + 1, :].astype(FULL), (rows, rows)).T
                    == lax.broadcasted_iota(jnp.int32, (rows, rows), 1).astype(FULL)
                ).astype(FULL)
                for query in range(per_row)
            ],
            axis=0,
        )
        highest = jnp.max(logits, axis=-1, keepdims=True)
        log_sum = highest + jnp.log(jnp.sum(jnp.exp(logits - highest), axis=-1, keepdims=True))
        missed = log_sum - jnp.sum(logits * target, axis=-1, keepdims=True)
        r.loss[...] = jnp.sum(missed, axis=0, keepdims=True) / queries
        logits_grad = (jnp.exp(logits - log_sum) - target) * (LOGIT_SCALE / queries)
        grad_upper, grad_lower = split(logits_grad)
        embed_grad = jnp.concatenate(
            [
                dot(grad_upper, doc_embed) + dot(grad_lower, doc_embed),
                dot_tn(grad_upper, query_embed) + dot_tn(grad_lower, query_embed),
            ],
            axis=0,
        )
        along = jnp.sum(embed_grad * projected, axis=-1, keepdims=True)
        proj_grad = (scale * embed_grad - projected * (scale * scale * scale * along)).astype(LOW)
        r.proj_grad[...] = proj_grad.astype(FULL)
        r.own_grad[...] = jnp.zeros_like(r.own_grad)

        @pl.when(is_query)
        def _():
            for query in range(per_row):
                r.own_grad[query : query + 1, :] = r.proj_grad[pl.ds(query * rows + row, 1), :]

        @pl.when(jnp.logical_not(is_query))
        def _():
            r.own_grad[0:1, :] = r.proj_grad[pl.ds(queries + row, 1), :]

        pooled_grad = dot_nt(r.own_grad[...].astype(LOW), w_proj[...])[0:8] * share
        final_grad = jnp.zeros((width, model), FULL)
        for query in range(per_row):
            final_grad = jnp.where(seg_column == query, pooled_grad[query : query + 1, :], final_grad)

        hidden = r.hidden_two[...]
        hidden_grad, r.small[0, 2:3, 0:model] = norm_backward(
            hidden, inverse_root(hidden), r.gain_final[...][None], final_grad
        )
        r.hidden_grad[...] = hidden_grad
        r.branch[...] = hidden_grad.astype(LOW)
        own_half = pl.ds(pl.multiple_of(tower * half, LANES), half)
        other_half = pl.ds(pl.multiple_of((1 - tower) * half, LANES), half)
        send_branch = to_partner(r.branch.at[:, other_half], r.branch_half.at[width : 2 * width], 6)
        send_branch.start()
        r.branch_half[0:width, :] = r.branch[:, own_half]

        r.proj_grad_half[...] = r.proj_grad[:, own_half].astype(LOW)
        r.w_proj_whole[...] = dot_tn(r.pooled[...].astype(LOW), r.proj_grad_half[...])
        if direct:
            r.w_proj_grad[...] = r.w_proj_whole[pl.ds(pl.multiple_of(row * own_rows, 8), own_rows), :]

        @tiles(ff, TILE)
        def _(index, columns):
            active_grad = dot_nt(r.branch[...], w_out[columns, :])
            r.inner_grad[:, columns] = (active_grad * r.slope[:, columns].astype(FULL)).astype(LOW)

        own_ff = pl.ds(pl.multiple_of(tower * ff_half, LANES), ff_half)
        other_ff = pl.ds(pl.multiple_of((1 - tower) * ff_half, LANES), ff_half)
        send_inner = to_partner(r.inner_grad.at[:, other_ff], r.inner_half.at[width : 2 * width], 7)
        send_inner.start()
        r.inner_half[0:width, :] = r.inner_grad[:, own_ff]

        send_active.wait()
        send_branch.wait()

        @tiles(ff, model)
        def _(index, columns):
            value = dot_tn(r.active[:, columns], r.branch_half[...])
            if direct:
                per_tile = model * rows // ff
                for unit in range(per_tile):
                    for spot in range(per_tile):
                        start = (spot * per_tile + unit) * own_rows
                        r.grads[unit, index // 2, index % 2, spot // 2, spot % 2] = value[
                            start : start + own_rows, :
                        ].astype(LOW)
            else:
                keep(index, value)

        for unit in range(OUT_UNIT, IN_UNIT):
            begin(unit)
        after_stage(0)

        @tiles(model, model // 3)
        def _(index, columns):
            r.normed_grad[:, columns] = dot_nt(r.inner_grad[...], w_in[columns, :])

        hidden = r.hidden_one[...]
        through, r.small[0, 1:2, 0:model] = norm_backward(
            hidden, inverse_root(hidden), r.gain_ff[...][None], r.normed_grad[...]
        )
        hidden_grad = r.hidden_grad[...] + through
        r.hidden_grad[...] = hidden_grad
        r.attn[...] = hidden_grad.astype(LOW)
        send_attn = to_partner(r.attn.at[:, other_half], r.attn_half.at[width : 2 * width], 8)
        send_attn.start()
        r.attn_half[0:width, :] = r.attn[:, own_half]

        send_two.wait()
        send_inner.wait()

        @tiles(ff_half, half)
        def _(index, columns):
            keep(IN_UNIT + index, dot_tn(r.normed_two[...], r.inner_half[:, columns]))

        for unit in range(IN_UNIT, ATTN_UNIT):
            begin(unit)
        after_stage(1)

        r.mixed_grad[...] = dot_nt(r.attn[...], w_attn_out[...]).astype(LOW)
        send_mixed.wait()
        send_attn.wait()
        keep(ATTN_UNIT, dot_tn(r.mixed[...], r.attn_half[...]))
        begin(ATTN_UNIT)
        after_stage(2)

        def attention_back(pair):
            columns = pl.ds(pl.multiple_of(pair * 2 * head_size, LANES), 2 * head_size)
            query = r.qkv[:, columns]
            value = r.qkv[:, pl.ds(pl.multiple_of(2 * model + pair * 2 * head_size, LANES), 2 * head_size)]
            mixed_grad = r.mixed_grad[:, columns]
            place = lax.broadcasted_iota(jnp.int32, (width, 2 * head_size), 1)
            key_sides, value_sides = [], []
            for side in range(2):
                head = 2 * pair + side
                own = (place >= head_size) if side else (place < head_size)
                prob_low = r.probs[head]
                prob = prob_low.astype(FULL)
                prob_grad = dot_nt(jnp.where(own, value, jnp.zeros_like(value)), mixed_grad)
                weighted = prob * prob_grad
                score_grad = weighted - prob * jnp.sum(weighted, axis=0, keepdims=True)
                score_low = score_grad.astype(LOW)
                key_sides.append(dot(score_low, query))
                value_sides.append(dot(prob_low, mixed_grad))
                here = pl.ds(pl.multiple_of(head * head_size, head_size), head_size)
                r.queries_turned[here, :] = dot(r.keys_turned[here, :], score_low).astype(LOW)
                r.score_grad[...] = score_grad
                total = jnp.zeros((8, wide), FULL)
                blank = jnp.zeros((8, wide - width), FULL)
                for block in range(width // 8):
                    line = jnp.concatenate([r.score_grad[8 * block : 8 * block + 8, :], blank], axis=1)
                    total = total + pltpu.roll(line, (wide + width - 1 - 8 * block) % wide, 1)
                for line in range(8):
                    r.diagonals[line, pl.ds(head, 1), :] = total[line : line + 1, :]
            after = place >= head_size
            r.qkv_grad[:, pl.ds(pl.multiple_of(model + pair * 2 * head_size, LANES), 2 * head_size)] = (
                jnp.where(after, key_sides[1], key_sides[0]).astype(LOW)
            )
            r.qkv_grad[:, pl.ds(pl.multiple_of(2 * model + pair * 2 * head_size, LANES), 2 * head_size)] = (
                jnp.where(after, value_sides[1], value_sides[0]).astype(LOW)
            )

        pairs = heads // 2
        lax.fori_loop(0, pairs // 2, lambda pair, carry: (attention_back(pair), carry)[1], 0)
        after_stage(3)
        lax.fori_loop(pairs // 2, pairs, lambda pair, carry: (attention_back(pair), carry)[1], 0)
        after_stage(4)
        r.qkv_grad[:, 0:model] = r.queries_turned[...].T

        own_whole = pl.ds(pl.multiple_of(tower * model, LANES), model)
        other_whole = pl.ds(pl.multiple_of((1 - tower) * model, LANES), model)
        own_value = pl.ds(pl.multiple_of(2 * model + tower * half, LANES), half)
        other_value = pl.ds(pl.multiple_of(2 * model + (1 - tower) * half, LANES), half)
        send_qk = to_partner(
            r.qkv_grad.at[:, other_whole], r.qkv_half.at[width : 2 * width, 0:model], 9
        )
        send_value = to_partner(
            r.qkv_grad.at[:, other_value], r.qkv_half.at[width : 2 * width, model:], 10
        )
        send_qk.start()
        send_value.start()
        r.qkv_half[0:width, 0:model] = r.qkv_grad[:, own_whole]
        r.qkv_half[0:width, model:] = r.qkv_grad[:, own_value]

        normed_grad = dot_nt(r.qkv_grad[:, 0 : 2 * model], w_query_key[...])
        r.normed_grad[...] = normed_grad + dot_nt(r.qkv_grad[:, 2 * model :], w_value[...])
        inputs = r.tokens[...].astype(FULL)
        through, r.small[0, 0:1, 0:model] = norm_backward(
            inputs, inverse_root(inputs), r.gain_attn[...][None], r.normed_grad[...]
        )
        r.tokens_grad[...] = r.hidden_grad[...] + through

        offsets = jnp.zeros((16, wide), FULL)
        for line in range(8):
            row_lines = r.diagonals[line]
            offsets = offsets + (pltpu.roll(row_lines, wide - line, 1) if line else row_lines)
        offset_upper, offset_lower = split(offsets)
        hot_low = r.hot[...]
        sums = dot_nt(offset_upper, hot_low) + dot_nt(offset_lower, hot_low)
        r.small[0, 0:8, model : model + buckets] = sums[0:8]
        r.small[0, 0:8, model + LANES : model + LANES + buckets] = sums[8:16]

        send_one.wait()
        send_qk.wait()
        send_value.wait()

        @tiles(model + half, half)
        def _(index, columns):
            keep(QKV_UNIT + index, dot_tn(r.normed_one[...], r.qkv_half[:, columns]))

        for unit in range(QKV_UNIT, UNITS):
            begin(unit)
        after_stage(5)

        def small_begin(bit):
            peer = partner if bit == row_bits else (tower, jnp.bitwise_xor(row, 1 << bit))
            return pltpu.make_async_remote_copy(
                src_ref=r.small.at[bit],
                dst_ref=r.small_in.at[bit],
                send_sem=r.small_send.at[bit],
                recv_sem=r.small_recv.at[bit],
                device_id=peer,
                device_id_type=MESH,
            )

        def small_finish(bit):
            small_begin(bit).wait_recv()
            r.small[bit + 1] = r.small[bit] + r.small_in[bit]
            if bit < row_bits:
                small_begin(bit + 1).start()

        small_begin(0).start()
        if direct:
            rest = events[sum(AFTER_STAGE) :]
            for index, event in enumerate(rest):
                finish(*event)
                if index % 3 == 1 and index // 3 <= row_bits:
                    small_finish(index // 3)
            for unit in range(UNITS):
                for phase in range(row_bits):
                    exchange(unit, phase).wait_send()
        else:
            for bit in range(row_bits + 1):
                small_finish(bit)
        for bit in range(row_bits + 1):
            small_begin(bit).wait_send()
        total = row_bits + 1
        r.gain_attn_grad[...] = r.small[total, 0, 0:model]
        r.gain_ff_grad[...] = r.small[total, 1, 0:model]
        r.gain_final_grad[...] = r.small[total, 2, 0:model]
        r.rel_bias_grad[0:8, :] = r.small[total, 0:8, model : model + buckets]
        r.rel_bias_grad[8:heads, :] = r.small[total, 0 : heads - 8, model + LANES : model + LANES + buckets]

    return kernel


def on_device(rows):
    def step(
        tokens,
        query_segments,
        doc_lengths,
        bucket_table,
        positives,
        gain_attn,
        w_query_key,
        w_value,
        w_attn_out,
        rel_bias,
        gain_ff,
        w_in,
        w_out,
        gain_final,
        w_proj,
    ):
        width, model = tokens.shape[1:]
        ff = w_in.shape[1]
        buckets, heads = rel_bias.shape
        per_row = positives.shape[1]
        half = model // 2
        wide = 2 * width
        queries = rows * per_row
        row_bits = rows.bit_length() - 1
        own_rows = model // rows
        vmem = pl.BlockSpec(memory_space=pltpu.VMEM)
        smem = pl.BlockSpec(memory_space=pltpu.SMEM)
        hbm = pl.BlockSpec(memory_space=pl.ANY)
        direct = in_kernel_sums(rows, model)
        inputs = dict(
            tokens=(tokens[0], vmem),
            query_segments=(query_segments, vmem),
            doc_lengths=(doc_lengths, smem),
            bucket_table=(bucket_table[None], vmem),
            positives=(positives.T, vmem),
            gain_attn=(gain_attn, vmem),
            w_query_key=(w_query_key, hbm),
            w_value=(w_value, hbm),
            w_attn_out=(w_attn_out, hbm),
            rel_bias=(rel_bias.T, vmem),
            gain_ff=(gain_ff, vmem),
            w_in=(w_in, hbm),
            w_out=(w_out, hbm),
            gain_final=(gain_final, vmem),
            w_proj=(w_proj, hbm),
        )
        outputs = dict(
            loss=((1, 1), FULL),
            tokens_grad=((width, model), FULL),
            gain_attn_grad=((model,), FULL),
            gain_ff_grad=((model,), FULL),
            gain_final_grad=((model,), FULL),
            rel_bias_grad=((heads, buckets), FULL),
        )
        whole = ((model, half), FULL)
        if direct:
            outputs.update(
                w_query_key_grad=((own_rows, model), FULL),
                w_value_grad=((own_rows, half), FULL),
                w_attn_out_grad=((own_rows, half), FULL),
                w_in_grad=((own_rows, ff // 2), FULL),
                w_out_grad=((ff // rows, half), FULL),
                w_proj_grad=((own_rows, half), FULL),
            )
            held = dict(
                w_proj_whole=whole, grads=((UNITS,) + (2,) * row_bits + (own_rows, half), LOW)
            )
            arrived = [
                pltpu.VMEM((UNITS,) + (2,) * (row_bits - 1 - phase) + (own_rows, half), LOW)
                for phase in range(row_bits)
            ]
        else:
            outputs.update(w_proj_whole=whole, grads=((UNITS, model, half), LOW))
            held = {}
            arrived = []
        scratch = dict(
            w_query_key_here=(w_query_key.shape, LOW),
            w_value_here=(w_value.shape, LOW),
            w_attn_out_here=(w_attn_out.shape, LOW),
            w_in_here=(w_in.shape, LOW),
            w_out_here=(w_out.shape, LOW),
            w_proj_here=(w_proj.shape, LOW),
            hot=((buckets, wide), LOW),
            table=((16, wide), FULL),
            allowed=((width, width), FULL),
            normed_one=((2 * width, model), LOW),
            qkv=((width, 3 * model), LOW),
            keys_turned=((model, width), LOW),
            values_turned=((model, width), LOW),
            probs=((heads, width, width), LOW),
            mixed_turned=((model, width), LOW),
            mixed=((2 * width, model), LOW),
            hidden_one=((width, model), FULL),
            normed_two=((2 * width, model), LOW),
            active=((2 * width, ff), LOW),
            slope=((width, ff), LOW),
            hidden_two=((width, model), FULL),
            pooled_queries=((rows * per_row * model // LANES, LANES), FULL),
            pooled_docs=((rows * 8, LANES), FULL),
            pooled=((queries + rows, model), FULL),
            proj_grad=((queries + rows, model), FULL),
            proj_grad_half=((queries + rows, half), LOW),
            own_grad=((16, model), FULL),
            hidden_grad=((width, model), FULL),
            branch=((width, model), LOW),
            branch_half=((2 * width, half), LOW),
            inner_grad=((width, ff), LOW),
            inner_half=((2 * width, ff // 2), LOW),
            normed_grad=((width, model), FULL),
            attn=((width, model), LOW),
            attn_half=((2 * width, half), LOW),
            mixed_grad=((width, model), LOW),
            score_grad=((width, width), FULL),
            diagonals=((8, 16, wide), FULL),
            queries_turned=((model, width), LOW),
            qkv_grad=((width, 3 * model), LOW),
            qkv_half=((2 * width, model + half), LOW),
            small=((row_bits + 2, 8, model + 2 * LANES), FULL),
            small_in=((row_bits + 1, 8, model + 2 * LANES), FULL),
        )
        scratch.update(held)
        semaphores = dict(
            load_sem=((6,)),
            core_send=((11,)),
            core_recv=((11,)),
            spread_send=((rows,)),
            spread_recv=((rows,)),
            small_send=((row_bits + 1,)),
            small_recv=((row_bits + 1,)),
            sum_send=((UNITS, row_bits)),
            sum_recv=((UNITS, row_bits)),
        )
        names = [*inputs, *outputs, *scratch, *semaphores]
        sizes = (rows, width, model, ff, heads, buckets, per_row)
        results = pl.pallas_call(
            make_kernel(sizes, names),
            out_shape=[jax.ShapeDtypeStruct(shape, kind) for shape, kind in outputs.values()],
            in_specs=[spec for _, spec in inputs.values()],
            out_specs=[vmem] * len(outputs),
            scratch_shapes=[pltpu.VMEM(shape, kind) for shape, kind in scratch.values()]
            + [pltpu.SemaphoreType.DMA(shape) for shape in semaphores.values()]
            + arrived,
            compiler_params=pltpu.CompilerParams(
                collective_id=0, has_side_effects=True, vmem_limit_bytes=VMEM_LIMIT
            ),
        )(*[array for array, _ in inputs.values()])
        r = SimpleNamespace(**dict(zip(outputs, results)))

        if not direct:
            rows_of = dict(scatter_dimension=0, tiled=True)
            r.w_out_grad = lax.psum_scatter(
                r.grads[:IN_UNIT].reshape(ff, half), "rows", **rows_of
            ).astype(FULL)
            others = r.grads[IN_UNIT:].transpose(1, 0, 2).reshape(model, -1)
            others = lax.psum_scatter(others, "rows", **rows_of).astype(FULL)
            r.w_in_grad = others[:, : ff // 2]
            r.w_attn_out_grad = others[:, ff // 2 : ff // 2 + half]
            r.w_query_key_grad = others[:, ff // 2 + half : ff // 2 + half + model]
            r.w_value_grad = others[:, ff // 2 + half + model :]
            r.w_proj_grad = lax.dynamic_slice_in_dim(
                r.w_proj_whole, lax.axis_index("rows") * own_rows, own_rows, 0
            )
        return (
            r.loss[0, 0],
            r.tokens_grad[None],
            r.gain_attn_grad,
            r.w_query_key_grad,
            r.w_value_grad,
            r.w_attn_out_grad,
            r.rel_bias_grad.T,
            r.gain_ff_grad,
            r.w_in_grad,
            r.w_out_grad,
            r.gain_final_grad,
            r.w_proj_grad,
        )

    return step


def solution(mesh):
    return jax.shard_map(
        on_device(mesh.shape["rows"]),
        mesh=mesh,
        in_specs=(P("tower", "rows", None), P("rows", None), P("rows")) + (P(),) * 12,
        out_specs=(
            P(),
            P("tower", "rows", None),
            P(),
            P("rows", "tower"),
            P("rows", "tower"),
            P("rows", "tower"),
            P(),
            P(),
            P("rows", "tower"),
            P("rows", "tower"),
            P(),
            P("rows", "tower"),
        ),
        check_vma=False,
    )
```

```python
import math
from types import SimpleNamespace

import jax
import jax.numpy as jnp
from jax import lax
from jax.experimental import pallas as pl
from jax.experimental.pallas import tpu as pltpu
from jax.sharding import PartitionSpec as P

EPSILON = 1e-06
LOGIT_SCALE = 50.0
MASKED = -1000000000.0
MESH = pl.DeviceIdType.MESH
LOW = jnp.bfloat16
FULL = jnp.float32
LANES = 128
TILE = 512
VMEM_LIMIT = 60 * 2**20

Z_HALF, Z_PAIR, Y, X = range(4)
X_FIRST = ((X,), (Y,), (Z_PAIR, Z_HALF))
Y_FIRST = ((Y,), (X,), (Z_PAIR, Z_HALF))
Z_THEN_X = ((Z_PAIR,), (X,), (Y, Z_HALF))
Z_THEN_Y = ((Z_PAIR,), (Y,), (X, Z_HALF))
ORDERS = (
    X_FIRST, Y_FIRST, Z_THEN_X, X_FIRST, Y_FIRST, Z_THEN_Y,
    X_FIRST, Y_FIRST, Z_THEN_X, X_FIRST, Y_FIRST, Z_THEN_Y,
)
BITS = 4
STEPS = 3
AFTER_STAGE = (0, 1, 3, 4, 4, 3)
STAGGER = 4
OUT_UNIT, IN_UNIT, ATTN_UNIT, QKV_UNIT, UNITS = 0, 4, 8, 9, 12


def dot(left, right):
    return jnp.dot(left, right, preferred_element_type=FULL)


def dot_nt(left, right):
    return lax.dot_general(left, right, (((1,), (1,)), ((), ())), preferred_element_type=FULL)


def dot_tn(left, right):
    return lax.dot_general(left, right, (((0,), (0,)), ((), ())), preferred_element_type=FULL)


def split(values):
    upper = values.astype(LOW)
    return upper, (values - upper.astype(FULL)).astype(LOW)


def inverse_root(values):
    return lax.rsqrt(jnp.mean(values * values, axis=-1, keepdims=True) + EPSILON)


def norm_backward(values, inverse, gain, upstream):
    scaled = upstream * gain
    gain_grad = jnp.sum(upstream * (values * inverse), axis=0, keepdims=True)
    inner = jnp.mean(scaled * values, axis=-1, keepdims=True)
    return inverse * scaled - values * (inverse * inverse * inverse * inner), gain_grad


def tiles(total, size):
    def over(body):
        def step(index, carry):
            body(index, pl.ds(pl.multiple_of(index * size, size), size))
            return carry

        lax.fori_loop(0, total // size, step, 0)

    return over


def in_kernel_sums(rows, model):
    return rows == 2**BITS and model % (16 * rows) == 0


def make_kernel(sizes, names):
    rows, width, model, ff, heads, buckets, per_row = sizes
    head_size = model // heads
    half = model // 2
    ff_half = ff // 2
    queries = rows * per_row
    parts = model // LANES
    query_message = parts * per_row
    row_bits = rows.bit_length() - 1
    direct = in_kernel_sums(rows, model)

    def kernel(*args):
        r = SimpleNamespace(**dict(zip(names, args)))
        arrived = args[len(names) :]
        tower = lax.axis_index("tower")
        row = lax.axis_index("rows")
        partner = (1 - tower, row)
        is_query = tower == 0
        own_rows = model // rows

        barrier = pltpu.get_barrier_semaphore()
        pl.semaphore_signal(barrier, inc=1, device_id=partner, device_id_type=MESH)

        def greet(step, carry):
            peer = (tower, jnp.bitwise_xor(row, step))
            pl.semaphore_signal(barrier, inc=1, device_id=peer, device_id_type=MESH)
            return carry

        lax.fori_loop(1, rows, greet, 0)

        loads = [
            pltpu.make_async_copy(far, near, r.load_sem.at[index])
            for index, (far, near) in enumerate(
                (
                    (r.w_query_key, r.w_query_key_here),
                    (r.w_value, r.w_value_here),
                    (r.w_attn_out, r.w_attn_out_here),
                    (r.w_in, r.w_in_here),
                    (r.w_out, r.w_out_here),
                    (r.w_proj, r.w_proj_here),
                )
            )
        ]
        for load in loads:
            load.start()

        def to_partner(src, dst, index):
            return pltpu.make_async_remote_copy(
                src_ref=src,
                dst_ref=dst,
                send_sem=r.core_send.at[index],
                recv_sem=r.core_recv.at[index],
                device_id=partner,
                device_id_type=MESH,
            )

        coordinate = [jnp.bitwise_and(lax.shift_right_logical(row, 3 - bit), 1) for bit in range(BITS)]

        def piece(unit, step, code):
            place = [slice(None)] * BITS
            for bits in ORDERS[unit][:step]:
                for bit in bits:
                    place[bit] = coordinate[bit]
            for spot, bit in enumerate(ORDERS[unit][step]):
                place[bit] = jnp.bitwise_xor(coordinate[bit], (code >> spot) & 1)
            return place

        def exchange(unit, step, code=1, half=None):
            place = piece(unit, step, code)
            into = arrived[step].at[unit]
            index = step + code - 1
            if step == STEPS - 1:
                into = into.at[code - 1]
            elif half is not None:
                place[Z_PAIR] = jnp.bitwise_xor(coordinate[Z_PAIR], 1 - half)
                into = into.at[:, place[Z_PAIR]]
                index = STEPS + 2 + half
            peer = row
            for spot, bit in enumerate(ORDERS[unit][step]):
                peer = jnp.bitwise_xor(peer, ((code >> spot) & 1) << (3 - bit))
            return pltpu.make_async_remote_copy(
                src_ref=r.grads.at[(unit, *place)],
                dst_ref=into,
                send_sem=r.sum_send.at[unit, index],
                recv_sem=r.sum_recv.at[unit, index],
                device_id=(tower, peer),
                device_id_type=MESH,
            )

        def exchanges(unit, step):
            if step == STEPS - 1:
                return [exchange(unit, step, code) for code in (1, 2, 3)]
            if step == 0 and unit < IN_UNIT and Z_PAIR not in ORDERS[unit][0]:
                return [exchange(unit, step, 1, half) for half in range(2)]
            return [exchange(unit, step)]

        def begin(unit):
            if direct:
                for copy in exchanges(unit, 0):
                    copy.start()

        def finish(unit, step):
            for copy in exchanges(unit, step):
                copy.wait_recv()
            kept = (unit, *piece(unit, step, 0))
            if step + 1 < STEPS:
                r.grads[kept] = r.grads[kept] + arrived[step][unit]
                for copy in exchanges(unit, step + 1):
                    copy.start()
                return
            total = r.grads[kept].astype(FULL)
            for other in range(3):
                total = total + arrived[step][unit, other].astype(FULL)
            if unit < IN_UNIT:
                spot = unit - OUT_UNIT
                r.w_out_grad[spot * own_rows : (spot + 1) * own_rows, :] = total
            elif unit < ATTN_UNIT:
                spot = unit - IN_UNIT
                r.w_in_grad[:, spot * half : (spot + 1) * half] = total
            elif unit < QKV_UNIT:
                r.w_attn_out_grad[...] = total
            elif unit < UNITS - 1:
                spot = unit - QKV_UNIT
                r.w_query_key_grad[:, spot * half : (spot + 1) * half] = total
            else:
                r.w_value_grad[...] = total

        events = sorted(
            ((unit, step) for unit in range(UNITS) for step in range(STEPS)),
            key=lambda event: (event[0] + STAGGER * event[1], -event[1]),
        )

        def after_stage(stage):
            if direct:
                first = sum(AFTER_STAGE[:stage])
                for event in events[first : first + AFTER_STAGE[stage]]:
                    finish(*event)

        def keep(unit, value):
            value = value.astype(LOW)
            r.grads[unit] = value.reshape(r.grads.shape[1:]) if direct else value

        lane = lax.broadcasted_iota(jnp.int32, (8, width), 1)
        doc_row = jnp.where(lane < r.doc_lengths[0], 0, 1)
        seg_row = jnp.where(is_query, jnp.broadcast_to(r.query_segments[...], (8, width)), doc_row)
        eye = (
            lax.broadcasted_iota(jnp.int32, (width, width), 0)
            == lax.broadcasted_iota(jnp.int32, (width, width), 1)
        ).astype(FULL)
        seg_column = dot_nt(eye.astype(LOW), seg_row.astype(FULL).astype(LOW))[:, 0:1].astype(jnp.int32)
        member = (seg_row == lax.broadcasted_iota(jnp.int32, (8, width), 0)).astype(FULL)
        share = 1.0 / jnp.maximum(jnp.sum(member, axis=-1, keepdims=True), 1.0)

        wide = 2 * width
        table = jnp.concatenate(
            [r.bucket_table[...], jnp.zeros((1, 1), jnp.int32)], axis=1
        )
        turned = (
            lax.broadcasted_iota(jnp.int32, (wide, wide), 0)
            + lax.broadcasted_iota(jnp.int32, (wide, wide), 1)
            == wide - 2
        ).astype(FULL).astype(LOW)
        table_low = jnp.broadcast_to(table.astype(FULL), (8, wide)).astype(LOW)
        table_turned = dot(table_low, turned)[0:1]
        hot = (
            table_turned.astype(jnp.int32) == lax.broadcasted_iota(jnp.int32, (buckets, wide), 0)
        ).astype(FULL)
        r.hot[...] = hot.astype(LOW)
        bias_upper, bias_lower = split(r.rel_bias[...])
        bias_last = (r.rel_bias[...] - bias_upper.astype(FULL) - bias_lower.astype(FULL)).astype(LOW)
        hot_low = hot.astype(LOW)
        r.table[0:heads, :] = dot(bias_upper, hot_low) + dot(bias_lower, hot_low) + dot(bias_last, hot_low)

        r.small[0] = jnp.zeros((8, model + 2 * LANES), FULL)
        r.diagonals[...] = jnp.zeros_like(r.diagonals)

        inputs = r.tokens[...].astype(FULL)
        normed = (inputs * inverse_root(inputs) * r.gain_attn[...][None]).astype(LOW)
        r.normed_one[0:width, :] = normed
        loads[0].wait()
        w_query_key = r.w_query_key_here

        @tiles(2 * model, TILE)
        def _(index, columns):
            r.qkv[:, columns] = dot(r.normed_one[0:width, :], w_query_key[:, columns]).astype(LOW)

        loads[1].wait()
        w_value = r.w_value_here
        r.qkv[:, 2 * model :] = dot(normed, w_value[...]).astype(LOW)

        r.keys_turned[...] = r.qkv[:, model : 2 * model].T
        r.values_turned[...] = r.qkv[:, 2 * model :].T

        allowed = seg_column == seg_row[0:1]
        r.allowed[...] = allowed.astype(FULL)

        @tiles(model, 2 * head_size)
        def _(pair, columns):
            query = r.qkv[:, columns]
            key = r.qkv[:, pl.ds(pl.multiple_of(model + pair * 2 * head_size, LANES), 2 * head_size)]
            place = lax.broadcasted_iota(jnp.int32, (width, 2 * head_size), 1)
            for side in range(2):
                head = 2 * pair + side
                own = (place >= head_size) if side else (place < head_size)
                score = dot_nt(jnp.where(own, key, jnp.zeros_like(key)), query)
                line = jnp.broadcast_to(r.table[pl.ds(head, 1), :], (width, wide))
                bias = pltpu.roll(line, width + 1, 1, stride=1, stride_axis=0)[:, :width]
                score = jnp.where(r.allowed[...] > 0.5, score + bias, MASKED)
                weights = jnp.exp(score - jnp.max(score, axis=0, keepdims=True))
                prob = (weights * (1.0 / jnp.sum(weights, axis=0, keepdims=True))).astype(LOW)
                r.probs[head] = prob
                here = pl.ds(pl.multiple_of(head * head_size, head_size), head_size)
                r.mixed_turned[here, :] = dot(r.values_turned[here, :], prob).astype(LOW)

        mixed = r.mixed_turned[...].T
        r.mixed[0:width, :] = mixed
        pl.semaphore_wait(barrier, rows)
        send_one = to_partner(r.normed_one.at[0:width], r.normed_one.at[width : 2 * width], 0)
        send_one.start()
        send_mixed = to_partner(r.mixed.at[0:width], r.mixed.at[width : 2 * width], 1)
        send_mixed.start()
        loads[2].wait()
        w_attn_out = r.w_attn_out_here
        hidden = r.tokens[...].astype(FULL) + dot(mixed, w_attn_out[...])
        r.hidden_one[...] = hidden
        r.normed_two[0:width, :] = (hidden * inverse_root(hidden) * r.gain_ff[...][None]).astype(LOW)
        send_two = to_partner(r.normed_two.at[0:width], r.normed_two.at[width : 2 * width], 2)
        send_two.start()

        loads[3].wait()
        w_in = r.w_in_here
        bend = math.sqrt(2.0 / math.pi)

        @tiles(ff, TILE)
        def _(index, columns):
            inner = dot(r.normed_two[0:width, :], w_in[:, columns])
            square = inner * inner
            curve = jnp.tanh(bend * (inner * (1.0 + 0.044715 * square)))
            lift = 0.5 * (1.0 + curve)
            r.active[0:width, columns] = (inner * lift).astype(LOW)
            slope = 0.5 * inner * (1.0 - curve * curve) * (bend * (1.0 + 3 * 0.044715 * square))
            r.slope[:, columns] = (lift + slope).astype(LOW)

        send_active = to_partner(r.active.at[0:width], r.active.at[width : 2 * width], 3)
        send_active.start()
        loads[4].wait()
        w_out = r.w_out_here

        hidden = r.hidden_one[...] + dot(r.active[0:width, :], w_out[...])
        r.hidden_two[...] = hidden
        normed_upper, normed_lower = split(hidden * inverse_root(hidden) * r.gain_final[...][None])
        member_low = member.astype(LOW)
        pooled = (dot(member_low, normed_upper) + dot(member_low, normed_lower)) * share
        pooled = pooled.astype(LOW).astype(FULL)

        own_queries = r.pooled_queries.at[pl.ds(pl.multiple_of(row * query_message, 8), query_message)]
        own_doc = r.pooled_docs.at[pl.ds(pl.multiple_of(row * 8, 8), 8)]

        def spread(block, act):
            def step(index, carry):
                act(
                    pltpu.make_async_remote_copy(
                        src_ref=block,
                        dst_ref=block,
                        send_sem=r.spread_send.at[index],
                        recv_sem=r.spread_recv.at[index],
                        device_id=(tower, jnp.bitwise_xor(row, index)),
                        device_id_type=MESH,
                    )
                )
                return carry

            lax.fori_loop(1, rows, step, 0)

        relay_queries = to_partner(r.pooled_queries, r.pooled_queries, 4)
        relay_docs = to_partner(r.pooled_docs, r.pooled_docs, 5)

        @pl.when(is_query)
        def _():
            for part in range(parts):
                spot = pl.multiple_of(row * query_message, 8) + part * per_row
                r.pooled_queries[pl.ds(spot, per_row), :] = pooled[
                    0:per_row, part * LANES : (part + 1) * LANES
                ]
            spread(own_queries, lambda copy: copy.start())
            spread(own_queries, lambda copy: copy.wait())
            relay_queries.start()
            relay_docs.wait_recv()
            relay_queries.wait_send()

        @pl.when(jnp.logical_not(is_query))
        def _():
            own_doc[...] = jnp.zeros((8, LANES), FULL)
            for part in range(parts):
                spot = pl.multiple_of(row * 8, 8) + part
                r.pooled_docs[pl.ds(spot, 1), :] = pooled[0:1, part * LANES : (part + 1) * LANES]
            spread(own_doc, lambda copy: copy.start())
            spread(own_doc, lambda copy: copy.wait())
            relay_docs.start()
            relay_queries.wait_recv()
            relay_docs.wait_send()

        for part in range(parts):
            lanes = slice(part * LANES, (part + 1) * LANES)
            for query in range(per_row):
                r.pooled[query * rows : (query + 1) * rows, lanes] = r.pooled_queries[
                    pl.ds(part * per_row + query, rows, stride=query_message), :
                ]
            r.pooled[queries:, lanes] = r.pooled_docs[pl.ds(part, rows, stride=8), :]

        loads[5].wait()
        w_proj = r.w_proj_here
        pooled_low = r.pooled[...].astype(LOW)
        projected = dot(pooled_low, w_proj[...])
        scale = lax.rsqrt(jnp.sum(projected * projected, axis=-1, keepdims=True) + EPSILON)
        embed = (projected * scale).astype(LOW)
        query_embed, doc_embed = embed[:queries], embed[queries:]
        logits = LOGIT_SCALE * dot_nt(query_embed, doc_embed)
        target = jnp.concatenate(
            [
                (
                    jnp.broadcast_to(r.positives[query : query + 1, :].astype(FULL), (rows, rows)).T
                    == lax.broadcasted_iota(jnp.int32, (rows, rows), 1).astype(FULL)
                ).astype(FULL)
                for query in range(per_row)
            ],
            axis=0,
        )
        highest = jnp.max(logits, axis=-1, keepdims=True)
        log_sum = highest + jnp.log(jnp.sum(jnp.exp(logits - highest), axis=-1, keepdims=True))
        missed = log_sum - jnp.sum(logits * target, axis=-1, keepdims=True)
        r.loss[...] = jnp.sum(missed, axis=0, keepdims=True) / queries
        logits_grad = (jnp.exp(logits - log_sum) - target) * (LOGIT_SCALE / queries)
        grad_upper, grad_lower = split(logits_grad)
        embed_grad = jnp.concatenate(
            [
                dot(grad_upper, doc_embed) + dot(grad_lower, doc_embed),
                dot_tn(grad_upper, query_embed) + dot_tn(grad_lower, query_embed),
            ],
            axis=0,
        )
        along = jnp.sum(embed_grad * projected, axis=-1, keepdims=True)
        proj_grad = (scale * embed_grad - projected * (scale * scale * scale * along)).astype(LOW)
        r.proj_grad[...] = proj_grad.astype(FULL)
        r.own_grad[...] = jnp.zeros_like(r.own_grad)

        @pl.when(is_query)
        def _():
            for query in range(per_row):
                r.own_grad[query : query + 1, :] = r.proj_grad[pl.ds(query * rows + row, 1), :]

        @pl.when(jnp.logical_not(is_query))
        def _():
            r.own_grad[0:1, :] = r.proj_grad[pl.ds(queries + row, 1), :]

        pooled_grad = dot_nt(r.own_grad[...].astype(LOW), w_proj[...])[0:8] * share
        final_grad = jnp.zeros((width, model), FULL)
        for query in range(per_row):
            final_grad = jnp.where(seg_column == query, pooled_grad[query : query + 1, :], final_grad)

        hidden = r.hidden_two[...]
        hidden_grad, r.small[0, 2:3, 0:model] = norm_backward(
            hidden, inverse_root(hidden), r.gain_final[...][None], final_grad
        )
        r.hidden_grad[...] = hidden_grad
        r.branch[...] = hidden_grad.astype(LOW)
        own_half = pl.ds(pl.multiple_of(tower * half, LANES), half)
        other_half = pl.ds(pl.multiple_of((1 - tower) * half, LANES), half)
        send_branch = to_partner(r.branch.at[:, other_half], r.branch_half.at[width : 2 * width], 6)
        send_branch.start()
        r.branch_half[0:width, :] = r.branch[:, own_half]

        r.proj_grad_half[...] = r.proj_grad[:, own_half].astype(LOW)
        r.w_proj_whole[...] = dot_tn(r.pooled[...].astype(LOW), r.proj_grad_half[...])
        if direct:
            r.w_proj_grad[...] = r.w_proj_whole[pl.ds(pl.multiple_of(row * own_rows, 8), own_rows), :]

        send_active.wait()
        send_branch.wait()
        per_tile = model * rows // ff
        if direct:
            for half_step in range(2):
                pair = jnp.bitwise_xor(coordinate[Z_PAIR], 1 - half_step)

                def tile(half_z, carry):
                    columns = pl.ds(pl.multiple_of((2 * half_z + pair) * model, model), model)
                    value = dot_tn(r.active[:, columns], r.branch_half[...])
                    for unit in range(per_tile):
                        for spot in range(per_tile):
                            start = (spot * per_tile + unit) * own_rows
                            r.grads[unit, half_z, pair, spot // 2, spot % 2] = value[
                                start : start + own_rows, :
                            ].astype(LOW)
                    return carry

                lax.fori_loop(0, 2, tile, 0)
                for unit in range(OUT_UNIT, IN_UNIT):
                    sends = exchanges(unit, 0)
                    if half_step < len(sends):
                        sends[half_step].start()
        else:

            @tiles(ff, model)
            def _(index, columns):
                keep(index, dot_tn(r.active[:, columns], r.branch_half[...]))

        after_stage(0)

        @tiles(ff, TILE)
        def _(index, columns):
            active_grad = dot_nt(r.branch[...], w_out[columns, :])
            r.inner_grad[:, columns] = (active_grad * r.slope[:, columns].astype(FULL)).astype(LOW)

        own_ff = pl.ds(pl.multiple_of(tower * ff_half, LANES), ff_half)
        other_ff = pl.ds(pl.multiple_of((1 - tower) * ff_half, LANES), ff_half)
        send_inner = to_partner(r.inner_grad.at[:, other_ff], r.inner_half.at[width : 2 * width], 7)
        send_inner.start()
        r.inner_half[0:width, :] = r.inner_grad[:, own_ff]

        r.normed_grad[...] = dot_nt(r.inner_grad[...], w_in[...])
        hidden = r.hidden_one[...]
        through, r.small[0, 1:2, 0:model] = norm_backward(
            hidden, inverse_root(hidden), r.gain_ff[...][None], r.normed_grad[...]
        )
        hidden_grad = r.hidden_grad[...] + through
        r.hidden_grad[...] = hidden_grad
        r.attn[...] = hidden_grad.astype(LOW)
        send_attn = to_partner(r.attn.at[:, other_half], r.attn_half.at[width : 2 * width], 8)
        send_attn.start()
        r.attn_half[0:width, :] = r.attn[:, own_half]

        send_two.wait()
        send_inner.wait()

        @tiles(ff_half, half)
        def _(index, columns):
            keep(IN_UNIT + index, dot_tn(r.normed_two[...], r.inner_half[:, columns]))

        for unit in range(IN_UNIT, ATTN_UNIT):
            begin(unit)
        after_stage(1)

        r.mixed_grad[...] = dot_nt(r.attn[...], w_attn_out[...]).astype(LOW)
        send_mixed.wait()
        send_attn.wait()
        keep(ATTN_UNIT, dot_tn(r.mixed[...], r.attn_half[...]))
        begin(ATTN_UNIT)
        after_stage(2)

        def attention_back(pair):
            columns = pl.ds(pl.multiple_of(pair * 2 * head_size, LANES), 2 * head_size)
            query = r.qkv[:, columns]
            value = r.qkv[:, pl.ds(pl.multiple_of(2 * model + pair * 2 * head_size, LANES), 2 * head_size)]
            mixed_grad = r.mixed_grad[:, columns]
            place = lax.broadcasted_iota(jnp.int32, (width, 2 * head_size), 1)
            key_sides, value_sides = [], []
            for side in range(2):
                head = 2 * pair + side
                own = (place >= head_size) if side else (place < head_size)
                prob_low = r.probs[head]
                prob = prob_low.astype(FULL)
                prob_grad = dot_nt(jnp.where(own, value, jnp.zeros_like(value)), mixed_grad)
                weighted = prob * prob_grad
                score_grad = weighted - prob * jnp.sum(weighted, axis=0, keepdims=True)
                score_low = score_grad.astype(LOW)
                key_sides.append(dot(score_low, query))
                value_sides.append(dot(prob_low, mixed_grad))
                here = pl.ds(pl.multiple_of(head * head_size, head_size), head_size)
                r.queries_turned[here, :] = dot(r.keys_turned[here, :], score_low).astype(LOW)
                r.score_grad[...] = score_grad
                total = jnp.zeros((8, wide), FULL)
                blank = jnp.zeros((8, wide - width), FULL)
                for block in range(width // 8):
                    line = jnp.concatenate([r.score_grad[8 * block : 8 * block + 8, :], blank], axis=1)
                    total = total + pltpu.roll(line, (wide + width - 1 - 8 * block) % wide, 1)
                for line in range(8):
                    r.diagonals[line, pl.ds(head, 1), :] = total[line : line + 1, :]
            after = place >= head_size
            r.qkv_grad[:, pl.ds(pl.multiple_of(model + pair * 2 * head_size, LANES), 2 * head_size)] = (
                jnp.where(after, key_sides[1], key_sides[0]).astype(LOW)
            )
            r.qkv_grad[:, pl.ds(pl.multiple_of(2 * model + pair * 2 * head_size, LANES), 2 * head_size)] = (
                jnp.where(after, value_sides[1], value_sides[0]).astype(LOW)
            )

        pairs = heads // 2
        lax.fori_loop(0, pairs // 2, lambda pair, carry: (attention_back(pair), carry)[1], 0)
        after_stage(3)
        lax.fori_loop(pairs // 2, pairs, lambda pair, carry: (attention_back(pair), carry)[1], 0)
        after_stage(4)
        r.qkv_grad[:, 0:model] = r.queries_turned[...].T

        own_whole = pl.ds(pl.multiple_of(tower * model, LANES), model)
        other_whole = pl.ds(pl.multiple_of((1 - tower) * model, LANES), model)
        own_value = pl.ds(pl.multiple_of(2 * model + tower * half, LANES), half)
        other_value = pl.ds(pl.multiple_of(2 * model + (1 - tower) * half, LANES), half)
        send_qk = to_partner(
            r.qkv_grad.at[:, other_whole], r.qkv_half.at[width : 2 * width, 0:model], 9
        )
        send_value = to_partner(
            r.qkv_grad.at[:, other_value], r.qkv_half.at[width : 2 * width, model:], 10
        )
        send_qk.start()
        send_value.start()
        r.qkv_half[0:width, 0:model] = r.qkv_grad[:, own_whole]
        r.qkv_half[0:width, model:] = r.qkv_grad[:, own_value]

        normed_grad = dot_nt(r.qkv_grad[:, 0 : 2 * model], w_query_key[...])
        r.normed_grad[...] = normed_grad + dot_nt(r.qkv_grad[:, 2 * model :], w_value[...])
        inputs = r.tokens[...].astype(FULL)
        through, r.small[0, 0:1, 0:model] = norm_backward(
            inputs, inverse_root(inputs), r.gain_attn[...][None], r.normed_grad[...]
        )
        r.tokens_grad[...] = r.hidden_grad[...] + through

        offsets = jnp.zeros((16, wide), FULL)
        for line in range(8):
            row_lines = r.diagonals[line]
            offsets = offsets + (pltpu.roll(row_lines, wide - line, 1) if line else row_lines)
        offset_upper, offset_lower = split(offsets)
        hot_low = r.hot[...]
        sums = dot_nt(offset_upper, hot_low) + dot_nt(offset_lower, hot_low)
        r.small[0, 0:8, model : model + buckets] = sums[0:8]
        r.small[0, 0:8, model + LANES : model + LANES + buckets] = sums[8:16]

        send_one.wait()
        send_qk.wait()
        send_value.wait()

        @tiles(model + half, half)
        def _(index, columns):
            keep(QKV_UNIT + index, dot_tn(r.normed_one[...], r.qkv_half[:, columns]))

        for unit in range(QKV_UNIT, UNITS):
            begin(unit)
        after_stage(5)

        def small_begin(bit):
            peer = partner if bit == row_bits else (tower, jnp.bitwise_xor(row, 1 << bit))
            return pltpu.make_async_remote_copy(
                src_ref=r.small.at[bit],
                dst_ref=r.small_in.at[bit],
                send_sem=r.small_send.at[bit],
                recv_sem=r.small_recv.at[bit],
                device_id=peer,
                device_id_type=MESH,
            )

        def small_finish(bit):
            small_begin(bit).wait_recv()
            r.small[bit + 1] = r.small[bit] + r.small_in[bit]
            if bit < row_bits:
                small_begin(bit + 1).start()

        small_begin(0).start()
        if direct:
            rest = events[sum(AFTER_STAGE) :]
            for index, event in enumerate(rest):
                finish(*event)
                if index % 3 == 1 and index // 3 <= row_bits:
                    small_finish(index // 3)
            for unit in range(UNITS):
                for step in range(STEPS):
                    for copy in exchanges(unit, step):
                        copy.wait_send()
        else:
            for bit in range(row_bits + 1):
                small_finish(bit)
        for bit in range(row_bits + 1):
            small_begin(bit).wait_send()
        total = row_bits + 1
        r.gain_attn_grad[...] = r.small[total, 0, 0:model]
        r.gain_ff_grad[...] = r.small[total, 1, 0:model]
        r.gain_final_grad[...] = r.small[total, 2, 0:model]
        r.rel_bias_grad[0:8, :] = r.small[total, 0:8, model : model + buckets]
        r.rel_bias_grad[8:heads, :] = r.small[total, 0 : heads - 8, model + LANES : model + LANES + buckets]

    return kernel


def copy_out(*args):
    *arrays, sems = args
    count = len(arrays) // 2
    copies = [
        pltpu.make_async_copy(arrays[index], arrays[count + index], sems.at[index])
        for index in range(count)
    ]
    for copy in copies:
        copy.start()
    for copy in copies:
        copy.wait()


def on_device(rows):
    def step(
        tokens,
        query_segments,
        doc_lengths,
        bucket_table,
        positives,
        gain_attn,
        w_query_key,
        w_value,
        w_attn_out,
        rel_bias,
        gain_ff,
        w_in,
        w_out,
        gain_final,
        w_proj,
    ):
        width, model = tokens.shape[1:]
        ff = w_in.shape[1]
        buckets, heads = rel_bias.shape
        per_row = positives.shape[1]
        half = model // 2
        wide = 2 * width
        queries = rows * per_row
        row_bits = rows.bit_length() - 1
        own_rows = model // rows
        vmem = pl.BlockSpec(memory_space=pltpu.VMEM)
        smem = pl.BlockSpec(memory_space=pltpu.SMEM)
        hbm = pl.BlockSpec(memory_space=pl.ANY)
        direct = in_kernel_sums(rows, model)
        inputs = dict(
            tokens=(tokens[0], vmem),
            query_segments=(query_segments, vmem),
            doc_lengths=(doc_lengths, smem),
            bucket_table=(bucket_table[None], vmem),
            positives=(positives.T, vmem),
            gain_attn=(gain_attn, vmem),
            w_query_key=(w_query_key, hbm),
            w_value=(w_value, hbm),
            w_attn_out=(w_attn_out, hbm),
            rel_bias=(rel_bias.T, vmem),
            gain_ff=(gain_ff, vmem),
            w_in=(w_in, hbm),
            w_out=(w_out, hbm),
            gain_final=(gain_final, vmem),
            w_proj=(w_proj, hbm),
        )
        outputs = dict(
            loss=((1, 1), FULL),
            tokens_grad=((width, model), FULL),
            gain_attn_grad=((model,), FULL),
            gain_ff_grad=((model,), FULL),
            gain_final_grad=((model,), FULL),
            rel_bias_grad=((heads, buckets), FULL),
        )
        whole = ((model, half), FULL)
        if direct:
            outputs.update(
                w_query_key_grad=((own_rows, model), FULL),
                w_value_grad=((own_rows, half), FULL),
                w_attn_out_grad=((own_rows, half), FULL),
                w_in_grad=((own_rows, ff // 2), FULL),
                w_out_grad=((ff // rows, half), FULL),
                w_proj_grad=((own_rows, half), FULL),
            )
            held = dict(
                w_proj_whole=whole, grads=((UNITS,) + (2,) * row_bits + (own_rows, half), LOW)
            )
            arrived = [
                pltpu.VMEM((UNITS, *count, own_rows, half), LOW) for count in ((2, 2, 2), (2, 2), (3,))
            ]
        else:
            outputs.update(w_proj_whole=whole, grads=((UNITS, model, half), LOW))
            held = {}
            arrived = []
        scratch = dict(
            w_query_key_here=(w_query_key.shape, LOW),
            w_value_here=(w_value.shape, LOW),
            w_attn_out_here=(w_attn_out.shape, LOW),
            w_in_here=(w_in.shape, LOW),
            w_out_here=(w_out.shape, LOW),
            w_proj_here=(w_proj.shape, LOW),
            hot=((buckets, wide), LOW),
            table=((16, wide), FULL),
            allowed=((width, width), FULL),
            normed_one=((2 * width, model), LOW),
            qkv=((width, 3 * model), LOW),
            keys_turned=((model, width), LOW),
            values_turned=((model, width), LOW),
            probs=((heads, width, width), LOW),
            mixed_turned=((model, width), LOW),
            mixed=((2 * width, model), LOW),
            hidden_one=((width, model), FULL),
            normed_two=((2 * width, model), LOW),
            active=((2 * width, ff), LOW),
            slope=((width, ff), LOW),
            hidden_two=((width, model), FULL),
            pooled_queries=((rows * per_row * model // LANES, LANES), FULL),
            pooled_docs=((rows * 8, LANES), FULL),
            pooled=((queries + rows, model), FULL),
            proj_grad=((queries + rows, model), FULL),
            proj_grad_half=((queries + rows, half), LOW),
            own_grad=((16, model), FULL),
            hidden_grad=((width, model), FULL),
            branch=((width, model), LOW),
            branch_half=((2 * width, half), LOW),
            inner_grad=((width, ff), LOW),
            inner_half=((2 * width, ff // 2), LOW),
            normed_grad=((width, model), FULL),
            attn=((width, model), LOW),
            attn_half=((2 * width, half), LOW),
            mixed_grad=((width, model), LOW),
            score_grad=((width, width), FULL),
            diagonals=((8, 16, wide), FULL),
            queries_turned=((model, width), LOW),
            qkv_grad=((width, 3 * model), LOW),
            qkv_half=((2 * width, model + half), LOW),
            small=((row_bits + 2, 8, model + 2 * LANES), FULL),
            small_in=((row_bits + 1, 8, model + 2 * LANES), FULL),
        )
        scratch.update(held)
        semaphores = dict(
            load_sem=((6,)),
            core_send=((11,)),
            core_recv=((11,)),
            spread_send=((rows,)),
            spread_recv=((rows,)),
            small_send=((row_bits + 1,)),
            small_recv=((row_bits + 1,)),
            sum_send=((UNITS, STEPS + 4)),
            sum_recv=((UNITS, STEPS + 4)),
        )
        names = [*inputs, *outputs, *scratch, *semaphores]
        sizes = (rows, width, model, ff, heads, buckets, per_row)
        results = pl.pallas_call(
            make_kernel(sizes, names),
            out_shape=[jax.ShapeDtypeStruct(shape, kind) for shape, kind in outputs.values()],
            in_specs=[spec for _, spec in inputs.values()],
            out_specs=[vmem] * len(outputs),
            scratch_shapes=[pltpu.VMEM(shape, kind) for shape, kind in scratch.values()]
            + [pltpu.SemaphoreType.DMA(shape) for shape in semaphores.values()]
            + arrived,
            compiler_params=pltpu.CompilerParams(
                collective_id=0, has_side_effects=True, vmem_limit_bytes=VMEM_LIMIT
            ),
        )(*[array for array, _ in inputs.values()])
        if direct:
            results = pl.pallas_call(
                copy_out,
                out_shape=[jax.ShapeDtypeStruct(shape, kind) for shape, kind in outputs.values()],
                in_specs=[vmem] * len(outputs),
                out_specs=[hbm] * len(outputs),
                scratch_shapes=[pltpu.SemaphoreType.DMA((len(outputs),))],
            )(*results)
        r = SimpleNamespace(**dict(zip(outputs, results)))

        if not direct:
            rows_of = dict(scatter_dimension=0, tiled=True)
            r.w_out_grad = lax.psum_scatter(
                r.grads[:IN_UNIT].reshape(ff, half), "rows", **rows_of
            ).astype(FULL)
            others = r.grads[IN_UNIT:].transpose(1, 0, 2).reshape(model, -1)
            others = lax.psum_scatter(others, "rows", **rows_of).astype(FULL)
            r.w_in_grad = others[:, : ff // 2]
            r.w_attn_out_grad = others[:, ff // 2 : ff // 2 + half]
            r.w_query_key_grad = others[:, ff // 2 + half : ff // 2 + half + model]
            r.w_value_grad = others[:, ff // 2 + half + model :]
            r.w_proj_grad = lax.dynamic_slice_in_dim(
                r.w_proj_whole, lax.axis_index("rows") * own_rows, own_rows, 0
            )
        return (
            r.loss[0, 0],
            r.tokens_grad[None],
            r.gain_attn_grad,
            r.w_query_key_grad,
            r.w_value_grad,
            r.w_attn_out_grad,
            r.rel_bias_grad.T,
            r.gain_ff_grad,
            r.w_in_grad,
            r.w_out_grad,
            r.gain_final_grad,
            r.w_proj_grad,
        )

    return step


def solution(mesh):
    return jax.shard_map(
        on_device(mesh.shape["rows"]),
        mesh=mesh,
        in_specs=(P("tower", "rows", None), P("rows", None), P("rows")) + (P(),) * 12,
        out_specs=(
            P(),
            P("tower", "rows", None),
            P(),
            P("rows", "tower"),
            P("rows", "tower"),
            P("rows", "tower"),
            P(),
            P(),
            P("rows", "tower"),
            P("rows", "tower"),
            P(),
            P("rows", "tower"),
        ),
        check_vma=False,
    )
```

```python
import functools
import math
from types import SimpleNamespace

import jax
import jax.numpy as jnp
from jax import lax
from jax.experimental import pallas as pl
from jax.experimental.pallas import tpu as pltpu
from jax.sharding import PartitionSpec as P

EPSILON = 1e-06
LOGIT_SCALE = 50.0
MASKED = -1000000000.0
MESH = pl.DeviceIdType.MESH
LOW = jnp.bfloat16
FULL = jnp.float32
LANES = 128
TILE = 512
VMEM_LIMIT = 60 * 2**20

Z_HALF, Z_PAIR, Y, X = range(4)
ORDERS = (
    ((X,), (Y,), (Z_PAIR, Z_HALF)),
    ((Y,), (X,), (Z_PAIR, Z_HALF)),
    ((X, Y), (Z_PAIR,), (Z_HALF,)),
    ((Z_PAIR,), (Y,), (X,), (Z_HALF,)),
    ((Z_PAIR,), (X,), (Y,), (Z_HALF,)),
    ((X,), (Y,), (Z_PAIR, Z_HALF)),
    ((Z_PAIR,), (Y,), (X, Z_HALF)),
    ((Z_PAIR,), (X,), (Y,), (Z_HALF,)),
    ((Y,), (X,), (Z_PAIR, Z_HALF)),
    ((X,), (Y,), (Z_PAIR, Z_HALF)),
    ((Z_PAIR,), (X,), (Y,), (Z_HALF,)),
    ((Y,), (X,), (Z_PAIR, Z_HALF)),
)
PLAN = (
    (),
    (),
    (),
    (),
    (),
    (),
    (),
    (),
    (),
    (),
    ((3, 0),),
    (),
    (),
    ((0, 0), (1, 0),),
    (),
    (),
    ((2, 0),),
    (),
    ((4, 0), (3, 1),),
    (),
    (),
    ((0, 1), (5, 0),),
    (),
    ((6, 0),),
    ((1, 1),),
    ((8, 0), (4, 1),),
    ((3, 2), (7, 0), (5, 1), (2, 1), (12, 0), (0, 2), (6, 1), (9, 0), (12, 1), (8, 1), (12, 2), (10, 0), (11, 0), (4, 2), (7, 1), (1, 2), (3, 3), (12, 3), (9, 1), (5, 2), (2, 2), (10, 1), (7, 2), (12, 4), (6, 2), (11, 1), (8, 2), (4, 3), (10, 2), (9, 2), (7, 3), (11, 2), (10, 3),),
)
BITS = 4
OUT_UNIT, IN_UNIT, ATTN_UNIT, QKV_UNIT, UNITS = 0, 4, 8, 9, 12
SMALL = UNITS


def dot(left, right):
    return jnp.dot(left, right, preferred_element_type=FULL)


def dot_nt(left, right):
    return lax.dot_general(left, right, (((1,), (1,)), ((), ())), preferred_element_type=FULL)


def dot_tn(left, right):
    return lax.dot_general(left, right, (((0,), (0,)), ((), ())), preferred_element_type=FULL)


def split(values):
    upper = values.astype(LOW)
    return upper, (values - upper.astype(FULL)).astype(LOW)


def inverse_root(values):
    return lax.rsqrt(jnp.mean(values * values, axis=-1, keepdims=True) + EPSILON)


def norm_backward(values, inverse, gain, upstream):
    scaled = upstream * gain
    gain_grad = jnp.sum(upstream * (values * inverse), axis=0, keepdims=True)
    inner = jnp.mean(scaled * values, axis=-1, keepdims=True)
    return inverse * scaled - values * (inverse * inverse * inverse * inner), gain_grad


def tiles(total, size):
    def over(body):
        def step(index, carry):
            body(index, pl.ds(pl.multiple_of(index * size, size), size))
            return carry

        lax.fori_loop(0, total // size, step, 0)

    return over


def in_kernel_sums(rows, model):
    return rows == 2**BITS and model % (16 * rows) == 0


def make_kernel(sizes, names, small_inputs):
    rows, width, model, ff, heads, buckets, per_row, count_in, count_out = sizes
    head_size = model // heads
    half = model // 2
    ff_half = ff // 2
    queries = rows * per_row
    parts = model // LANES
    query_message = parts * per_row
    row_bits = rows.bit_length() - 1
    direct = in_kernel_sums(rows, model)

    def kernel(*args):
        r = SimpleNamespace(**dict(zip(names, args)))
        extra = args[len(names) :]
        near_inputs, extra = extra[: len(small_inputs)], extra[len(small_inputs) :]
        far_inputs = [getattr(r, name) for name in small_inputs]
        r.__dict__.update(zip(small_inputs, near_inputs))
        far_results = args[count_in : count_in + count_out]
        near_results = extra[:count_out]
        leaving = []
        if direct:
            r.__dict__.update(zip(names[count_in : count_in + count_out], near_results))

        def publish(result):
            if direct:
                index = next(index for index, ref in enumerate(near_results) if ref is result)
                copy = pltpu.make_async_copy(result, far_results[index], r.leave_sem.at[index])
                copy.start()
                leaving.append(copy)

        parts_left = [4, 4, 1, 2, 1]

        def finished(group, result):
            parts_left[group] -= 1
            if not parts_left[group]:
                publish(result)

        landing = []
        if direct:
            landings = iter(extra[count_out:])
            landing = [[next(landings) for _ in steps] for steps in ORDERS]
        tower = lax.axis_index("tower")
        row = lax.axis_index("rows")
        partner = (1 - tower, row)
        is_query = tower == 0
        own_rows = model // rows

        barrier = pltpu.get_barrier_semaphore()
        pl.semaphore_signal(barrier, inc=1, device_id=partner, device_id_type=MESH)

        def greet(step, carry):
            peer = (tower, jnp.bitwise_xor(row, step))
            pl.semaphore_signal(barrier, inc=1, device_id=peer, device_id_type=MESH)
            return carry

        lax.fori_loop(1, rows, greet, 0)

        loads = [
            pltpu.make_async_copy(far, near, r.load_sem.at[index])
            for index, (far, near) in enumerate(
                (
                    (r.w_query_key, r.w_query_key_here),
                    (r.w_value, r.w_value_here),
                    (r.w_attn_out, r.w_attn_out_here),
                    (r.w_in, r.w_in_here),
                    (r.w_out, r.w_out_here),
                    (r.w_proj, r.w_proj_here),
                    *zip(far_inputs, near_inputs),
                )
            )
        ]

        def load(index):
            loads[index].start()

        def loaded(index):
            loads[index].wait()

        for index in range(6, len(loads)):
            load(index)
        for index in range(6):
            load(index)
        for index in range(6, len(loads)):
            loaded(index)

        def to_partner(src, dst, index):
            return pltpu.make_async_remote_copy(
                src_ref=src,
                dst_ref=dst,
                send_sem=r.core_send.at[index],
                recv_sem=r.core_recv.at[index],
                device_id=partner,
                device_id_type=MESH,
            )

        coordinate = [jnp.bitwise_and(lax.shift_right_logical(row, 3 - bit), 1) for bit in range(BITS)]

        def piece(unit, step, code):
            place = [slice(None)] * BITS
            for bits in ORDERS[unit][:step]:
                for bit in bits:
                    place[bit] = coordinate[bit]
            for spot, bit in enumerate(ORDERS[unit][step]):
                place[bit] = jnp.bitwise_xor(coordinate[bit], (code >> spot) & 1)
            return place

        def exchange(unit, step, code, half=None):
            place = piece(unit, step, code)
            into = landing[unit][step]
            if len(ORDERS[unit][step]) > 1:
                into = into.at[code - 1]
            elif half is not None:
                place[Z_PAIR] = jnp.bitwise_xor(coordinate[Z_PAIR], 1 - half)
                into = into.at[:, place[Z_PAIR]]
            peer = row
            for spot, bit in enumerate(ORDERS[unit][step]):
                peer = jnp.bitwise_xor(peer, ((code >> spot) & 1) << (3 - bit))
            return pltpu.make_async_remote_copy(
                src_ref=r.grads.at[(unit, *place)],
                dst_ref=into,
                send_sem=r.sum_send.at[unit],
                recv_sem=r.sum_recv.at[unit, step],
                device_id=(tower, peer),
                device_id_type=MESH,
            )

        def exchanges(unit, step):
            bits = ORDERS[unit][step]
            if step == 0 and unit < IN_UNIT and bits[0] in (X, Y) and len(bits) == 1:
                return [exchange(unit, step, 1, half) for half in range(2)]
            return [exchange(unit, step, code) for code in range(1, 2 ** len(bits))]

        def all_of(ref, send_sem, recv_sem):
            return pltpu.make_async_remote_copy(
                src_ref=ref,
                dst_ref=ref,
                send_sem=send_sem,
                recv_sem=recv_sem,
                device_id=partner,
                device_id_type=MESH,
            )

        def begin(unit):
            if direct:
                for copy in exchanges(unit, 0):
                    copy.start()

        def finish(unit, step):
            if unit == SMALL:
                small_finish(step)
                return
            all_of(landing[unit][step], r.sum_send.at[unit], r.sum_recv.at[unit, step]).wait_recv()
            kept = (unit, *piece(unit, step, 0))
            come = landing[unit][step]
            several = len(ORDERS[unit][step]) > 1
            if step + 1 < len(ORDERS[unit]):
                if several:
                    total = r.grads[kept].astype(FULL)
                    for other in range(3):
                        total = total + come[other].astype(FULL)
                    r.grads[kept] = total.astype(LOW)
                else:
                    r.grads[kept] = r.grads[kept] + come[...]
                for copy in exchanges(unit, step + 1):
                    copy.start()
                return
            total = r.grads[kept].astype(FULL)
            if several:
                for other in range(3):
                    total = total + come[other].astype(FULL)
            else:
                total = total + come[...].astype(FULL)
            if unit < IN_UNIT:
                spot = unit - OUT_UNIT
                r.w_out_grad[spot * own_rows : (spot + 1) * own_rows, :] = total
                finished(0, r.w_out_grad)
            elif unit < ATTN_UNIT:
                spot = unit - IN_UNIT
                r.w_in_grad[:, spot * half : (spot + 1) * half] = total
                finished(1, r.w_in_grad)
            elif unit < QKV_UNIT:
                r.w_attn_out_grad[...] = total
                finished(2, r.w_attn_out_grad)
            elif unit < UNITS - 1:
                spot = unit - QKV_UNIT
                r.w_query_key_grad[:, spot * half : (spot + 1) * half] = total
                finished(3, r.w_query_key_grad)
            else:
                r.w_value_grad[...] = total
                finished(4, r.w_value_grad)

        def small_exchange(step):
            peer = partner if step == row_bits else (tower, jnp.bitwise_xor(row, 1 << step))
            return pltpu.make_async_remote_copy(
                src_ref=r.small.at[step],
                dst_ref=r.small_in.at[step],
                send_sem=r.small_send.at[0],
                recv_sem=r.small_recv.at[step],
                device_id=peer,
                device_id_type=MESH,
            )

        def small_finish(step):
            small_exchange(step).wait_recv()
            r.small[step + 1] = r.small[step] + r.small_in[step]
            if step < row_bits:
                small_exchange(step + 1).start()

        def keep(unit, value):
            value = value.astype(LOW)
            r.grads[unit] = value.reshape(r.grads.shape[1:]) if direct else value

        lane = lax.broadcasted_iota(jnp.int32, (8, width), 1)
        doc_row = jnp.where(lane < r.doc_lengths[0], 0, 1)
        seg_row = jnp.where(is_query, jnp.broadcast_to(r.query_segments[...], (8, width)), doc_row)
        eye = (
            lax.broadcasted_iota(jnp.int32, (width, width), 0)
            == lax.broadcasted_iota(jnp.int32, (width, width), 1)
        ).astype(FULL)
        seg_column = dot_nt(eye.astype(LOW), seg_row.astype(FULL).astype(LOW))[:, 0:1].astype(jnp.int32)
        member = (seg_row == lax.broadcasted_iota(jnp.int32, (8, width), 0)).astype(FULL)
        share = 1.0 / jnp.maximum(jnp.sum(member, axis=-1, keepdims=True), 1.0)

        wide = 2 * width
        table = jnp.concatenate(
            [r.bucket_table[...], jnp.zeros((1, 1), jnp.int32)], axis=1
        )
        turned = (
            lax.broadcasted_iota(jnp.int32, (wide, wide), 0)
            + lax.broadcasted_iota(jnp.int32, (wide, wide), 1)
            == wide - 2
        ).astype(FULL).astype(LOW)
        table_low = jnp.broadcast_to(table.astype(FULL), (8, wide)).astype(LOW)
        table_turned = dot(table_low, turned)[0:1]
        hot = (
            table_turned.astype(jnp.int32) == lax.broadcasted_iota(jnp.int32, (buckets, wide), 0)
        ).astype(FULL)
        r.hot[...] = hot.astype(LOW)
        bias_upper, bias_lower = split(r.rel_bias[...])
        bias_last = (r.rel_bias[...] - bias_upper.astype(FULL) - bias_lower.astype(FULL)).astype(LOW)
        hot_low = hot.astype(LOW)
        r.table[0:heads, :] = dot(bias_upper, hot_low) + dot(bias_lower, hot_low) + dot(bias_last, hot_low)

        allowed = seg_column == seg_row[0:1]

        def spread_bias(head, carry):
            line = jnp.broadcast_to(r.table[pl.ds(head, 1), :], (width, wide))
            bias = pltpu.roll(line, width + 1, 1, stride=1, stride_axis=0)[:, :width]
            r.bias[head] = jnp.where(allowed, bias, MASKED)
            return carry

        lax.fori_loop(0, heads, spread_bias, 0)
        r.small[0] = jnp.zeros((8, model + 2 * LANES), FULL)
        r.diagonals[...] = jnp.zeros_like(r.diagonals)

        inputs = r.tokens[...].astype(FULL)
        normed = (inputs * inverse_root(inputs) * r.gain_attn[...][None]).astype(LOW)
        r.normed_one[0:width, :] = normed
        loaded(0)
        w_query_key = r.w_query_key_here

        for start in range(0, 2 * model, TILE):
            columns = slice(start, start + TILE)
            r.qkv[:, columns] = dot(normed, w_query_key[:, columns]).astype(LOW)

        loaded(1)
        w_value = r.w_value_here
        r.qkv[:, 2 * model :] = dot(normed, w_value[...]).astype(LOW)

        r.keys_turned[...] = r.qkv[:, model : 2 * model].T
        r.values_turned[...] = r.qkv[:, 2 * model :].T

        place = lax.broadcasted_iota(jnp.int32, (width, 2 * head_size), 1)

        def attend(pair):
            start = pair * 2 * head_size
            query = r.qkv[:, start : start + 2 * head_size]
            key = r.qkv[:, model + start : model + start + 2 * head_size]
            for side in range(2):
                head = 2 * pair + side
                own = (place >= head_size) if side else (place < head_size)
                score = dot_nt(jnp.where(own, key, jnp.zeros_like(key)), query) + r.bias[head]
                weights = jnp.exp(score - jnp.max(score, axis=0, keepdims=True))
                r.probs[head] = (weights * (1.0 / jnp.sum(weights, axis=0, keepdims=True))).astype(LOW)

        def mix(pair):
            for head in (2 * pair, 2 * pair + 1):
                here = slice(head * head_size, (head + 1) * head_size)
                r.mixed_turned[here, :] = dot(r.values_turned[here, :], r.probs[head]).astype(LOW)

        for pair in range(heads // 2):
            attend(pair)
            if pair:
                mix(pair - 1)
        mix(heads // 2 - 1)

        mixed = r.mixed_turned[...].T
        r.mixed[0:width, :] = mixed
        pl.semaphore_wait(barrier, rows)
        send_one = to_partner(r.normed_one.at[0:width], r.normed_one.at[width : 2 * width], 0)
        send_one.start()
        send_mixed = to_partner(r.mixed.at[0:width], r.mixed.at[width : 2 * width], 1)
        send_mixed.start()
        loaded(2)
        w_attn_out = r.w_attn_out_here
        hidden = r.tokens[...].astype(FULL) + dot(mixed, w_attn_out[...])
        r.hidden_one[...] = hidden
        normed_two = (hidden * inverse_root(hidden) * r.gain_ff[...][None]).astype(LOW)
        r.normed_two[0:width, :] = normed_two
        send_two = to_partner(r.normed_two.at[0:width], r.normed_two.at[width : 2 * width], 2)
        send_two.start()

        loaded(3)
        w_in = r.w_in_here
        bend = math.sqrt(2.0 / math.pi)

        for start in range(0, ff, TILE):
            columns = slice(start, start + TILE)
            inner = dot(normed_two, w_in[:, columns])
            curve = jnp.tanh(inner * (bend + (bend * 0.044715) * (inner * inner)))
            r.inner[:, columns] = inner
            r.active[0:width, columns] = (inner * (0.5 + 0.5 * curve)).astype(LOW)

        send_active = to_partner(r.active.at[0:width], r.active.at[width : 2 * width], 3)
        send_active.start()
        loaded(4)
        w_out = r.w_out_here

        hidden = r.hidden_one[...] + dot(r.active[0:width, :], w_out[...])
        r.hidden_two[...] = hidden
        normed_upper, normed_lower = split(hidden * inverse_root(hidden) * r.gain_final[...][None])
        member_low = member.astype(LOW)
        pooled = (dot(member_low, normed_upper) + dot(member_low, normed_lower)) * share
        pooled = pooled.astype(LOW).astype(FULL)

        own_queries = r.pooled_queries.at[pl.ds(pl.multiple_of(row * query_message, 8), query_message)]
        own_doc = r.pooled_docs.at[pl.ds(pl.multiple_of(row * 8, 8), 8)]

        def spread(block, whole):
            for index in range(1, rows):
                pltpu.make_async_remote_copy(
                    src_ref=block,
                    dst_ref=block,
                    send_sem=r.spread_sem.at[0],
                    recv_sem=r.spread_sem.at[1],
                    device_id=(tower, jnp.bitwise_xor(row, rows - index)),
                    device_id_type=MESH,
                ).start()
            others = whole.at[0 : whole.shape[0] // rows * (rows - 1)]
            every = all_of(others, r.spread_sem.at[0], r.spread_sem.at[1])
            every.wait_send()
            every.wait_recv()

        relay_queries = to_partner(r.pooled_queries, r.pooled_queries, 4)
        relay_docs = to_partner(r.pooled_docs, r.pooled_docs, 5)

        @pl.when(is_query)
        def _():
            for part in range(parts):
                spot = pl.multiple_of(row * query_message, 8) + part * per_row
                r.pooled_queries[pl.ds(spot, per_row), :] = pooled[
                    0:per_row, part * LANES : (part + 1) * LANES
                ]
            spread(own_queries, r.pooled_queries)
            relay_queries.start()
            relay_docs.wait_recv()
            relay_queries.wait_send()

        @pl.when(jnp.logical_not(is_query))
        def _():
            own_doc[...] = jnp.zeros((8, LANES), FULL)
            for part in range(parts):
                spot = pl.multiple_of(row * 8, 8) + part
                r.pooled_docs[pl.ds(spot, 1), :] = pooled[0:1, part * LANES : (part + 1) * LANES]
            spread(own_doc, r.pooled_docs)
            relay_docs.start()
            relay_queries.wait_recv()
            relay_docs.wait_send()

        for part in range(parts):
            lanes = slice(part * LANES, (part + 1) * LANES)
            for query in range(per_row):
                r.pooled[query * rows : (query + 1) * rows, lanes] = r.pooled_queries[
                    pl.ds(part * per_row + query, rows, stride=query_message), :
                ]
            r.pooled[queries:, lanes] = r.pooled_docs[pl.ds(part, rows, stride=8), :]

        loaded(5)
        w_proj = r.w_proj_here
        pooled_low = r.pooled[...].astype(LOW)
        projected = dot(pooled_low, w_proj[...])
        scale = lax.rsqrt(jnp.sum(projected * projected, axis=-1, keepdims=True) + EPSILON)
        embed = (projected * scale).astype(LOW)
        query_embed, doc_embed = embed[:queries], embed[queries:]
        logits = LOGIT_SCALE * dot_nt(query_embed, doc_embed)
        target = jnp.concatenate(
            [
                (
                    jnp.broadcast_to(r.positives[query : query + 1, :].astype(FULL), (rows, rows)).T
                    == lax.broadcasted_iota(jnp.int32, (rows, rows), 1).astype(FULL)
                ).astype(FULL)
                for query in range(per_row)
            ],
            axis=0,
        )
        highest = jnp.max(logits, axis=-1, keepdims=True)
        log_sum = highest + jnp.log(jnp.sum(jnp.exp(logits - highest), axis=-1, keepdims=True))
        missed = log_sum - jnp.sum(logits * target, axis=-1, keepdims=True)
        r.loss[...] = jnp.sum(missed, axis=0, keepdims=True) / queries
        publish(r.loss)
        logits_grad = (jnp.exp(logits - log_sum) - target) * (LOGIT_SCALE / queries)
        grad_upper, grad_lower = split(logits_grad)
        embed_grad = jnp.concatenate(
            [
                dot(grad_upper, doc_embed) + dot(grad_lower, doc_embed),
                dot_tn(grad_upper, query_embed) + dot_tn(grad_lower, query_embed),
            ],
            axis=0,
        )
        along = jnp.sum(embed_grad * projected, axis=-1, keepdims=True)
        proj_grad = (scale * embed_grad - projected * (scale * scale * scale * along)).astype(LOW)
        r.proj_grad[...] = proj_grad.astype(FULL)
        r.own_grad[...] = jnp.zeros_like(r.own_grad)

        @pl.when(is_query)
        def _():
            for query in range(per_row):
                r.own_grad[query : query + 1, :] = r.proj_grad[pl.ds(query * rows + row, 1), :]

        @pl.when(jnp.logical_not(is_query))
        def _():
            r.own_grad[0:1, :] = r.proj_grad[pl.ds(queries + row, 1), :]

        pooled_grad = dot_nt(r.own_grad[...].astype(LOW), w_proj[...])[0:8] * share
        final_grad = jnp.zeros((width, model), FULL)
        for query in range(per_row):
            final_grad = jnp.where(seg_column == query, pooled_grad[query : query + 1, :], final_grad)

        hidden = r.hidden_two[...]
        hidden_grad, r.small[0, 2:3, 0:model] = norm_backward(
            hidden, inverse_root(hidden), r.gain_final[...][None], final_grad
        )
        r.hidden_grad[...] = hidden_grad
        r.branch[...] = hidden_grad.astype(LOW)
        own_half = pl.ds(pl.multiple_of(tower * half, LANES), half)
        other_half = pl.ds(pl.multiple_of((1 - tower) * half, LANES), half)
        send_branch = to_partner(r.branch.at[:, other_half], r.branch_half.at[width : 2 * width], 6)
        send_branch.start()
        r.branch_half[0:width, :] = r.branch[:, own_half]

        r.proj_grad_half[...] = r.proj_grad[:, own_half].astype(LOW)
        r.w_proj_whole[...] = dot_tn(r.pooled[...].astype(LOW), r.proj_grad_half[...])
        if direct:
            r.w_proj_grad[...] = r.w_proj_whole[pl.ds(pl.multiple_of(row * own_rows, 8), own_rows), :]
            publish(r.w_proj_grad)

        send_active.wait()
        send_branch.wait()
        per_tile = model * rows // ff
        if direct:
            for half_step in range(2):
                pair = jnp.bitwise_xor(coordinate[Z_PAIR], 1 - half_step)

                def tile(half_z):
                    columns = pl.ds(pl.multiple_of((2 * half_z + pair) * model, model), model)
                    value = dot_tn(r.active[:, columns], r.branch_half[...])
                    for unit in range(per_tile):
                        for spot in range(per_tile):
                            start = (spot * per_tile + unit) * own_rows
                            r.grads[unit, half_z, pair, spot // 2, spot % 2] = value[
                                start : start + own_rows, :
                            ].astype(LOW)

                for half_z in range(2):
                    tile(half_z)
                for unit in range(OUT_UNIT, IN_UNIT):
                    sends = exchanges(unit, 0)
                    if len(sends) == 2:
                        sends[half_step].start()
                    elif half_step == (Z_PAIR not in ORDERS[unit][0]):
                        for copy in sends:
                            copy.start()
        else:

            @tiles(ff, model)
            def _(index, columns):
                keep(index, dot_tn(r.active[:, columns], r.branch_half[...]))

        pieces = []

        def then(body):
            pieces.append(body)
            return body

        def inner_back(index):
            columns = pl.ds(index * TILE, TILE)
            active_grad = dot_nt(r.branch[...], w_out[columns, :])
            inner = r.inner[:, columns]
            square = inner * inner
            curve = jnp.tanh(inner * (bend + (bend * 0.044715) * square))
            slope = (0.5 * inner) * (1.0 - curve * curve) * (bend + (bend * 3 * 0.044715) * square)
            r.inner_grad[:, columns] = (active_grad * ((0.5 + 0.5 * curve) + slope)).astype(LOW)

        for index in range(ff // TILE):
            then(functools.partial(inner_back, index))

        own_ff = pl.ds(pl.multiple_of(tower * ff_half, LANES), ff_half)
        other_ff = pl.ds(pl.multiple_of((1 - tower) * ff_half, LANES), ff_half)
        send_inner = to_partner(r.inner_grad.at[:, other_ff], r.inner_half.at[width : 2 * width], 7)
        send_attn = to_partner(r.attn.at[:, other_half], r.attn_half.at[width : 2 * width], 8)

        @then
        def _():
            send_inner.start()
            r.inner_half[0:width, :] = r.inner_grad[:, own_ff]
            r.normed_grad[...] = dot_nt(r.inner_grad[...], w_in[...])

        @then
        def _():
            hidden = r.hidden_one[...]
            through, r.small[0, 1:2, 0:model] = norm_backward(
                hidden, inverse_root(hidden), r.gain_ff[...][None], r.normed_grad[...]
            )
            hidden_grad = r.hidden_grad[...] + through
            r.hidden_grad[...] = hidden_grad
            r.attn[...] = hidden_grad.astype(LOW)
            send_attn.start()
            r.attn_half[0:width, :] = r.attn[:, own_half]
            send_two.wait()
            send_inner.wait()

        def in_grad(index):
            columns = pl.ds(index * half, half)
            keep(IN_UNIT + index, dot_tn(r.normed_two[...], r.inner_half[:, columns]))
            begin(IN_UNIT + index)

        for index in range(ATTN_UNIT - IN_UNIT):
            then(functools.partial(in_grad, index))

        @then
        def _():
            r.mixed_grad[...] = dot_nt(r.attn[...], w_attn_out[...]).astype(LOW)

        @then
        def _():
            send_mixed.wait()
            send_attn.wait()
            keep(ATTN_UNIT, dot_tn(r.mixed[...], r.attn_half[...]))
            begin(ATTN_UNIT)

        def attention_back(pair):
            columns = pl.ds(pl.multiple_of(pair * 2 * head_size, LANES), 2 * head_size)
            query = r.qkv[:, columns]
            value = r.qkv[:, pl.ds(pl.multiple_of(2 * model + pair * 2 * head_size, LANES), 2 * head_size)]
            mixed_grad = r.mixed_grad[:, columns]
            place = lax.broadcasted_iota(jnp.int32, (width, 2 * head_size), 1)
            key_sides, value_sides = [], []
            for side in range(2):
                head = 2 * pair + side
                own = (place >= head_size) if side else (place < head_size)
                prob_low = r.probs[head]
                prob = prob_low.astype(FULL)
                prob_grad = dot_nt(jnp.where(own, value, jnp.zeros_like(value)), mixed_grad)
                weighted = prob * prob_grad
                score_grad = weighted - prob * jnp.sum(weighted, axis=0, keepdims=True)
                score_low = score_grad.astype(LOW)
                key_sides.append(dot(score_low, query))
                value_sides.append(dot(prob_low, mixed_grad))
                here = pl.ds(pl.multiple_of(head * head_size, head_size), head_size)
                r.queries_turned[here, :] = dot(r.keys_turned[here, :], score_low).astype(LOW)
                r.score_grad[...] = score_grad
                total = jnp.zeros((8, wide), FULL)
                blank = jnp.zeros((8, wide - width), FULL)
                for block in range(width // 8):
                    line = jnp.concatenate([r.score_grad[8 * block : 8 * block + 8, :], blank], axis=1)
                    total = total + pltpu.roll(line, (wide + width - 1 - 8 * block) % wide, 1)
                for line in range(8):
                    r.diagonals[line, pl.ds(head, 1), :] = total[line : line + 1, :]
            after = place >= head_size
            r.qkv_grad[:, pl.ds(pl.multiple_of(model + pair * 2 * head_size, LANES), 2 * head_size)] = (
                jnp.where(after, key_sides[1], key_sides[0]).astype(LOW)
            )
            r.qkv_grad[:, pl.ds(pl.multiple_of(2 * model + pair * 2 * head_size, LANES), 2 * head_size)] = (
                jnp.where(after, value_sides[1], value_sides[0]).astype(LOW)
            )

        for pair in range(heads // 2):
            then(functools.partial(attention_back, pair))

        own_whole = pl.ds(pl.multiple_of(tower * model, LANES), model)
        other_whole = pl.ds(pl.multiple_of((1 - tower) * model, LANES), model)
        own_value = pl.ds(pl.multiple_of(2 * model + tower * half, LANES), half)
        other_value = pl.ds(pl.multiple_of(2 * model + (1 - tower) * half, LANES), half)
        send_qk = to_partner(
            r.qkv_grad.at[:, other_whole], r.qkv_half.at[width : 2 * width, 0:model], 9
        )
        send_value = to_partner(
            r.qkv_grad.at[:, other_value], r.qkv_half.at[width : 2 * width, model:], 10
        )

        @then
        def _():
            r.qkv_grad[:, 0:model] = r.queries_turned[...].T
            send_qk.start()
            send_value.start()
            r.qkv_half[0:width, 0:model] = r.qkv_grad[:, own_whole]
            r.qkv_half[0:width, model:] = r.qkv_grad[:, own_value]
            send_one.wait()
            send_qk.wait()
            send_value.wait()

        def qkv_back(index):
            columns = pl.ds(index * half, half)
            keep(QKV_UNIT + index, dot_tn(r.normed_one[...], r.qkv_half[:, columns]))
            begin(QKV_UNIT + index)

        for index in range(UNITS - QKV_UNIT):
            then(functools.partial(qkv_back, index))

        @then
        def _():
            normed_grad = dot_nt(r.qkv_grad[:, 0 : 2 * model], w_query_key[...])
            r.normed_grad[...] = normed_grad + dot_nt(r.qkv_grad[:, 2 * model :], w_value[...])

        @then
        def _():
            inputs = r.tokens[...].astype(FULL)
            through, r.small[0, 0:1, 0:model] = norm_backward(
                inputs, inverse_root(inputs), r.gain_attn[...][None], r.normed_grad[...]
            )
            r.tokens_grad[...] = r.hidden_grad[...] + through
            publish(r.tokens_grad)

            offsets = jnp.zeros((16, wide), FULL)
            for line in range(8):
                row_lines = r.diagonals[line]
                offsets = offsets + (pltpu.roll(row_lines, wide - line, 1) if line else row_lines)
            offset_upper, offset_lower = split(offsets)
            hot_low = r.hot[...]
            sums = dot_nt(offset_upper, hot_low) + dot_nt(offset_lower, hot_low)
            r.small[0, 0:8, model : model + buckets] = sums[0:8]
            r.small[0, 0:8, model + LANES : model + LANES + buckets] = sums[8:16]
            small_exchange(0).start()

        for index in range(len(pieces) + 1):
            if index:
                pieces[index - 1]()
            if direct:
                for event in PLAN[index]:
                    finish(*event)

        if not direct:
            for step in range(row_bits + 1):
                small_finish(step)
        total = row_bits + 1
        r.gain_attn_grad[...] = r.small[total, 0, 0:model]
        r.gain_ff_grad[...] = r.small[total, 1, 0:model]
        r.gain_final_grad[...] = r.small[total, 2, 0:model]
        r.rel_bias_grad[0:8, :] = r.small[total, 0:8, model : model + buckets]
        r.rel_bias_grad[8:heads, :] = r.small[total, 0 : heads - 8, model + LANES : model + LANES + buckets]
        for result in (r.gain_attn_grad, r.gain_ff_grad, r.gain_final_grad, r.rel_bias_grad):
            publish(result)
        if direct:
            sent = r.w_proj_whole.at[0 : (rows - 1) * own_rows // 2]
            for unit in range(UNITS):
                all_of(sent, r.sum_send.at[unit], r.sum_recv.at[unit, 0]).wait_send()
        all_of(r.small_in, r.small_send.at[0], r.small_recv.at[0]).wait_send()
        for copy in leaving:
            copy.wait()

    return kernel


def copy_out(*args):
    count = (len(args) - 2) // 3
    here = args[2 * count : 3 * count]
    ways = [
        (
            pltpu.make_async_copy(args[index], here[index], args[-2].at[index]),
            pltpu.make_async_copy(here[index], args[count + index], args[-1].at[index]),
        )
        for index in range(count)
    ]
    for come, _ in ways:
        come.start()
    for come, leave in ways:
        come.wait()
        leave.start()
    for _, leave in ways:
        leave.wait()


def on_device(rows):
    def step(
        tokens,
        query_segments,
        doc_lengths,
        bucket_table,
        positives,
        gain_attn,
        w_query_key,
        w_value,
        w_attn_out,
        rel_bias,
        gain_ff,
        w_in,
        w_out,
        gain_final,
        w_proj,
    ):
        width, model = tokens.shape[1:]
        ff = w_in.shape[1]
        buckets, heads = rel_bias.shape
        per_row = positives.shape[1]
        half = model // 2
        wide = 2 * width
        queries = rows * per_row
        row_bits = rows.bit_length() - 1
        own_rows = model // rows
        vmem = pl.BlockSpec(memory_space=pltpu.VMEM)
        hbm = pl.BlockSpec(memory_space=pl.ANY)
        direct = in_kernel_sums(rows, model)
        inputs = dict(
            tokens=(tokens[0], pltpu.VMEM),
            query_segments=(query_segments, pltpu.VMEM),
            doc_lengths=(doc_lengths, pltpu.SMEM),
            bucket_table=(bucket_table[None], pltpu.VMEM),
            positives=(positives.T, pltpu.VMEM),
            gain_attn=(gain_attn, pltpu.VMEM),
            w_query_key=(w_query_key, None),
            w_value=(w_value, None),
            w_attn_out=(w_attn_out, None),
            rel_bias=(rel_bias.T, pltpu.VMEM),
            gain_ff=(gain_ff, pltpu.VMEM),
            w_in=(w_in, None),
            w_out=(w_out, None),
            gain_final=(gain_final, pltpu.VMEM),
            w_proj=(w_proj, None),
        )
        outputs = dict(
            loss=((1, 1), FULL),
            tokens_grad=((width, model), FULL),
            gain_attn_grad=((model,), FULL),
            gain_ff_grad=((model,), FULL),
            gain_final_grad=((model,), FULL),
            rel_bias_grad=((heads, buckets), FULL),
        )
        whole = ((model, half), FULL)
        if direct:
            outputs.update(
                w_query_key_grad=((own_rows, model), FULL),
                w_value_grad=((own_rows, half), FULL),
                w_attn_out_grad=((own_rows, half), FULL),
                w_in_grad=((own_rows, ff // 2), FULL),
                w_out_grad=((ff // rows, half), FULL),
                w_proj_grad=((own_rows, half), FULL),
            )
            held = dict(
                w_proj_whole=whole, grads=((UNITS,) + (2,) * row_bits + (own_rows, half), LOW)
            )
            arrived = []
            for steps in ORDERS:
                left = BITS
                for bits in steps:
                    left -= len(bits)
                    several = (3,) if len(bits) > 1 else ()
                    arrived.append(pltpu.VMEM(several + (2,) * left + (own_rows, half), LOW))
        else:
            outputs.update(w_proj_whole=whole, grads=((UNITS, model, half), LOW))
            held = {}
            arrived = []
        scratch = dict(
            w_query_key_here=(w_query_key.shape, LOW),
            w_value_here=(w_value.shape, LOW),
            w_attn_out_here=(w_attn_out.shape, LOW),
            w_in_here=(w_in.shape, LOW),
            w_out_here=(w_out.shape, LOW),
            w_proj_here=(w_proj.shape, LOW),
            hot=((buckets, wide), LOW),
            table=((16, wide), FULL),
            bias=((heads, width, width), FULL),
            normed_one=((2 * width, model), LOW),
            qkv=((width, 3 * model), LOW),
            keys_turned=((model, width), LOW),
            values_turned=((model, width), LOW),
            probs=((heads, width, width), LOW),
            mixed_turned=((model, width), LOW),
            mixed=((2 * width, model), LOW),
            hidden_one=((width, model), FULL),
            normed_two=((2 * width, model), LOW),
            active=((2 * width, ff), LOW),
            inner=((width, ff), FULL),
            hidden_two=((width, model), FULL),
            pooled_queries=((rows * per_row * model // LANES, LANES), FULL),
            pooled_docs=((rows * 8, LANES), FULL),
            pooled=((queries + rows, model), FULL),
            proj_grad=((queries + rows, model), FULL),
            proj_grad_half=((queries + rows, half), LOW),
            own_grad=((16, model), FULL),
            hidden_grad=((width, model), FULL),
            branch=((width, model), LOW),
            branch_half=((2 * width, half), LOW),
            inner_grad=((width, ff), LOW),
            inner_half=((2 * width, ff // 2), LOW),
            normed_grad=((width, model), FULL),
            attn=((width, model), LOW),
            attn_half=((2 * width, half), LOW),
            mixed_grad=((width, model), LOW),
            score_grad=((width, width), FULL),
            diagonals=((8, 16, wide), FULL),
            queries_turned=((model, width), LOW),
            qkv_grad=((width, 3 * model), LOW),
            qkv_half=((2 * width, model + half), LOW),
            small=((row_bits + 2, 8, model + 2 * LANES), FULL),
            small_in=((row_bits + 1, 8, model + 2 * LANES), FULL),
        )
        scratch.update(held)
        semaphores = dict(
            load_sem=((len(inputs),)),
            core_send=((11,)),
            core_recv=((11,)),
            spread_sem=((2,)),
            small_send=((1,)),
            small_recv=((row_bits + 1,)),
            sum_send=((UNITS,)),
            leave_sem=(len(outputs),),
            sum_recv=((UNITS, BITS)),
        )
        names = [*inputs, *outputs, *scratch, *semaphores]
        small_inputs = [name for name, (_, place) in inputs.items() if place is not None]
        nears = [pltpu.VMEM(shape, kind) for shape, kind in outputs.values()] if direct else []
        sizes = (rows, width, model, ff, heads, buckets, per_row, len(inputs), len(outputs))
        results = pl.pallas_call(
            make_kernel(sizes, names, small_inputs),
            out_shape=[jax.ShapeDtypeStruct(shape, kind) for shape, kind in outputs.values()],
            in_specs=[hbm] * len(inputs),
            out_specs=[hbm if direct else vmem] * len(outputs),
            scratch_shapes=[pltpu.VMEM(shape, kind) for shape, kind in scratch.values()]
            + [pltpu.SemaphoreType.DMA(shape) for shape in semaphores.values()]
            + [inputs[name][1](inputs[name][0].shape, inputs[name][0].dtype) for name in small_inputs]
            + nears
            + arrived,
            compiler_params=pltpu.CompilerParams(
                collective_id=0, has_side_effects=True, vmem_limit_bytes=VMEM_LIMIT
            ),
        )(*[array for array, _ in inputs.values()])
        if direct:
            results = pl.pallas_call(
                copy_out,
                out_shape=[jax.ShapeDtypeStruct(shape, kind) for shape, kind in outputs.values()],
                in_specs=[hbm] * len(outputs),
                out_specs=[hbm] * len(outputs),
                scratch_shapes=nears + [pltpu.SemaphoreType.DMA((len(outputs),))] * 2,
            )(*results)
        r = SimpleNamespace(**dict(zip(outputs, results)))

        if not direct:
            rows_of = dict(scatter_dimension=0, tiled=True)
            r.w_out_grad = lax.psum_scatter(
                r.grads[:IN_UNIT].reshape(ff, half), "rows", **rows_of
            ).astype(FULL)
            others = r.grads[IN_UNIT:].transpose(1, 0, 2).reshape(model, -1)
            others = lax.psum_scatter(others, "rows", **rows_of).astype(FULL)
            r.w_in_grad = others[:, : ff // 2]
            r.w_attn_out_grad = others[:, ff // 2 : ff // 2 + half]
            r.w_query_key_grad = others[:, ff // 2 + half : ff // 2 + half + model]
            r.w_value_grad = others[:, ff // 2 + half + model :]
            r.w_proj_grad = lax.dynamic_slice_in_dim(
                r.w_proj_whole, lax.axis_index("rows") * own_rows, own_rows, 0
            )
        return (
            r.loss[0, 0],
            r.tokens_grad[None],
            r.gain_attn_grad,
            r.w_query_key_grad,
            r.w_value_grad,
            r.w_attn_out_grad,
            r.rel_bias_grad.T,
            r.gain_ff_grad,
            r.w_in_grad,
            r.w_out_grad,
            r.gain_final_grad,
            r.w_proj_grad,
        )

    return step


def solution(mesh):
    return jax.shard_map(
        on_device(mesh.shape["rows"]),
        mesh=mesh,
        in_specs=(P("tower", "rows", None), P("rows", None), P("rows")) + (P(),) * 12,
        out_specs=(
            P(),
            P("tower", "rows", None),
            P(),
            P("rows", "tower"),
            P("rows", "tower"),
            P("rows", "tower"),
            P(),
            P(),
            P("rows", "tower"),
            P("rows", "tower"),
            P(),
            P("rows", "tower"),
        ),
        check_vma=False,
    )
```

```python
import functools
import math
from types import SimpleNamespace

import jax
import jax.numpy as jnp
from jax import lax
from jax.experimental import pallas as pl
from jax.experimental.pallas import tpu as pltpu
from jax.sharding import PartitionSpec as P

EPSILON = 1e-06
LOGIT_SCALE = 50.0
MASKED = -1000000000.0
MESH = pl.DeviceIdType.MESH
LOW = jnp.bfloat16
FULL = jnp.float32
LANES = 128
TILE = 512
VMEM_LIMIT = 60 * 2**20

Z_HALF, Z_PAIR, Y, X = range(4)
ORDERS = (
    ((X,), (Y,), (Z_PAIR, Z_HALF)),
    ((Y,), (X,), (Z_PAIR,), (Z_HALF,)),
    ((Z_PAIR,), (Y,), (Z_HALF,), (X,)),
    ((Z_PAIR,), (Y,), (Z_HALF,), (X,)),
    ((X,), (Y,), (Z_PAIR, Z_HALF)),
    ((Y,), (X,), (Z_PAIR,), (Z_HALF,)),
    ((Z_PAIR,), (X,), (Y,), (Z_HALF,)),
    ((X,), (Z_PAIR,), (Y,), (Z_HALF,)),
    ((Z_PAIR,), (Y,), (X, Z_HALF)),
    ((X,), (Y,), (Z_PAIR,), (Z_HALF,)),
    ((X,), (Y,), (Z_PAIR,), (Z_HALF,)),
    ((Y,), (X,), (Z_PAIR,), (Z_HALF,)),
)
PLAN = (
    (),
    (),
    (),
    (),
    (),
    (),
    (),
    (),
    (),
    (),
    (),
    (),
    ((0, 0), (1, 0), (2, 0),),
    (),
    (),
    (),
    (),
    (),
    (),
    (),
    (),
    ((3, 0), (4, 0),),
    ((5, 0),),
    (),
    (),
    (),
    (),
    ((0, 1), (6, 0), (7, 0), (2, 1), (1, 1), (3, 1), (8, 0), (4, 1), (0, 2), (9, 0), (7, 1), (5, 1), (11, 0), (2, 2), (1, 2), (8, 1), (3, 2), (4, 2), (10, 0), (9, 1), (12, 0), (5, 2), (7, 2), (1, 3), (6, 1), (10, 1), (9, 2), (12, 1), (5, 3), (7, 3), (11, 1), (6, 2), (2, 3), (10, 2), (9, 3), (8, 2), (12, 2), (3, 3), (11, 2), (6, 3), (10, 3), (12, 3), (12, 4), (11, 3),),
)
BITS = 4
OUT_UNIT, IN_UNIT, ATTN_UNIT, QKV_UNIT, UNITS = 0, 4, 8, 9, 12
SMALL = UNITS


def dot(left, right):
    return jnp.dot(left, right, preferred_element_type=FULL)


def dot_nt(left, right):
    return lax.dot_general(left, right, (((1,), (1,)), ((), ())), preferred_element_type=FULL)


def dot_tn(left, right):
    return lax.dot_general(left, right, (((0,), (0,)), ((), ())), preferred_element_type=FULL)


def split(values):
    upper = values.astype(LOW)
    return upper, (values - upper.astype(FULL)).astype(LOW)


def inverse_root(values):
    return lax.rsqrt(jnp.mean(values * values, axis=-1, keepdims=True) + EPSILON)


def norm_backward(values, inverse, gain, upstream):
    scaled = upstream * gain
    gain_grad = jnp.sum(upstream * (values * inverse), axis=0, keepdims=True)
    inner = jnp.mean(scaled * values, axis=-1, keepdims=True)
    return inverse * scaled - values * (inverse * inverse * inverse * inner), gain_grad


def tiles(total, size):
    def over(body):
        def step(index, carry):
            body(index, pl.ds(pl.multiple_of(index * size, size), size))
            return carry

        lax.fori_loop(0, total // size, step, 0)

    return over


def in_kernel_sums(rows, model):
    return rows == 2**BITS and model % (16 * rows) == 0


def make_kernel(sizes, names, small_inputs):
    rows, width, model, ff, heads, buckets, per_row, count_in, count_out = sizes
    head_size = model // heads
    half = model // 2
    ff_half = ff // 2
    queries = rows * per_row
    parts = model // LANES
    query_message = parts * per_row
    row_bits = rows.bit_length() - 1
    direct = in_kernel_sums(rows, model)

    def kernel(*args):
        r = SimpleNamespace(**dict(zip(names, args)))
        extra = args[len(names) :]
        near_inputs, extra = extra[: len(small_inputs)], extra[len(small_inputs) :]
        far_inputs = [getattr(r, name) for name in small_inputs]
        r.__dict__.update(zip(small_inputs, near_inputs))
        far_results = args[count_in : count_in + count_out]
        near_results = extra[:count_out]
        leaving = []
        if direct:
            r.__dict__.update(zip(names[count_in : count_in + count_out], near_results))

        def publish(result):
            if direct:
                index = next(index for index, ref in enumerate(near_results) if ref is result)
                copy = pltpu.make_async_copy(result, far_results[index], r.leave_sem.at[index])
                copy.start()
                leaving.append(copy)

        parts_left = [4, 4, 1, 2, 1]

        def finished(group, result):
            parts_left[group] -= 1
            if not parts_left[group]:
                publish(result)

        landing = []
        if direct:
            landings = iter(extra[count_out:])
            landing = [[next(landings) for _ in steps] for steps in ORDERS]
        tower = lax.axis_index("tower")
        row = lax.axis_index("rows")
        partner = (1 - tower, row)
        is_query = tower == 0
        own_rows = model // rows

        barrier = pltpu.get_barrier_semaphore()
        pl.semaphore_signal(barrier, inc=1, device_id=partner, device_id_type=MESH)

        def greet(step, carry):
            peer = (tower, jnp.bitwise_xor(row, step))
            pl.semaphore_signal(barrier, inc=1, device_id=peer, device_id_type=MESH)
            return carry

        lax.fori_loop(1, rows, greet, 0)

        loads = [
            pltpu.make_async_copy(far, near, r.load_sem.at[index])
            for index, (far, near) in enumerate(
                (
                    (r.w_query_key, r.w_query_key_here),
                    (r.w_value, r.w_value_here),
                    (r.w_attn_out, r.w_attn_out_here),
                    (r.w_in, r.w_in_here),
                    (r.w_out, r.w_out_here),
                    (r.w_proj, r.w_proj_here),
                    *zip(far_inputs, near_inputs),
                )
            )
        ]

        def load(index):
            loads[index].start()

        def loaded(index):
            loads[index].wait()

        for index in range(6, len(loads)):
            load(index)
        for index in range(6):
            load(index)
        for index in range(6, len(loads)):
            loaded(index)

        def to_partner(src, dst, index):
            return pltpu.make_async_remote_copy(
                src_ref=src,
                dst_ref=dst,
                send_sem=r.core_send.at[index],
                recv_sem=r.core_recv.at[index],
                device_id=partner,
                device_id_type=MESH,
            )

        coordinate = [jnp.bitwise_and(lax.shift_right_logical(row, 3 - bit), 1) for bit in range(BITS)]

        def piece(unit, step, code):
            place = [slice(None)] * BITS
            for bits in ORDERS[unit][:step]:
                for bit in bits:
                    place[bit] = coordinate[bit]
            for spot, bit in enumerate(ORDERS[unit][step]):
                place[bit] = jnp.bitwise_xor(coordinate[bit], (code >> spot) & 1)
            return place

        def exchange(unit, step, code, half=None):
            place = piece(unit, step, code)
            into = landing[unit][step]
            if len(ORDERS[unit][step]) > 1:
                into = into.at[code - 1]
            elif half is not None:
                place[Z_PAIR] = jnp.bitwise_xor(coordinate[Z_PAIR], 1 - half)
                into = into.at[:, place[Z_PAIR]]
            peer = row
            for spot, bit in enumerate(ORDERS[unit][step]):
                peer = jnp.bitwise_xor(peer, ((code >> spot) & 1) << (3 - bit))
            return pltpu.make_async_remote_copy(
                src_ref=r.grads.at[(unit, *place)],
                dst_ref=into,
                send_sem=r.sum_send.at[unit],
                recv_sem=r.sum_recv.at[unit, step],
                device_id=(tower, peer),
                device_id_type=MESH,
            )

        def exchanges(unit, step):
            bits = ORDERS[unit][step]
            if step == 0 and unit < IN_UNIT and bits[0] in (X, Y) and len(bits) == 1:
                return [exchange(unit, step, 1, half) for half in range(2)]
            return [exchange(unit, step, code) for code in range(1, 2 ** len(bits))]

        def all_of(ref, send_sem, recv_sem):
            return pltpu.make_async_remote_copy(
                src_ref=ref,
                dst_ref=ref,
                send_sem=send_sem,
                recv_sem=recv_sem,
                device_id=partner,
                device_id_type=MESH,
            )

        def begin(unit):
            if direct:
                for copy in exchanges(unit, 0):
                    copy.start()

        def finish(unit, step):
            if unit == SMALL:
                small_finish(step)
                return
            all_of(landing[unit][step], r.sum_send.at[unit], r.sum_recv.at[unit, step]).wait_recv()
            kept = (unit, *piece(unit, step, 0))
            come = landing[unit][step]
            several = len(ORDERS[unit][step]) > 1
            if step + 1 < len(ORDERS[unit]):
                if several:
                    total = r.grads[kept].astype(FULL)
                    for other in range(3):
                        total = total + come[other].astype(FULL)
                    r.grads[kept] = total.astype(LOW)
                else:
                    r.grads[kept] = r.grads[kept] + come[...]
                for copy in exchanges(unit, step + 1):
                    copy.start()
                return
            total = r.grads[kept].astype(FULL)
            if several:
                for other in range(3):
                    total = total + come[other].astype(FULL)
            else:
                total = total + come[...].astype(FULL)
            if unit < IN_UNIT:
                spot = unit - OUT_UNIT
                r.w_out_grad[spot * own_rows : (spot + 1) * own_rows, :] = total
                finished(0, r.w_out_grad)
            elif unit < ATTN_UNIT:
                spot = unit - IN_UNIT
                r.w_in_grad[:, spot * half : (spot + 1) * half] = total
                finished(1, r.w_in_grad)
            elif unit < QKV_UNIT:
                r.w_attn_out_grad[...] = total
                finished(2, r.w_attn_out_grad)
            elif unit < UNITS - 1:
                spot = unit - QKV_UNIT
                r.w_query_key_grad[:, spot * half : (spot + 1) * half] = total
                finished(3, r.w_query_key_grad)
            else:
                r.w_value_grad[...] = total
                finished(4, r.w_value_grad)

        def small_exchange(step):
            peer = partner if step == row_bits else (tower, jnp.bitwise_xor(row, 1 << step))
            return pltpu.make_async_remote_copy(
                src_ref=r.small.at[step],
                dst_ref=r.small_in.at[step],
                send_sem=r.small_send.at[0],
                recv_sem=r.small_recv.at[step],
                device_id=peer,
                device_id_type=MESH,
            )

        def small_finish(step):
            small_exchange(step).wait_recv()
            r.small[step + 1] = r.small[step] + r.small_in[step]
            if step < row_bits:
                small_exchange(step + 1).start()

        def keep(unit, value):
            value = value.astype(LOW)
            r.grads[unit] = value.reshape(r.grads.shape[1:]) if direct else value

        lane = lax.broadcasted_iota(jnp.int32, (8, width), 1)
        doc_row = jnp.where(lane < r.doc_lengths[0], 0, 1)
        seg_row = jnp.where(is_query, jnp.broadcast_to(r.query_segments[...], (8, width)), doc_row)
        eye = (
            lax.broadcasted_iota(jnp.int32, (width, width), 0)
            == lax.broadcasted_iota(jnp.int32, (width, width), 1)
        ).astype(FULL)
        seg_column = dot_nt(eye.astype(LOW), seg_row.astype(FULL).astype(LOW))[:, 0:1].astype(jnp.int32)
        member = (seg_row == lax.broadcasted_iota(jnp.int32, (8, width), 0)).astype(FULL)
        share = 1.0 / jnp.maximum(jnp.sum(member, axis=-1, keepdims=True), 1.0)

        wide = 2 * width
        table = jnp.concatenate(
            [r.bucket_table[...], jnp.zeros((1, 1), jnp.int32)], axis=1
        )
        turned = (
            lax.broadcasted_iota(jnp.int32, (wide, wide), 0)
            + lax.broadcasted_iota(jnp.int32, (wide, wide), 1)
            == wide - 2
        ).astype(FULL).astype(LOW)
        table_low = jnp.broadcast_to(table.astype(FULL), (8, wide)).astype(LOW)
        table_turned = dot(table_low, turned)[0:1]
        hot = (
            table_turned.astype(jnp.int32) == lax.broadcasted_iota(jnp.int32, (buckets, wide), 0)
        ).astype(FULL)
        r.hot[...] = hot.astype(LOW)
        bias_upper, bias_lower = split(r.rel_bias[...])
        bias_last = (r.rel_bias[...] - bias_upper.astype(FULL) - bias_lower.astype(FULL)).astype(LOW)
        hot_low = hot.astype(LOW)
        r.table[0:heads, :] = dot(bias_upper, hot_low) + dot(bias_lower, hot_low) + dot(bias_last, hot_low)

        allowed = seg_column == seg_row[0:1]

        def spread_bias(head, carry):
            line = jnp.broadcast_to(r.table[pl.ds(head, 1), :], (width, wide))
            bias = pltpu.roll(line, width + 1, 1, stride=1, stride_axis=0)[:, :width]
            r.bias[head] = jnp.where(allowed, bias, MASKED)
            return carry

        lax.fori_loop(0, heads, spread_bias, 0)
        r.small[0] = jnp.zeros((8, model + 2 * LANES), FULL)
        r.diagonals[...] = jnp.zeros_like(r.diagonals)

        inputs = r.tokens[...].astype(FULL)
        normed = (inputs * inverse_root(inputs) * r.gain_attn[...][None]).astype(LOW)
        r.normed_one[0:width, :] = normed
        loaded(0)
        w_query_key = r.w_query_key_here

        for start in range(0, 2 * model, TILE):
            columns = slice(start, start + TILE)
            r.qkv[:, columns] = dot(normed, w_query_key[:, columns]).astype(LOW)

        loaded(1)
        w_value = r.w_value_here
        r.qkv[:, 2 * model :] = dot(normed, w_value[...]).astype(LOW)

        r.keys_turned[...] = r.qkv[:, model : 2 * model].T
        r.values_turned[...] = r.qkv[:, 2 * model :].T

        place = lax.broadcasted_iota(jnp.int32, (width, 2 * head_size), 1)

        def attend(pair):
            start = pair * 2 * head_size
            query = r.qkv[:, start : start + 2 * head_size]
            key = r.qkv[:, model + start : model + start + 2 * head_size]
            for side in range(2):
                head = 2 * pair + side
                own = (place >= head_size) if side else (place < head_size)
                score = dot_nt(jnp.where(own, key, jnp.zeros_like(key)), query) + r.bias[head]
                weights = jnp.exp(score - jnp.max(score, axis=0, keepdims=True))
                r.probs[head] = (weights * (1.0 / jnp.sum(weights, axis=0, keepdims=True))).astype(LOW)

        def mix(pair):
            for head in (2 * pair, 2 * pair + 1):
                here = slice(head * head_size, (head + 1) * head_size)
                r.mixed_turned[here, :] = dot(r.values_turned[here, :], r.probs[head]).astype(LOW)

        for pair in range(heads // 2):
            attend(pair)
            if pair:
                mix(pair - 1)
        mix(heads // 2 - 1)

        mixed = r.mixed_turned[...].T
        r.mixed[0:width, :] = mixed
        pl.semaphore_wait(barrier, rows)
        send_one = to_partner(r.normed_one.at[0:width], r.normed_one.at[width : 2 * width], 0)
        send_one.start()
        send_mixed = to_partner(r.mixed.at[0:width], r.mixed.at[width : 2 * width], 1)
        send_mixed.start()
        loaded(2)
        w_attn_out = r.w_attn_out_here
        hidden = r.tokens[...].astype(FULL) + dot(mixed, w_attn_out[...])
        r.hidden_one[...] = hidden
        normed_two = (hidden * inverse_root(hidden) * r.gain_ff[...][None]).astype(LOW)
        r.normed_two[0:width, :] = normed_two
        send_two = to_partner(r.normed_two.at[0:width], r.normed_two.at[width : 2 * width], 2)
        send_two.start()

        loaded(3)
        w_in = r.w_in_here
        bend = math.sqrt(2.0 / math.pi)

        for start in range(0, ff, TILE):
            columns = slice(start, start + TILE)
            inner = dot(normed_two, w_in[:, columns])
            curve = jnp.tanh(inner * (bend + (bend * 0.044715) * (inner * inner)))
            r.inner[:, columns] = inner
            r.active[0:width, columns] = (inner * (0.5 + 0.5 * curve)).astype(LOW)

        send_active = to_partner(r.active.at[0:width], r.active.at[width : 2 * width], 3)
        send_active.start()
        loaded(4)
        w_out = r.w_out_here

        hidden = r.hidden_one[...] + dot(r.active[0:width, :], w_out[...])
        r.hidden_two[...] = hidden
        inverse_final = inverse_root(hidden)
        normed_upper, normed_lower = split(hidden * inverse_final * r.gain_final[...][None])
        member_low = member.astype(LOW)
        pooled = (dot(member_low, normed_upper) + dot(member_low, normed_lower)) * share
        pooled = pooled.astype(LOW).astype(FULL)

        own_queries = r.pooled_queries.at[pl.ds(pl.multiple_of(row * query_message, 8), query_message)]
        own_doc = r.pooled_docs.at[pl.ds(pl.multiple_of(row * 8, 8), 8)]

        def spread(block, whole):
            for index in range(1, rows):
                pltpu.make_async_remote_copy(
                    src_ref=block,
                    dst_ref=block,
                    send_sem=r.spread_sem.at[0],
                    recv_sem=r.spread_sem.at[1],
                    device_id=(tower, jnp.bitwise_xor(row, rows - index)),
                    device_id_type=MESH,
                ).start()
            others = whole.at[0 : whole.shape[0] // rows * (rows - 1)]
            every = all_of(others, r.spread_sem.at[0], r.spread_sem.at[1])
            every.wait_send()
            every.wait_recv()

        relay_queries = to_partner(r.pooled_queries, r.pooled_queries, 4)
        relay_docs = to_partner(r.pooled_docs, r.pooled_docs, 5)

        @pl.when(is_query)
        def _():
            for part in range(parts):
                spot = pl.multiple_of(row * query_message, 8) + part * per_row
                r.pooled_queries[pl.ds(spot, per_row), :] = pooled[
                    0:per_row, part * LANES : (part + 1) * LANES
                ]
            spread(own_queries, r.pooled_queries)
            relay_queries.start()
            relay_docs.wait_recv()
            relay_queries.wait_send()

        @pl.when(jnp.logical_not(is_query))
        def _():
            own_doc[...] = jnp.zeros((8, LANES), FULL)
            for part in range(parts):
                spot = pl.multiple_of(row * 8, 8) + part
                r.pooled_docs[pl.ds(spot, 1), :] = pooled[0:1, part * LANES : (part + 1) * LANES]
            spread(own_doc, r.pooled_docs)
            relay_docs.start()
            relay_queries.wait_recv()
            relay_docs.wait_send()

        for part in range(parts):
            lanes = slice(part * LANES, (part + 1) * LANES)
            for query in range(per_row):
                r.pooled[query * rows : (query + 1) * rows, lanes] = r.pooled_queries[
                    pl.ds(part * per_row + query, rows, stride=query_message), :
                ]
            r.pooled[queries:, lanes] = r.pooled_docs[pl.ds(part, rows, stride=8), :]

        loaded(5)
        w_proj = r.w_proj_here
        pooled_low = r.pooled[...].astype(LOW)
        projected = dot(pooled_low, w_proj[...])
        scale = lax.rsqrt(jnp.sum(projected * projected, axis=-1, keepdims=True) + EPSILON)
        embed = (projected * scale).astype(LOW)
        query_embed, doc_embed = embed[:queries], embed[queries:]
        logits = LOGIT_SCALE * dot_nt(query_embed, doc_embed)
        target = jnp.concatenate(
            [
                (
                    jnp.broadcast_to(r.positives[query : query + 1, :].astype(FULL), (rows, rows)).T
                    == lax.broadcasted_iota(jnp.int32, (rows, rows), 1).astype(FULL)
                ).astype(FULL)
                for query in range(per_row)
            ],
            axis=0,
        )
        highest = jnp.max(logits, axis=-1, keepdims=True)
        log_sum = highest + jnp.log(jnp.sum(jnp.exp(logits - highest), axis=-1, keepdims=True))
        missed = log_sum - jnp.sum(logits * target, axis=-1, keepdims=True)
        r.loss[...] = jnp.sum(missed, axis=0, keepdims=True) / queries
        publish(r.loss)
        logits_grad = (jnp.exp(logits - log_sum) - target) * (LOGIT_SCALE / queries)
        grad_upper, grad_lower = split(logits_grad)
        embed_grad = jnp.concatenate(
            [
                dot(grad_upper, doc_embed) + dot(grad_lower, doc_embed),
                dot_tn(grad_upper, query_embed) + dot_tn(grad_lower, query_embed),
            ],
            axis=0,
        )
        along = jnp.sum(embed_grad * projected, axis=-1, keepdims=True)
        proj_grad = (scale * embed_grad - projected * (scale * scale * scale * along)).astype(LOW)
        r.proj_grad[...] = proj_grad.astype(FULL)
        r.own_grad[...] = jnp.zeros_like(r.own_grad)

        @pl.when(is_query)
        def _():
            for query in range(per_row):
                r.own_grad[query : query + 1, :] = r.proj_grad[pl.ds(query * rows + row, 1), :]

        @pl.when(jnp.logical_not(is_query))
        def _():
            r.own_grad[0:1, :] = r.proj_grad[pl.ds(queries + row, 1), :]

        pooled_grad = dot_nt(r.own_grad[...].astype(LOW), w_proj[...])[0:8] * share
        final_grad = jnp.zeros((width, model), FULL)
        for query in range(per_row):
            final_grad = jnp.where(seg_column == query, pooled_grad[query : query + 1, :], final_grad)

        hidden = r.hidden_two[...]
        hidden_grad, r.small[0, 2:3, 0:model] = norm_backward(
            hidden, inverse_final, r.gain_final[...][None], final_grad
        )
        r.hidden_grad[...] = hidden_grad
        r.branch[...] = hidden_grad.astype(LOW)
        own_half = pl.ds(pl.multiple_of(tower * half, LANES), half)
        other_half = pl.ds(pl.multiple_of((1 - tower) * half, LANES), half)
        send_branch = to_partner(r.branch.at[:, other_half], r.branch_half.at[width : 2 * width], 6)
        send_branch.start()
        r.branch_half[0:width, :] = r.branch[:, own_half]

        per_tile = model * rows // ff
        if direct:
            for half_step in range(2):
                pair = jnp.bitwise_xor(coordinate[Z_PAIR], 1 - half_step)
                spans = [pl.ds(pl.multiple_of((2 * half_z + pair) * model, model), model) for half_z in range(2)]
                if half_step == 0:
                    own_parts = [
                        dot_tn(r.active[0:width, span], r.branch_half[0:width, :]) for span in spans
                    ]
                    send_active.wait()
                    send_branch.wait()

                def tile(half_z):
                    if half_step == 0:
                        value = own_parts[half_z] + dot_tn(
                            r.active[width : 2 * width, spans[half_z]], r.branch_half[width : 2 * width, :]
                        )
                    else:
                        value = dot_tn(r.active[:, spans[half_z]], r.branch_half[...])
                    for unit in range(per_tile):
                        for spot in range(per_tile):
                            start = (spot * per_tile + unit) * own_rows
                            r.grads[unit, half_z, pair, spot // 2, spot % 2] = value[
                                start : start + own_rows, :
                            ].astype(LOW)

                for half_z in range(2):
                    tile(half_z)
                for unit in range(OUT_UNIT, IN_UNIT):
                    sends = exchanges(unit, 0)
                    if len(sends) == 2:
                        sends[half_step].start()
                    elif half_step == (Z_PAIR not in ORDERS[unit][0]):
                        for copy in sends:
                            copy.start()
        else:
            send_active.wait()
            send_branch.wait()

            @tiles(ff, model)
            def _(index, columns):
                keep(index, dot_tn(r.active[:, columns], r.branch_half[...]))

        pieces = []

        def then(body):
            pieces.append(body)
            return body

        def inner_back(index):
            columns = pl.ds(index * TILE, TILE)
            active_grad = dot_nt(r.branch[...], w_out[columns, :])
            inner = r.inner[:, columns]
            square = inner * inner
            curve = jnp.tanh(inner * (bend + (bend * 0.044715) * square))
            slope = (0.5 * inner) * (1.0 - curve * curve) * (bend + (bend * 3 * 0.044715) * square)
            r.inner_grad[:, columns] = (active_grad * ((0.5 + 0.5 * curve) + slope)).astype(LOW)

        for index in range(ff // TILE):
            then(functools.partial(inner_back, index))

        own_ff = pl.ds(pl.multiple_of(tower * ff_half, LANES), ff_half)
        other_ff = pl.ds(pl.multiple_of((1 - tower) * ff_half, LANES), ff_half)
        send_inner = to_partner(r.inner_grad.at[:, other_ff], r.inner_half.at[width : 2 * width], 7)
        send_attn = to_partner(r.attn.at[:, other_half], r.attn_half.at[width : 2 * width], 8)

        @then
        def _():
            send_inner.start()
            r.inner_half[0:width, :] = r.inner_grad[:, own_ff]
            r.normed_grad[...] = dot_nt(r.inner_grad[...], w_in[...])

        @then
        def _():
            hidden = r.hidden_one[...]
            through, r.small[0, 1:2, 0:model] = norm_backward(
                hidden, inverse_root(hidden), r.gain_ff[...][None], r.normed_grad[...]
            )
            hidden_grad = r.hidden_grad[...] + through
            r.hidden_grad[...] = hidden_grad
            r.attn[...] = hidden_grad.astype(LOW)
            send_attn.start()
            r.attn_half[0:width, :] = r.attn[:, own_half]
            send_two.wait()
            send_inner.wait()

        def in_grad(index):
            columns = pl.ds(index * half, half)
            keep(IN_UNIT + index, dot_tn(r.normed_two[...], r.inner_half[:, columns]))
            begin(IN_UNIT + index)

        for index in range(ATTN_UNIT - IN_UNIT):
            then(functools.partial(in_grad, index))

        @then
        def _():
            r.mixed_grad[...] = dot_nt(r.attn[...], w_attn_out[...]).astype(LOW)

        @then
        def _():
            send_mixed.wait()
            send_attn.wait()
            keep(ATTN_UNIT, dot_tn(r.mixed[...], r.attn_half[...]))
            begin(ATTN_UNIT)

        def attention_back(pair):
            columns = pl.ds(pl.multiple_of(pair * 2 * head_size, LANES), 2 * head_size)
            query = r.qkv[:, columns]
            value = r.qkv[:, pl.ds(pl.multiple_of(2 * model + pair * 2 * head_size, LANES), 2 * head_size)]
            mixed_grad = r.mixed_grad[:, columns]
            place = lax.broadcasted_iota(jnp.int32, (width, 2 * head_size), 1)
            key_sides, value_sides = [], []
            for side in range(2):
                head = 2 * pair + side
                own = (place >= head_size) if side else (place < head_size)
                prob_low = r.probs[head]
                prob = prob_low.astype(FULL)
                prob_grad = dot_nt(jnp.where(own, value, jnp.zeros_like(value)), mixed_grad)
                weighted = prob * prob_grad
                score_grad = weighted - prob * jnp.sum(weighted, axis=0, keepdims=True)
                score_low = score_grad.astype(LOW)
                key_sides.append(dot(score_low, query))
                value_sides.append(dot(prob_low, mixed_grad))
                here = pl.ds(pl.multiple_of(head * head_size, head_size), head_size)
                r.queries_turned[here, :] = dot(r.keys_turned[here, :], score_low).astype(LOW)
                r.score_grad[...] = score_grad
                total = jnp.zeros((8, wide), FULL)
                blank = jnp.zeros((8, wide - width), FULL)
                for block in range(width // 8):
                    line = jnp.concatenate([r.score_grad[8 * block : 8 * block + 8, :], blank], axis=1)
                    total = total + pltpu.roll(line, (wide + width - 1 - 8 * block) % wide, 1)
                for line in range(8):
                    r.diagonals[line, pl.ds(head, 1), :] = total[line : line + 1, :]
            after = place >= head_size
            r.qkv_grad[:, pl.ds(pl.multiple_of(model + pair * 2 * head_size, LANES), 2 * head_size)] = (
                jnp.where(after, key_sides[1], key_sides[0]).astype(LOW)
            )
            r.qkv_grad[:, pl.ds(pl.multiple_of(2 * model + pair * 2 * head_size, LANES), 2 * head_size)] = (
                jnp.where(after, value_sides[1], value_sides[0]).astype(LOW)
            )

        for pair in range(heads // 2):
            then(functools.partial(attention_back, pair))

        own_whole = pl.ds(pl.multiple_of(tower * model, LANES), model)
        other_whole = pl.ds(pl.multiple_of((1 - tower) * model, LANES), model)
        own_value = pl.ds(pl.multiple_of(2 * model + tower * half, LANES), half)
        other_value = pl.ds(pl.multiple_of(2 * model + (1 - tower) * half, LANES), half)
        send_qk = to_partner(
            r.qkv_grad.at[:, other_whole], r.qkv_half.at[width : 2 * width, 0:model], 9
        )
        send_value = to_partner(
            r.qkv_grad.at[:, other_value], r.qkv_half.at[width : 2 * width, model:], 10
        )

        @then
        def _():
            r.qkv_grad[:, 0:model] = r.queries_turned[...].T
            send_qk.start()
            send_value.start()
            r.qkv_half[0:width, 0:model] = r.qkv_grad[:, own_whole]
            r.qkv_half[0:width, model:] = r.qkv_grad[:, own_value]
            send_one.wait()
            send_qk.wait()
            send_value.wait()

        def qkv_back(index):
            columns = pl.ds(index * half, half)
            keep(QKV_UNIT + index, dot_tn(r.normed_one[...], r.qkv_half[:, columns]))
            begin(QKV_UNIT + index)

        for index in range(UNITS - QKV_UNIT):
            then(functools.partial(qkv_back, index))

        @then
        def _():
            normed_grad = dot_nt(r.qkv_grad[:, 0 : 2 * model], w_query_key[...])
            r.normed_grad[...] = normed_grad + dot_nt(r.qkv_grad[:, 2 * model :], w_value[...])

        @then
        def _():
            inputs = r.tokens[...].astype(FULL)
            through, r.small[0, 0:1, 0:model] = norm_backward(
                inputs, inverse_root(inputs), r.gain_attn[...][None], r.normed_grad[...]
            )
            r.tokens_grad[...] = r.hidden_grad[...] + through
            publish(r.tokens_grad)

            offsets = jnp.zeros((16, wide), FULL)
            for line in range(8):
                row_lines = r.diagonals[line]
                offsets = offsets + (pltpu.roll(row_lines, wide - line, 1) if line else row_lines)
            offset_upper, offset_lower = split(offsets)
            hot_low = r.hot[...]
            sums = dot_nt(offset_upper, hot_low) + dot_nt(offset_lower, hot_low)
            r.small[0, 0:8, model : model + buckets] = sums[0:8]
            r.small[0, 0:8, model + LANES : model + LANES + buckets] = sums[8:16]
            small_exchange(0).start()

        @then
        def _():
            r.proj_grad_half[...] = r.proj_grad[:, own_half].astype(LOW)
            r.w_proj_whole[...] = dot_tn(r.pooled[...].astype(LOW), r.proj_grad_half[...])
            if direct:
                r.w_proj_grad[...] = r.w_proj_whole[pl.ds(pl.multiple_of(row * own_rows, 8), own_rows), :]
                publish(r.w_proj_grad)

        for index in range(len(pieces) + 1):
            if index:
                pieces[index - 1]()
            if direct:
                for event in PLAN[index]:
                    finish(*event)

        if not direct:
            for step in range(row_bits + 1):
                small_finish(step)
        total = row_bits + 1
        r.gain_attn_grad[...] = r.small[total, 0, 0:model]
        r.gain_ff_grad[...] = r.small[total, 1, 0:model]
        r.gain_final_grad[...] = r.small[total, 2, 0:model]
        r.rel_bias_grad[0:8, :] = r.small[total, 0:8, model : model + buckets]
        r.rel_bias_grad[8:heads, :] = r.small[total, 0 : heads - 8, model + LANES : model + LANES + buckets]
        for result in (r.gain_attn_grad, r.gain_ff_grad, r.gain_final_grad, r.rel_bias_grad):
            publish(result)
        if direct:
            sent = r.w_proj_whole.at[0 : (rows - 1) * own_rows // 2]
            for unit in range(UNITS):
                all_of(sent, r.sum_send.at[unit], r.sum_recv.at[unit, 0]).wait_send()
        all_of(r.small_in, r.small_send.at[0], r.small_recv.at[0]).wait_send()
        for copy in leaving:
            copy.wait()

    return kernel


def copy_out(*args):
    count = (len(args) - 2) // 3
    here = args[2 * count : 3 * count]
    ways = [
        (
            pltpu.make_async_copy(args[index], here[index], args[-2].at[index]),
            pltpu.make_async_copy(here[index], args[count + index], args[-1].at[index]),
        )
        for index in range(count)
    ]
    for come, _ in ways:
        come.start()
    for come, leave in ways:
        come.wait()
        leave.start()
    for _, leave in ways:
        leave.wait()


def on_device(rows):
    def step(
        tokens,
        query_segments,
        doc_lengths,
        bucket_table,
        positives,
        gain_attn,
        w_query_key,
        w_value,
        w_attn_out,
        rel_bias,
        gain_ff,
        w_in,
        w_out,
        gain_final,
        w_proj,
    ):
        width, model = tokens.shape[1:]
        ff = w_in.shape[1]
        buckets, heads = rel_bias.shape
        per_row = positives.shape[1]
        half = model // 2
        wide = 2 * width
        queries = rows * per_row
        row_bits = rows.bit_length() - 1
        own_rows = model // rows
        vmem = pl.BlockSpec(memory_space=pltpu.VMEM)
        hbm = pl.BlockSpec(memory_space=pl.ANY)
        direct = in_kernel_sums(rows, model)
        inputs = dict(
            tokens=(tokens[0], pltpu.VMEM),
            query_segments=(query_segments, pltpu.VMEM),
            doc_lengths=(doc_lengths, pltpu.SMEM),
            bucket_table=(bucket_table[None], pltpu.VMEM),
            positives=(positives.T, pltpu.VMEM),
            gain_attn=(gain_attn, pltpu.VMEM),
            w_query_key=(w_query_key, None),
            w_value=(w_value, None),
            w_attn_out=(w_attn_out, None),
            rel_bias=(rel_bias.T, pltpu.VMEM),
            gain_ff=(gain_ff, pltpu.VMEM),
            w_in=(w_in, None),
            w_out=(w_out, None),
            gain_final=(gain_final, pltpu.VMEM),
            w_proj=(w_proj, None),
        )
        outputs = dict(
            loss=((1, 1), FULL),
            tokens_grad=((width, model), FULL),
            gain_attn_grad=((model,), FULL),
            gain_ff_grad=((model,), FULL),
            gain_final_grad=((model,), FULL),
            rel_bias_grad=((heads, buckets), FULL),
        )
        whole = ((model, half), FULL)
        if direct:
            outputs.update(
                w_query_key_grad=((own_rows, model), FULL),
                w_value_grad=((own_rows, half), FULL),
                w_attn_out_grad=((own_rows, half), FULL),
                w_in_grad=((own_rows, ff // 2), FULL),
                w_out_grad=((ff // rows, half), FULL),
                w_proj_grad=((own_rows, half), FULL),
            )
            held = dict(
                w_proj_whole=whole, grads=((UNITS,) + (2,) * row_bits + (own_rows, half), LOW)
            )
            arrived = []
            for steps in ORDERS:
                left = BITS
                for bits in steps:
                    left -= len(bits)
                    several = (3,) if len(bits) > 1 else ()
                    arrived.append(pltpu.VMEM(several + (2,) * left + (own_rows, half), LOW))
        else:
            outputs.update(w_proj_whole=whole, grads=((UNITS, model, half), LOW))
            held = {}
            arrived = []
        scratch = dict(
            w_query_key_here=(w_query_key.shape, LOW),
            w_value_here=(w_value.shape, LOW),
            w_attn_out_here=(w_attn_out.shape, LOW),
            w_in_here=(w_in.shape, LOW),
            w_out_here=(w_out.shape, LOW),
            w_proj_here=(w_proj.shape, LOW),
            hot=((buckets, wide), LOW),
            table=((16, wide), FULL),
            bias=((heads, width, width), FULL),
            normed_one=((2 * width, model), LOW),
            qkv=((width, 3 * model), LOW),
            keys_turned=((model, width), LOW),
            values_turned=((model, width), LOW),
            probs=((heads, width, width), LOW),
            mixed_turned=((model, width), LOW),
            mixed=((2 * width, model), LOW),
            hidden_one=((width, model), FULL),
            normed_two=((2 * width, model), LOW),
            active=((2 * width, ff), LOW),
            inner=((width, ff), FULL),
            hidden_two=((width, model), FULL),
            pooled_queries=((rows * per_row * model // LANES, LANES), FULL),
            pooled_docs=((rows * 8, LANES), FULL),
            pooled=((queries + rows, model), FULL),
            proj_grad=((queries + rows, model), FULL),
            proj_grad_half=((queries + rows, half), LOW),
            own_grad=((16, model), FULL),
            hidden_grad=((width, model), FULL),
            branch=((width, model), LOW),
            branch_half=((2 * width, half), LOW),
            inner_grad=((width, ff), LOW),
            inner_half=((2 * width, ff // 2), LOW),
            normed_grad=((width, model), FULL),
            attn=((width, model), LOW),
            attn_half=((2 * width, half), LOW),
            mixed_grad=((width, model), LOW),
            score_grad=((width, width), FULL),
            diagonals=((8, 16, wide), FULL),
            queries_turned=((model, width), LOW),
            qkv_grad=((width, 3 * model), LOW),
            qkv_half=((2 * width, model + half), LOW),
            small=((row_bits + 2, 8, model + 2 * LANES), FULL),
            small_in=((row_bits + 1, 8, model + 2 * LANES), FULL),
        )
        scratch.update(held)
        semaphores = dict(
            load_sem=((len(inputs),)),
            core_send=((11,)),
            core_recv=((11,)),
            spread_sem=((2,)),
            small_send=((1,)),
            small_recv=((row_bits + 1,)),
            sum_send=((UNITS,)),
            leave_sem=(len(outputs),),
            sum_recv=((UNITS, BITS)),
        )
        names = [*inputs, *outputs, *scratch, *semaphores]
        small_inputs = [name for name, (_, place) in inputs.items() if place is not None]
        nears = [pltpu.VMEM(shape, kind) for shape, kind in outputs.values()] if direct else []
        sizes = (rows, width, model, ff, heads, buckets, per_row, len(inputs), len(outputs))
        results = pl.pallas_call(
            make_kernel(sizes, names, small_inputs),
            out_shape=[jax.ShapeDtypeStruct(shape, kind) for shape, kind in outputs.values()],
            in_specs=[hbm] * len(inputs),
            out_specs=[hbm if direct else vmem] * len(outputs),
            scratch_shapes=[pltpu.VMEM(shape, kind) for shape, kind in scratch.values()]
            + [pltpu.SemaphoreType.DMA(shape) for shape in semaphores.values()]
            + [inputs[name][1](inputs[name][0].shape, inputs[name][0].dtype) for name in small_inputs]
            + nears
            + arrived,
            compiler_params=pltpu.CompilerParams(
                collective_id=0, has_side_effects=True, vmem_limit_bytes=VMEM_LIMIT
            ),
        )(*[array for array, _ in inputs.values()])
        if direct:
            results = pl.pallas_call(
                copy_out,
                out_shape=[jax.ShapeDtypeStruct(shape, kind) for shape, kind in outputs.values()],
                in_specs=[hbm] * len(outputs),
                out_specs=[hbm] * len(outputs),
                scratch_shapes=nears + [pltpu.SemaphoreType.DMA((len(outputs),))] * 2,
            )(*results)
        r = SimpleNamespace(**dict(zip(outputs, results)))

        if not direct:
            rows_of = dict(scatter_dimension=0, tiled=True)
            r.w_out_grad = lax.psum_scatter(
                r.grads[:IN_UNIT].reshape(ff, half), "rows", **rows_of
            ).astype(FULL)
            others = r.grads[IN_UNIT:].transpose(1, 0, 2).reshape(model, -1)
            others = lax.psum_scatter(others, "rows", **rows_of).astype(FULL)
            r.w_in_grad = others[:, : ff // 2]
            r.w_attn_out_grad = others[:, ff // 2 : ff // 2 + half]
            r.w_query_key_grad = others[:, ff // 2 + half : ff // 2 + half + model]
            r.w_value_grad = others[:, ff // 2 + half + model :]
            r.w_proj_grad = lax.dynamic_slice_in_dim(
                r.w_proj_whole, lax.axis_index("rows") * own_rows, own_rows, 0
            )
        return (
            r.loss[0, 0],
            r.tokens_grad[None],
            r.gain_attn_grad,
            r.w_query_key_grad,
            r.w_value_grad,
            r.w_attn_out_grad,
            r.rel_bias_grad.T,
            r.gain_ff_grad,
            r.w_in_grad,
            r.w_out_grad,
            r.gain_final_grad,
            r.w_proj_grad,
        )

    return step


def solution(mesh):
    return jax.shard_map(
        on_device(mesh.shape["rows"]),
        mesh=mesh,
        in_specs=(P("tower", "rows", None), P("rows", None), P("rows")) + (P(),) * 12,
        out_specs=(
            P(),
            P("tower", "rows", None),
            P(),
            P("rows", "tower"),
            P("rows", "tower"),
            P("rows", "tower"),
            P(),
            P(),
            P("rows", "tower"),
            P("rows", "tower"),
            P(),
            P("rows", "tower"),
        ),
        check_vma=False,
    )
```

```python
import functools
import math
from types import SimpleNamespace

import jax
import jax.numpy as jnp
from jax import lax
from jax.experimental import pallas as pl
from jax.experimental.pallas import tpu as pltpu
from jax.sharding import PartitionSpec as P

EPSILON = 1e-06
LOGIT_SCALE = 50.0
MASKED = -1000000000.0
MESH = pl.DeviceIdType.MESH
LOW = jnp.bfloat16
FULL = jnp.float32
LANES = 128
TILE = 512
VMEM_LIMIT = 60 * 2**20
WIDER_VMEM_LIMIT = 62 * 2**20

Z_HALF, Z_PAIR, Y, X = range(4)
ORDERS = (
    ((X,), (Y,), (Z_PAIR, Z_HALF)),
    ((X,), (Y,), (Z_PAIR, Z_HALF)),
    ((Z_PAIR,), (Y,), (X,), (Z_HALF,)),
    ((Y,), (X,), (Z_PAIR,), (Z_HALF,)),
    ((Y,), (X,), (Z_PAIR,), (Z_HALF,)),
    ((Z_PAIR,), (X,), (Z_HALF,), (Y,)),
    ((X,), (Y,), (Z_PAIR,), (Z_HALF,)),
    ((Z_PAIR,), (X,), (Y,), (Z_HALF,)),
    ((Z_PAIR,), (X,), (Y,), (Z_HALF,)),
    ((X,), (Y,), (Z_PAIR,), (Z_HALF,)),
    ((Y,), (Z_PAIR,), (X, Z_HALF)),
    ((Y,), (X,), (Z_PAIR,), (Z_HALF,)),
)
PLAN = (
    (),
    (),
    (),
    (),
    (),
    (),
    (),
    (),
    (),
    (),
    (),
    ((2, 0), (3, 0),),
    (),
    (),
    (),
    (),
    ((0, 0),),
    (),
    (),
    (),
    (),
    ((1, 0), (4, 0), (5, 0),),
    (),
    (),
    (),
    ((2, 1),),
    (),
    ((6, 0), (0, 1), (7, 0), (3, 1), (1, 1), (4, 1), (8, 0), (5, 1), (0, 2), (10, 0), (3, 2), (1, 2), (9, 0), (4, 2), (11, 0), (2, 2), (12, 0), (5, 2), (6, 1), (10, 1), (7, 1), (3, 3), (4, 3), (9, 1), (2, 3), (12, 1), (8, 1), (5, 3), (6, 2), (7, 2), (11, 1), (8, 2), (9, 2), (12, 2), (10, 2), (6, 3), (7, 3), (11, 2), (8, 3), (9, 3), (12, 3), (12, 4), (11, 3),),
)
BITS = 4
OUT_UNIT, IN_UNIT, ATTN_UNIT, QKV_UNIT, UNITS = 0, 4, 8, 9, 12
SMALL = UNITS


def dot(left, right):
    return jnp.dot(left, right, preferred_element_type=FULL)


def dot_nt(left, right):
    return lax.dot_general(left, right, (((1,), (1,)), ((), ())), preferred_element_type=FULL)


def dot_tn(left, right):
    return lax.dot_general(left, right, (((0,), (0,)), ((), ())), preferred_element_type=FULL)


def split(values):
    upper = values.astype(LOW)
    return upper, (values - upper.astype(FULL)).astype(LOW)


def inverse_root(values):
    return lax.rsqrt(jnp.mean(values * values, axis=-1, keepdims=True) + EPSILON)


def norm_backward(values, inverse, gain, upstream):
    scaled = upstream * gain
    gain_grad = jnp.sum(upstream * (values * inverse), axis=0, keepdims=True)
    inner = jnp.mean(scaled * values, axis=-1, keepdims=True)
    return inverse * scaled - values * (inverse * inverse * inverse * inner), gain_grad


def tiles(total, size):
    def over(body):
        def step(index, carry):
            body(index, pl.ds(pl.multiple_of(index * size, size), size))
            return carry

        lax.fori_loop(0, total // size, step, 0)

    return over


def in_kernel_sums(rows, model):
    return rows == 2**BITS and model % (16 * rows) == 0


def make_kernel(sizes, names, small_inputs):
    rows, width, model, ff, heads, buckets, per_row, count_in, count_out = sizes
    head_size = model // heads
    half = model // 2
    ff_half = ff // 2
    assert heads * buckets <= half
    queries = rows * per_row
    parts = model // LANES
    query_message = -(-parts * per_row // 16) * 16
    doc_message = 16
    row_bits = rows.bit_length() - 1
    direct = in_kernel_sums(rows, model)

    def kernel(*args):
        r = SimpleNamespace(**dict(zip(names, args)))
        extra = args[len(names) :]
        near_inputs, extra = extra[: len(small_inputs)], extra[len(small_inputs) :]
        far_inputs = [getattr(r, name) for name in small_inputs]
        r.__dict__.update(zip(small_inputs, near_inputs))
        far_results = args[count_in : count_in + count_out]
        near_results = extra[:count_out]
        leaving = []
        if direct:
            r.__dict__.update(zip(names[count_in : count_in + count_out], near_results))

        def publish(result):
            if direct:
                index = next(index for index, ref in enumerate(near_results) if ref is result)
                copy = pltpu.make_async_copy(result, far_results[index], r.leave_sem.at[index])
                copy.start()
                leaving.append(copy)

        parts_left = [4, 4, 1, 2, 1]

        def finished(group, result):
            parts_left[group] -= 1
            if not parts_left[group]:
                publish(result)

        landing = []
        if direct:
            landings = iter(extra[count_out:])
            landing = [[next(landings) for _ in steps] for steps in ORDERS]
        tower = lax.axis_index("tower")
        row = lax.axis_index("rows")
        partner = (1 - tower, row)
        is_query = tower == 0
        own_rows = model // rows

        barrier = pltpu.get_barrier_semaphore()
        pl.semaphore_signal(barrier, inc=1, device_id=partner, device_id_type=MESH)

        def greet(step, carry):
            peer = (tower, jnp.bitwise_xor(row, step))
            pl.semaphore_signal(barrier, inc=1, device_id=peer, device_id_type=MESH)
            return carry

        lax.fori_loop(1, rows, greet, 0)

        loads = [
            pltpu.make_async_copy(far, near, r.load_sem.at[index])
            for index, (far, near) in enumerate(
                (
                    (r.w_query_key, r.w_query_key_here),
                    (r.w_value, r.w_value_here),
                    (r.w_attn_out, r.w_attn_out_here),
                    (r.w_in, r.w_in_here),
                    (r.w_out, r.w_out_here),
                    (r.w_proj, r.w_proj_here),
                    *zip(far_inputs, near_inputs),
                )
            )
        ]

        def load(index):
            loads[index].start()

        def loaded(index):
            loads[index].wait()

        for index in range(6, len(loads)):
            load(index)
        for index in range(6):
            load(index)
        for index in range(6, len(loads)):
            loaded(index)

        def to_partner(src, dst, index):
            return pltpu.make_async_remote_copy(
                src_ref=src,
                dst_ref=dst,
                send_sem=r.core_send.at[index],
                recv_sem=r.core_recv.at[index],
                device_id=partner,
                device_id_type=MESH,
            )

        coordinate = [jnp.bitwise_and(lax.shift_right_logical(row, 3 - bit), 1) for bit in range(BITS)]

        def piece(unit, step, code):
            place = [slice(None)] * BITS
            for bits in ORDERS[unit][:step]:
                for bit in bits:
                    place[bit] = coordinate[bit]
            for spot, bit in enumerate(ORDERS[unit][step]):
                place[bit] = jnp.bitwise_xor(coordinate[bit], (code >> spot) & 1)
            return place

        def exchange(unit, step, code, half=None):
            place = piece(unit, step, code)
            into = landing[unit][step]
            if len(ORDERS[unit][step]) > 1:
                into = into.at[code - 1]
            elif half is not None:
                place[Z_PAIR] = jnp.bitwise_xor(coordinate[Z_PAIR], 1 - half)
                into = into.at[:, place[Z_PAIR]]
            peer = row
            for spot, bit in enumerate(ORDERS[unit][step]):
                peer = jnp.bitwise_xor(peer, ((code >> spot) & 1) << (3 - bit))
            return pltpu.make_async_remote_copy(
                src_ref=r.grads.at[(unit, *place)],
                dst_ref=into,
                send_sem=r.sum_send.at[unit],
                recv_sem=r.sum_recv.at[unit, step],
                device_id=(tower, peer),
                device_id_type=MESH,
            )

        def exchanges(unit, step):
            bits = ORDERS[unit][step]
            if step == 0 and unit < IN_UNIT and bits[0] in (X, Y) and len(bits) == 1:
                return [exchange(unit, step, 1, half) for half in range(2)]
            return [exchange(unit, step, code) for code in range(1, 2 ** len(bits))]

        def all_of(ref, send_sem, recv_sem):
            return pltpu.make_async_remote_copy(
                src_ref=ref,
                dst_ref=ref,
                send_sem=send_sem,
                recv_sem=recv_sem,
                device_id=partner,
                device_id_type=MESH,
            )

        def begin(unit):
            if direct:
                for copy in exchanges(unit, 0):
                    copy.start()

        def finish(unit, step):
            if unit == SMALL:
                small_finish(step)
                return
            all_of(landing[unit][step], r.sum_send.at[unit], r.sum_recv.at[unit, step]).wait_recv()
            kept = (unit, *piece(unit, step, 0))
            come = landing[unit][step]
            several = len(ORDERS[unit][step]) > 1
            if step + 1 < len(ORDERS[unit]):
                if several:
                    total = r.grads[kept].astype(FULL)
                    for other in range(3):
                        total = total + come[other].astype(FULL)
                    r.grads[kept] = total.astype(LOW)
                else:
                    r.grads[kept] = r.grads[kept] + come[...]
                for copy in exchanges(unit, step + 1):
                    copy.start()
                return
            total = r.grads[kept].astype(FULL)
            if several:
                for other in range(3):
                    total = total + come[other].astype(FULL)
            else:
                total = total + come[...].astype(FULL)
            if unit < IN_UNIT:
                spot = unit - OUT_UNIT
                r.w_out_grad[spot * own_rows : (spot + 1) * own_rows, :] = total
                finished(0, r.w_out_grad)
            elif unit < ATTN_UNIT:
                spot = unit - IN_UNIT
                r.w_in_grad[:, spot * half : (spot + 1) * half] = total
                finished(1, r.w_in_grad)
            elif unit < QKV_UNIT:
                r.w_attn_out_grad[...] = total
                finished(2, r.w_attn_out_grad)
            elif unit < UNITS - 1:
                spot = unit - QKV_UNIT
                r.w_query_key_grad[:, spot * half : (spot + 1) * half] = total
                finished(3, r.w_query_key_grad)
            else:
                r.w_value_grad[...] = total
                finished(4, r.w_value_grad)

        def small_exchange(step):
            peer = partner if step == row_bits else (tower, jnp.bitwise_xor(row, 1 << step))
            return pltpu.make_async_remote_copy(
                src_ref=r.small.at[step],
                dst_ref=r.small_in.at[step],
                send_sem=r.small_send.at[0],
                recv_sem=r.small_recv.at[step],
                device_id=peer,
                device_id_type=MESH,
            )

        def small_finish(step):
            small_exchange(step).wait_recv()
            r.small[step + 1] = r.small[step] + r.small_in[step]
            if step < row_bits:
                small_exchange(step + 1).start()

        def keep(unit, value):
            value = value.astype(LOW)
            r.grads[unit] = value.reshape(r.grads.shape[1:]) if direct else value

        lane = lax.broadcasted_iota(jnp.int32, (8, width), 1)
        doc_row = jnp.where(lane < r.doc_lengths[0], 0, 1)
        seg_row = jnp.where(is_query, jnp.broadcast_to(r.query_segments[...], (8, width)), doc_row)
        eye = (
            lax.broadcasted_iota(jnp.int32, (width, width), 0)
            == lax.broadcasted_iota(jnp.int32, (width, width), 1)
        ).astype(FULL)
        seg_column = dot_nt(eye.astype(LOW), seg_row.astype(FULL).astype(LOW))[:, 0:1].astype(jnp.int32)
        member = (seg_row == lax.broadcasted_iota(jnp.int32, (8, width), 0)).astype(FULL)
        share = 1.0 / jnp.maximum(jnp.sum(member, axis=-1, keepdims=True), 1.0)

        wide = 2 * width
        table = jnp.concatenate(
            [r.bucket_table[...], jnp.zeros((1, 1), jnp.int32)], axis=1
        )
        turned = (
            lax.broadcasted_iota(jnp.int32, (wide, wide), 0)
            + lax.broadcasted_iota(jnp.int32, (wide, wide), 1)
            == wide - 2
        ).astype(FULL).astype(LOW)
        table_low = jnp.broadcast_to(table.astype(FULL), (8, wide)).astype(LOW)
        table_turned = dot(table_low, turned)[0:1]
        hot = (
            table_turned.astype(jnp.int32) == lax.broadcasted_iota(jnp.int32, (buckets, wide), 0)
        ).astype(FULL)
        r.hot[...] = hot.astype(LOW)
        bias_upper, bias_lower = split(r.rel_bias[...])
        bias_last = (r.rel_bias[...] - bias_upper.astype(FULL) - bias_lower.astype(FULL)).astype(LOW)
        hot_low = hot.astype(LOW)
        r.table[0:heads, :] = dot(bias_upper, hot_low) + dot(bias_lower, hot_low) + dot(bias_last, hot_low)

        allowed = seg_column == seg_row[0:1]

        def spread_bias(head, carry):
            line = jnp.broadcast_to(r.table[pl.ds(head, 1), :], (width, wide))
            bias = pltpu.roll(line, width + 1, 1, stride=1, stride_axis=0)[:, :width]
            r.bias[head] = jnp.where(allowed, bias, MASKED)
            return carry

        lax.fori_loop(0, heads, spread_bias, 0)
        r.small[0] = jnp.zeros((8, half), FULL)

        def note_gain(which, gain_grad):
            r.small[0, 2 * which : 2 * which + 1, :] = gain_grad[:, 0:half]
            r.small[0, 2 * which + 1 : 2 * which + 2, :] = gain_grad[:, half:]
        r.diagonals[...] = jnp.zeros_like(r.diagonals)

        inputs = r.tokens[...].astype(FULL)
        normed = (inputs * inverse_root(inputs) * r.gain_attn[...][None]).astype(LOW)
        r.normed_one[0:width, :] = normed
        loaded(0)
        w_query_key = r.w_query_key_here

        for start in range(0, 2 * model, TILE):
            columns = slice(start, start + TILE)
            r.qkv[:, columns] = dot(normed, w_query_key[:, columns]).astype(LOW)

        loaded(1)
        w_value = r.w_value_here
        r.qkv[:, 2 * model :] = dot(normed, w_value[...]).astype(LOW)

        r.keys_turned[...] = r.qkv[:, model : 2 * model].T
        r.values_turned[...] = r.qkv[:, 2 * model :].T

        place = lax.broadcasted_iota(jnp.int32, (width, 2 * head_size), 1)

        def attend(pair):
            start = pair * 2 * head_size
            query = r.qkv[:, start : start + 2 * head_size]
            key = r.qkv[:, model + start : model + start + 2 * head_size]
            for side in range(2):
                head = 2 * pair + side
                own = (place >= head_size) if side else (place < head_size)
                score = dot_nt(jnp.where(own, key, jnp.zeros_like(key)), query) + r.bias[head]
                weights = jnp.exp(score - jnp.max(score, axis=0, keepdims=True))
                r.probs[head] = (weights * (1.0 / jnp.sum(weights, axis=0, keepdims=True))).astype(LOW)

        def mix(pair):
            for head in (2 * pair, 2 * pair + 1):
                here = slice(head * head_size, (head + 1) * head_size)
                r.mixed_turned[here, :] = dot(r.values_turned[here, :], r.probs[head]).astype(LOW)

        for pair in range(heads // 2):
            attend(pair)
            if pair:
                mix(pair - 1)
        mix(heads // 2 - 1)

        mixed = r.mixed_turned[...].T
        r.mixed[0:width, :] = mixed
        pl.semaphore_wait(barrier, rows)
        send_one = to_partner(r.normed_one.at[0:width], r.normed_one.at[width : 2 * width], 0)
        send_one.start()
        send_mixed = to_partner(r.mixed.at[0:width], r.mixed.at[width : 2 * width], 1)
        send_mixed.start()
        loaded(2)
        w_attn_out = r.w_attn_out_here
        hidden = r.tokens[...].astype(FULL) + dot(mixed, w_attn_out[...])
        r.hidden_one[...] = hidden
        normed_two = (hidden * inverse_root(hidden) * r.gain_ff[...][None]).astype(LOW)
        r.normed_two[0:width, :] = normed_two
        send_two = to_partner(r.normed_two.at[0:width], r.normed_two.at[width : 2 * width], 2)
        send_two.start()

        loaded(3)
        w_in = r.w_in_here
        bend = math.sqrt(2.0 / math.pi)

        for start in range(0, ff, TILE):
            columns = slice(start, start + TILE)
            inner = dot(normed_two, w_in[:, columns])
            curve = jnp.tanh(inner * (bend + (bend * 0.044715) * (inner * inner)))
            r.inner[:, columns] = inner
            r.active[0:width, columns] = (inner * (0.5 + 0.5 * curve)).astype(LOW)

        send_active = to_partner(r.active.at[0:width], r.active.at[width : 2 * width], 3)
        send_active.start()
        loaded(4)
        w_out = r.w_out_here

        hidden = r.hidden_one[...] + dot(r.active[0:width, :], w_out[...])
        r.hidden_two[...] = hidden
        inverse_final = inverse_root(hidden)
        normed_upper, normed_lower = split(hidden * inverse_final * r.gain_final[...][None])
        member_low = member.astype(LOW)
        pooled = (dot(member_low, normed_upper) + dot(member_low, normed_lower)) * share
        pooled = pooled.astype(LOW).astype(FULL)

        own_queries = r.pooled_queries.at[pl.ds(pl.multiple_of(row * query_message, 16), query_message)]
        own_doc = r.pooled_docs.at[pl.ds(pl.multiple_of(row * doc_message, 16), doc_message)]
        r.stage[...] = jnp.zeros_like(r.stage)

        def spread(block, whole):
            for index in range(1, rows):
                pltpu.make_async_remote_copy(
                    src_ref=block,
                    dst_ref=block,
                    send_sem=r.spread_sem.at[0],
                    recv_sem=r.spread_sem.at[1],
                    device_id=(tower, jnp.bitwise_xor(row, rows - index)),
                    device_id_type=MESH,
                ).start()
            others = whole.at[0 : whole.shape[0] // rows * (rows - 1)]
            every = all_of(others, r.spread_sem.at[0], r.spread_sem.at[1])
            every.wait_send()
            every.wait_recv()

        relay_queries = to_partner(r.pooled_queries, r.pooled_queries, 4)
        relay_docs = to_partner(r.pooled_docs, r.pooled_docs, 5)

        @pl.when(is_query)
        def _():
            for part in range(parts):
                r.stage[part * per_row : (part + 1) * per_row, :] = pooled[
                    0:per_row, part * LANES : (part + 1) * LANES
                ]
            own_queries[...] = r.stage[...].astype(LOW)
            spread(own_queries, r.pooled_queries)
            relay_queries.start()
            relay_docs.wait_recv()
            relay_queries.wait_send()

        @pl.when(jnp.logical_not(is_query))
        def _():
            for part in range(parts):
                r.stage[part : part + 1, :] = pooled[0:1, part * LANES : (part + 1) * LANES]
            own_doc[...] = r.stage[0:doc_message, :].astype(LOW)
            spread(own_doc, r.pooled_docs)
            relay_docs.start()
            relay_queries.wait_recv()
            relay_docs.wait_send()

        r.queries_wide[...] = r.pooled_queries[...].astype(FULL)
        r.docs_wide[...] = r.pooled_docs[...].astype(FULL)

        for part in range(parts):
            lanes = slice(part * LANES, (part + 1) * LANES)
            for query in range(per_row):
                r.pooled[query * rows : (query + 1) * rows, lanes] = r.queries_wide[
                    pl.ds(part * per_row + query, rows, stride=query_message), :
                ]
            r.pooled[queries:, lanes] = r.docs_wide[pl.ds(part, rows, stride=doc_message), :]

        loaded(5)
        w_proj = r.w_proj_here
        pooled_low = r.pooled[...].astype(LOW)
        projected = dot(pooled_low, w_proj[...])
        scale = lax.rsqrt(jnp.sum(projected * projected, axis=-1, keepdims=True) + EPSILON)
        embed = (projected * scale).astype(LOW)
        query_embed, doc_embed = embed[:queries], embed[queries:]
        logits = LOGIT_SCALE * dot_nt(query_embed, doc_embed)
        target = jnp.concatenate(
            [
                (
                    jnp.broadcast_to(r.positives[query : query + 1, :].astype(FULL), (rows, rows)).T
                    == lax.broadcasted_iota(jnp.int32, (rows, rows), 1).astype(FULL)
                ).astype(FULL)
                for query in range(per_row)
            ],
            axis=0,
        )
        highest = jnp.max(logits, axis=-1, keepdims=True)
        log_sum = highest + jnp.log(jnp.sum(jnp.exp(logits - highest), axis=-1, keepdims=True))
        missed = log_sum - jnp.sum(logits * target, axis=-1, keepdims=True)
        r.loss[...] = jnp.sum(missed, axis=0, keepdims=True) / queries
        publish(r.loss)
        logits_grad = (jnp.exp(logits - log_sum) - target) * (LOGIT_SCALE / queries)
        grad_upper, grad_lower = split(logits_grad)
        embed_grad = jnp.concatenate(
            [
                dot(grad_upper, doc_embed) + dot(grad_lower, doc_embed),
                dot_tn(grad_upper, query_embed) + dot_tn(grad_lower, query_embed),
            ],
            axis=0,
        )
        along = jnp.sum(embed_grad * projected, axis=-1, keepdims=True)
        proj_grad = (scale * embed_grad - projected * (scale * scale * scale * along)).astype(LOW)
        r.proj_grad[...] = proj_grad.astype(FULL)
        r.own_grad[...] = jnp.zeros_like(r.own_grad)

        @pl.when(is_query)
        def _():
            for query in range(per_row):
                r.own_grad[query : query + 1, :] = r.proj_grad[pl.ds(query * rows + row, 1), :]

        @pl.when(jnp.logical_not(is_query))
        def _():
            r.own_grad[0:1, :] = r.proj_grad[pl.ds(queries + row, 1), :]

        pooled_grad = dot_nt(r.own_grad[...].astype(LOW), w_proj[...])[0:8] * share
        final_grad = jnp.zeros((width, model), FULL)
        for query in range(per_row):
            final_grad = jnp.where(seg_column == query, pooled_grad[query : query + 1, :], final_grad)

        hidden = r.hidden_two[...]
        hidden_grad, gain_grad = norm_backward(
            hidden, inverse_final, r.gain_final[...][None], final_grad
        )
        note_gain(2, gain_grad)
        r.hidden_grad[...] = hidden_grad
        r.branch[...] = hidden_grad.astype(LOW)
        own_half = pl.ds(pl.multiple_of(tower * half, LANES), half)
        other_half = pl.ds(pl.multiple_of((1 - tower) * half, LANES), half)
        send_branch = to_partner(r.branch.at[:, other_half], r.branch_half.at[width : 2 * width], 6)
        send_branch.start()
        r.branch_half[0:width, :] = r.branch[:, own_half]

        per_tile = model * rows // ff
        if direct:
            for half_step in range(2):
                pair = jnp.bitwise_xor(coordinate[Z_PAIR], 1 - half_step)
                spans = [pl.ds(pl.multiple_of((2 * half_z + pair) * model, model), model) for half_z in range(2)]
                if half_step == 0:
                    own_parts = [
                        dot_tn(r.active[0:width, span], r.branch_half[0:width, :]) for span in spans
                    ]
                    send_active.wait()
                    send_branch.wait()

                def tile(half_z):
                    if half_step == 0:
                        value = own_parts[half_z] + dot_tn(
                            r.active[width : 2 * width, spans[half_z]], r.branch_half[width : 2 * width, :]
                        )
                    else:
                        value = dot_tn(r.active[:, spans[half_z]], r.branch_half[...])
                    for unit in range(per_tile):
                        for spot in range(per_tile):
                            start = (spot * per_tile + unit) * own_rows
                            r.grads[unit, half_z, pair, spot // 2, spot % 2] = value[
                                start : start + own_rows, :
                            ].astype(LOW)

                for half_z in range(2):
                    tile(half_z)
                for unit in range(OUT_UNIT, IN_UNIT):
                    sends = exchanges(unit, 0)
                    if len(sends) == 2:
                        sends[half_step].start()
                    elif half_step == (Z_PAIR not in ORDERS[unit][0]):
                        for copy in sends:
                            copy.start()
        else:
            send_active.wait()
            send_branch.wait()

            @tiles(ff, model)
            def _(index, columns):
                keep(index, dot_tn(r.active[:, columns], r.branch_half[...]))

        pieces = []

        def then(body):
            pieces.append(body)
            return body

        def inner_back(index):
            columns = pl.ds(index * TILE, TILE)
            active_grad = dot_nt(r.branch[...], w_out[columns, :])
            inner = r.inner[:, columns]
            square = inner * inner
            curve = jnp.tanh(inner * (bend + (bend * 0.044715) * square))
            slope = (0.5 * inner) * (1.0 - curve * curve) * (bend + (bend * 3 * 0.044715) * square)
            r.inner_grad[:, columns] = (active_grad * ((0.5 + 0.5 * curve) + slope)).astype(LOW)

        for index in range(ff // TILE):
            then(functools.partial(inner_back, index))

        own_ff = pl.ds(pl.multiple_of(tower * ff_half, LANES), ff_half)
        other_ff = pl.ds(pl.multiple_of((1 - tower) * ff_half, LANES), ff_half)
        send_inner = to_partner(r.inner_grad.at[:, other_ff], r.inner_half.at[width : 2 * width], 7)
        send_attn = to_partner(r.attn.at[:, other_half], r.attn_half.at[width : 2 * width], 8)

        @then
        def _():
            send_inner.start()
            r.inner_half[0:width, :] = r.inner_grad[:, own_ff]
            r.normed_grad[...] = dot_nt(r.inner_grad[...], w_in[...])

        @then
        def _():
            hidden = r.hidden_one[...]
            through, gain_grad = norm_backward(
                hidden, inverse_root(hidden), r.gain_ff[...][None], r.normed_grad[...]
            )
            note_gain(1, gain_grad)
            hidden_grad = r.hidden_grad[...] + through
            r.hidden_grad[...] = hidden_grad
            r.attn[...] = hidden_grad.astype(LOW)
            send_attn.start()
            r.attn_half[0:width, :] = r.attn[:, own_half]
            send_two.wait()
            send_inner.wait()

        def in_grad(index):
            columns = pl.ds(index * half, half)
            keep(IN_UNIT + index, dot_tn(r.normed_two[...], r.inner_half[:, columns]))
            begin(IN_UNIT + index)

        for index in range(ATTN_UNIT - IN_UNIT):
            then(functools.partial(in_grad, index))

        @then
        def _():
            r.mixed_grad[...] = dot_nt(r.attn[...], w_attn_out[...]).astype(LOW)

        @then
        def _():
            send_mixed.wait()
            send_attn.wait()
            keep(ATTN_UNIT, dot_tn(r.mixed[...], r.attn_half[...]))
            begin(ATTN_UNIT)

        def attention_back(pair):
            columns = pl.ds(pl.multiple_of(pair * 2 * head_size, LANES), 2 * head_size)
            query = r.qkv[:, columns]
            value = r.qkv[:, pl.ds(pl.multiple_of(2 * model + pair * 2 * head_size, LANES), 2 * head_size)]
            mixed_grad = r.mixed_grad[:, columns]
            place = lax.broadcasted_iota(jnp.int32, (width, 2 * head_size), 1)
            key_sides, value_sides = [], []
            for side in range(2):
                head = 2 * pair + side
                own = (place >= head_size) if side else (place < head_size)
                prob_low = r.probs[head]
                prob = prob_low.astype(FULL)
                prob_grad = dot_nt(jnp.where(own, value, jnp.zeros_like(value)), mixed_grad)
                weighted = prob * prob_grad
                score_grad = weighted - prob * jnp.sum(weighted, axis=0, keepdims=True)
                score_low = score_grad.astype(LOW)
                key_sides.append(dot(score_low, query))
                value_sides.append(dot(prob_low, mixed_grad))
                here = pl.ds(pl.multiple_of(head * head_size, head_size), head_size)
                r.queries_turned[here, :] = dot(r.keys_turned[here, :], score_low).astype(LOW)
                r.score_grad[...] = score_grad
                total = jnp.zeros((8, wide), FULL)
                blank = jnp.zeros((8, wide - width), FULL)
                for block in range(width // 8):
                    line = jnp.concatenate([r.score_grad[8 * block : 8 * block + 8, :], blank], axis=1)
                    total = total + pltpu.roll(line, (wide + width - 1 - 8 * block) % wide, 1)
                for line in range(8):
                    r.diagonals[line, pl.ds(head, 1), :] = total[line : line + 1, :]
            after = place >= head_size
            r.qkv_grad[:, pl.ds(pl.multiple_of(model + pair * 2 * head_size, LANES), 2 * head_size)] = (
                jnp.where(after, key_sides[1], key_sides[0]).astype(LOW)
            )
            r.qkv_grad[:, pl.ds(pl.multiple_of(2 * model + pair * 2 * head_size, LANES), 2 * head_size)] = (
                jnp.where(after, value_sides[1], value_sides[0]).astype(LOW)
            )

        for pair in range(heads // 2):
            then(functools.partial(attention_back, pair))

        own_whole = pl.ds(pl.multiple_of(tower * model, LANES), model)
        other_whole = pl.ds(pl.multiple_of((1 - tower) * model, LANES), model)
        own_value = pl.ds(pl.multiple_of(2 * model + tower * half, LANES), half)
        other_value = pl.ds(pl.multiple_of(2 * model + (1 - tower) * half, LANES), half)
        send_qk = to_partner(
            r.qkv_grad.at[:, other_whole], r.qkv_half.at[width : 2 * width, 0:model], 9
        )
        send_value = to_partner(
            r.qkv_grad.at[:, other_value], r.qkv_half.at[width : 2 * width, model:], 10
        )

        @then
        def _():
            r.qkv_grad[:, 0:model] = r.queries_turned[...].T
            send_qk.start()
            send_value.start()
            r.qkv_half[0:width, 0:model] = r.qkv_grad[:, own_whole]
            r.qkv_half[0:width, model:] = r.qkv_grad[:, own_value]
            send_one.wait()
            send_qk.wait()
            send_value.wait()

        def qkv_back(index):
            columns = pl.ds(index * half, half)
            keep(QKV_UNIT + index, dot_tn(r.normed_one[...], r.qkv_half[:, columns]))
            begin(QKV_UNIT + index)

        for index in range(UNITS - QKV_UNIT):
            then(functools.partial(qkv_back, index))

        @then
        def _():
            normed_grad = dot_nt(r.qkv_grad[:, 0 : 2 * model], w_query_key[...])
            r.normed_grad[...] = normed_grad + dot_nt(r.qkv_grad[:, 2 * model :], w_value[...])

        @then
        def _():
            inputs = r.tokens[...].astype(FULL)
            through, gain_grad = norm_backward(
                inputs, inverse_root(inputs), r.gain_attn[...][None], r.normed_grad[...]
            )
            note_gain(0, gain_grad)
            r.tokens_grad[...] = r.hidden_grad[...] + through
            publish(r.tokens_grad)

            offsets = jnp.zeros((16, wide), FULL)
            for line in range(8):
                row_lines = r.diagonals[line]
                offsets = offsets + (pltpu.roll(row_lines, wide - line, 1) if line else row_lines)
            offset_upper, offset_lower = split(offsets)
            hot_low = r.hot[...]
            sums = dot_nt(offset_upper, hot_low) + dot_nt(offset_lower, hot_low)
            for head in range(heads):
                r.small[0, 6:7, head * buckets : (head + 1) * buckets] = sums[head : head + 1]
            small_exchange(0).start()

        @then
        def _():
            r.proj_grad_half[...] = r.proj_grad[:, own_half].astype(LOW)
            r.w_proj_whole[...] = dot_tn(r.pooled[...].astype(LOW), r.proj_grad_half[...])
            if direct:
                r.w_proj_grad[...] = r.w_proj_whole[pl.ds(pl.multiple_of(row * own_rows, 8), own_rows), :]
                publish(r.w_proj_grad)

        for index in range(len(pieces) + 1):
            if index:
                pieces[index - 1]()
            if direct:
                for event in PLAN[index]:
                    finish(*event)

        if not direct:
            for step in range(row_bits + 1):
                small_finish(step)
        total = row_bits + 1
        for which, result in enumerate((r.gain_attn_grad, r.gain_ff_grad, r.gain_final_grad)):
            result[0:half] = r.small[total, 2 * which]
            result[half:model] = r.small[total, 2 * which + 1]
        for head in range(heads):
            r.rel_bias_grad[head : head + 1, :] = r.small[total, 6:7, head * buckets : (head + 1) * buckets]
        for result in (r.gain_attn_grad, r.gain_ff_grad, r.gain_final_grad, r.rel_bias_grad):
            publish(result)
        if direct:
            sent = r.w_proj_whole.at[0 : (rows - 1) * own_rows // 2]
            for unit in range(UNITS):
                all_of(sent, r.sum_send.at[unit], r.sum_recv.at[unit, 0]).wait_send()
        all_of(r.small_in, r.small_send.at[0], r.small_recv.at[0]).wait_send()
        for copy in leaving:
            copy.wait()

    return kernel


def copy_out(*args):
    count = (len(args) - 2) // 3
    here = args[2 * count : 3 * count]
    ways = [
        (
            pltpu.make_async_copy(args[index], here[index], args[-2].at[index]),
            pltpu.make_async_copy(here[index], args[count + index], args[-1].at[index]),
        )
        for index in range(count)
    ]
    for come, _ in ways:
        come.start()
    for come, leave in ways:
        come.wait()
        leave.start()
    for _, leave in ways:
        leave.wait()


def on_device(rows):
    def step(
        tokens,
        query_segments,
        doc_lengths,
        bucket_table,
        positives,
        gain_attn,
        w_query_key,
        w_value,
        w_attn_out,
        rel_bias,
        gain_ff,
        w_in,
        w_out,
        gain_final,
        w_proj,
    ):
        width, model = tokens.shape[1:]
        ff = w_in.shape[1]
        buckets, heads = rel_bias.shape
        per_row = positives.shape[1]
        half = model // 2
        wide = 2 * width
        query_message = -(-per_row * model // LANES // 16) * 16
        queries = rows * per_row
        row_bits = rows.bit_length() - 1
        own_rows = model // rows
        vmem = pl.BlockSpec(memory_space=pltpu.VMEM)
        hbm = pl.BlockSpec(memory_space=pl.ANY)
        direct = in_kernel_sums(rows, model)
        inputs = dict(
            tokens=(tokens[0], pltpu.VMEM),
            query_segments=(query_segments, pltpu.VMEM),
            doc_lengths=(doc_lengths, pltpu.SMEM),
            bucket_table=(bucket_table[None], pltpu.VMEM),
            positives=(positives.T, pltpu.VMEM),
            gain_attn=(gain_attn, pltpu.VMEM),
            w_query_key=(w_query_key, None),
            w_value=(w_value, None),
            w_attn_out=(w_attn_out, None),
            rel_bias=(rel_bias.T, pltpu.VMEM),
            gain_ff=(gain_ff, pltpu.VMEM),
            w_in=(w_in, None),
            w_out=(w_out, None),
            gain_final=(gain_final, pltpu.VMEM),
            w_proj=(w_proj, None),
        )
        outputs = dict(
            loss=((1, 1), FULL),
            tokens_grad=((width, model), FULL),
            gain_attn_grad=((model,), FULL),
            gain_ff_grad=((model,), FULL),
            gain_final_grad=((model,), FULL),
            rel_bias_grad=((heads, buckets), FULL),
        )
        whole = ((model, half), FULL)
        if direct:
            outputs.update(
                w_query_key_grad=((own_rows, model), FULL),
                w_value_grad=((own_rows, half), FULL),
                w_attn_out_grad=((own_rows, half), FULL),
                w_in_grad=((own_rows, ff // 2), FULL),
                w_out_grad=((ff // rows, half), FULL),
                w_proj_grad=((own_rows, half), FULL),
            )
            held = dict(
                w_proj_whole=whole, grads=((UNITS,) + (2,) * row_bits + (own_rows, half), LOW)
            )
            arrived = []
            for steps in ORDERS:
                left = BITS
                for bits in steps:
                    left -= len(bits)
                    several = (3,) if len(bits) > 1 else ()
                    arrived.append(pltpu.VMEM(several + (2,) * left + (own_rows, half), LOW))
        else:
            outputs.update(w_proj_whole=whole, grads=((UNITS, model, half), LOW))
            held = {}
            arrived = []
        scratch = dict(
            w_query_key_here=(w_query_key.shape, LOW),
            w_value_here=(w_value.shape, LOW),
            w_attn_out_here=(w_attn_out.shape, LOW),
            w_in_here=(w_in.shape, LOW),
            w_out_here=(w_out.shape, LOW),
            w_proj_here=(w_proj.shape, LOW),
            hot=((buckets, wide), LOW),
            table=((16, wide), FULL),
            bias=((heads, width, width), FULL),
            normed_one=((2 * width, model), LOW),
            qkv=((width, 3 * model), LOW),
            keys_turned=((model, width), LOW),
            values_turned=((model, width), LOW),
            probs=((heads, width, width), LOW),
            mixed_turned=((model, width), LOW),
            mixed=((2 * width, model), LOW),
            hidden_one=((width, model), FULL),
            normed_two=((2 * width, model), LOW),
            active=((2 * width, ff), LOW),
            inner=((width, ff), FULL),
            hidden_two=((width, model), FULL),
            pooled_queries=((rows * query_message, LANES), LOW),
            pooled_docs=((rows * 16, LANES), LOW),
            queries_wide=((rows * query_message, LANES), FULL),
            docs_wide=((rows * 16, LANES), FULL),
            stage=((query_message, LANES), FULL),
            pooled=((queries + rows, model), FULL),
            proj_grad=((queries + rows, model), FULL),
            proj_grad_half=((queries + rows, half), LOW),
            own_grad=((16, model), FULL),
            hidden_grad=((width, model), FULL),
            branch=((width, model), LOW),
            branch_half=((2 * width, half), LOW),
            inner_grad=((width, ff), LOW),
            inner_half=((2 * width, ff // 2), LOW),
            normed_grad=((width, model), FULL),
            attn=((width, model), LOW),
            attn_half=((2 * width, half), LOW),
            mixed_grad=((width, model), LOW),
            score_grad=((width, width), FULL),
            diagonals=((8, 16, wide), FULL),
            queries_turned=((model, width), LOW),
            qkv_grad=((width, 3 * model), LOW),
            qkv_half=((2 * width, model + half), LOW),
            small=((row_bits + 2, 8, half), FULL),
            small_in=((row_bits + 1, 8, half), FULL),
        )
        scratch.update(held)
        semaphores = dict(
            load_sem=((len(inputs),)),
            core_send=((11,)),
            core_recv=((11,)),
            spread_sem=((2,)),
            small_send=((1,)),
            small_recv=((row_bits + 1,)),
            sum_send=((UNITS,)),
            leave_sem=(len(outputs),),
            sum_recv=((UNITS, BITS)),
        )
        names = [*inputs, *outputs, *scratch, *semaphores]
        small_inputs = [name for name, (_, place) in inputs.items() if place is not None]
        nears = [pltpu.VMEM(shape, kind) for shape, kind in outputs.values()] if direct else []
        sizes = (rows, width, model, ff, heads, buckets, per_row, len(inputs), len(outputs))
        results = pl.pallas_call(
            make_kernel(sizes, names, small_inputs),
            out_shape=[jax.ShapeDtypeStruct(shape, kind) for shape, kind in outputs.values()],
            in_specs=[hbm] * len(inputs),
            out_specs=[hbm if direct else vmem] * len(outputs),
            scratch_shapes=[pltpu.VMEM(shape, kind) for shape, kind in scratch.values()]
            + [pltpu.SemaphoreType.DMA(shape) for shape in semaphores.values()]
            + [inputs[name][1](inputs[name][0].shape, inputs[name][0].dtype) for name in small_inputs]
            + nears
            + arrived,
            compiler_params=pltpu.CompilerParams(
                collective_id=0,
                has_side_effects=True,
                vmem_limit_bytes=VMEM_LIMIT if direct else WIDER_VMEM_LIMIT,
            ),
        )(*[array for array, _ in inputs.values()])
        if direct:
            results = pl.pallas_call(
                copy_out,
                out_shape=[jax.ShapeDtypeStruct(shape, kind) for shape, kind in outputs.values()],
                in_specs=[hbm] * len(outputs),
                out_specs=[hbm] * len(outputs),
                scratch_shapes=nears + [pltpu.SemaphoreType.DMA((len(outputs),))] * 2,
            )(*results)
        r = SimpleNamespace(**dict(zip(outputs, results)))

        if not direct:
            rows_of = dict(scatter_dimension=0, tiled=True)
            r.w_out_grad = lax.psum_scatter(
                r.grads[:IN_UNIT].reshape(ff, half), "rows", **rows_of
            ).astype(FULL)
            others = r.grads[IN_UNIT:].transpose(1, 0, 2).reshape(model, -1)
            others = lax.psum_scatter(others, "rows", **rows_of).astype(FULL)
            r.w_in_grad = others[:, : ff // 2]
            r.w_attn_out_grad = others[:, ff // 2 : ff // 2 + half]
            r.w_query_key_grad = others[:, ff // 2 + half : ff // 2 + half + model]
            r.w_value_grad = others[:, ff // 2 + half + model :]
            r.w_proj_grad = lax.dynamic_slice_in_dim(
                r.w_proj_whole, lax.axis_index("rows") * own_rows, own_rows, 0
            )
        return (
            r.loss[0, 0],
            r.tokens_grad[None],
            r.gain_attn_grad,
            r.w_query_key_grad,
            r.w_value_grad,
            r.w_attn_out_grad,
            r.rel_bias_grad.T,
            r.gain_ff_grad,
            r.w_in_grad,
            r.w_out_grad,
            r.gain_final_grad,
            r.w_proj_grad,
        )

    return step


def solution(mesh):
    return jax.shard_map(
        on_device(mesh.shape["rows"]),
        mesh=mesh,
        in_specs=(P("tower", "rows", None), P("rows", None), P("rows")) + (P(),) * 12,
        out_specs=(
            P(),
            P("tower", "rows", None),
            P(),
            P("rows", "tower"),
            P("rows", "tower"),
            P("rows", "tower"),
            P(),
            P(),
            P("rows", "tower"),
            P("rows", "tower"),
            P(),
            P("rows", "tower"),
        ),
        check_vma=False,
    )
```

```python
import functools
import math
from types import SimpleNamespace

import jax
import jax.numpy as jnp
from jax import lax
from jax.experimental import pallas as pl
from jax.experimental.pallas import tpu as pltpu
from jax.sharding import PartitionSpec as P

EPSILON = 1e-06
LOGIT_SCALE = 50.0
MASKED = -1000000000.0
MESH = pl.DeviceIdType.MESH
LOW = jnp.bfloat16
FULL = jnp.float32
LANES = 128
TILE = 512
VMEM_LIMIT = 60 * 2**20
WIDER_VMEM_LIMIT = 62 * 2**20

Z_HALF, Z_PAIR, Y, X = range(4)
ORDERS = (
    ((X,), (Y,), (Z_PAIR, Z_HALF)),
    ((X,), (Y,), (Z_PAIR, Z_HALF)),
    ((Z_PAIR,), (Y,), (X,), (Z_HALF,)),
    ((Y,), (X,), (Z_PAIR,), (Z_HALF,)),
    ((Y,), (X,), (Z_PAIR,), (Z_HALF,)),
    ((Z_PAIR,), (X,), (Z_HALF,), (Y,)),
    ((X,), (Y,), (Z_PAIR,), (Z_HALF,)),
    ((Z_PAIR,), (X,), (Y,), (Z_HALF,)),
    ((Z_PAIR,), (X,), (Y,), (Z_HALF,)),
    ((X,), (Y,), (Z_PAIR,), (Z_HALF,)),
    ((Y,), (Z_PAIR,), (X, Z_HALF)),
    ((Y,), (X,), (Z_PAIR,), (Z_HALF,)),
)
PLAN = (
    (),
    (),
    (),
    (),
    (),
    (),
    (),
    (),
    (),
    (),
    (),
    ((2, 0), (3, 0),),
    (),
    (),
    (),
    (),
    ((0, 0),),
    (),
    (),
    (),
    (),
    ((1, 0), (4, 0), (5, 0),),
    (),
    (),
    (),
    ((2, 1),),
    (),
    ((6, 0), (0, 1), (7, 0), (3, 1), (1, 1), (4, 1), (8, 0), (5, 1), (0, 2), (10, 0), (3, 2), (1, 2), (9, 0), (4, 2), (11, 0), (2, 2), (12, 0), (5, 2), (6, 1), (10, 1), (7, 1), (3, 3), (4, 3), (9, 1), (2, 3), (12, 1), (8, 1), (5, 3), (6, 2), (7, 2), (11, 1), (8, 2), (9, 2), (12, 2), (10, 2), (6, 3), (7, 3), (11, 2), (8, 3), (9, 3), (12, 3), (12, 4), (11, 3),),
)
BITS = 4
OUT_UNIT, IN_UNIT, ATTN_UNIT, QKV_UNIT, UNITS = 0, 4, 8, 9, 12
SMALL = UNITS


def dot(left, right):
    return jnp.dot(left, right, preferred_element_type=FULL)


def dot_nt(left, right):
    return lax.dot_general(left, right, (((1,), (1,)), ((), ())), preferred_element_type=FULL)


def dot_tn(left, right):
    return lax.dot_general(left, right, (((0,), (0,)), ((), ())), preferred_element_type=FULL)


def split(values):
    upper = values.astype(LOW)
    return upper, (values - upper.astype(FULL)).astype(LOW)


def inverse_root(values):
    return lax.rsqrt(jnp.mean(values * values, axis=-1, keepdims=True) + EPSILON)


def norm_backward(values, inverse, gain, upstream):
    scaled = upstream * gain
    gain_grad = jnp.sum(upstream * (values * inverse), axis=0, keepdims=True)
    inner = jnp.mean(scaled * values, axis=-1, keepdims=True)
    return inverse * scaled - values * (inverse * inverse * inverse * inner), gain_grad


def tiles(total, size):
    def over(body):
        def step(index, carry):
            body(index, pl.ds(pl.multiple_of(index * size, size), size))
            return carry

        lax.fori_loop(0, total // size, step, 0)

    return over


def in_kernel_sums(rows, model):
    return rows == 2**BITS and model % (16 * rows) == 0


def make_kernel(sizes, names, small_inputs):
    rows, width, model, ff, heads, buckets, per_row, count_in, count_out = sizes
    head_size = model // heads
    half = model // 2
    ff_half = ff // 2
    assert heads * buckets <= half
    queries = rows * per_row
    parts = model // LANES
    query_message = -(-parts * per_row // 16) * 16
    doc_message = 16
    row_bits = rows.bit_length() - 1
    direct = in_kernel_sums(rows, model)

    def kernel(*args):
        r = SimpleNamespace(**dict(zip(names, args)))
        extra = args[len(names) :]
        near_inputs, extra = extra[: len(small_inputs)], extra[len(small_inputs) :]
        far_inputs = [getattr(r, name) for name in small_inputs]
        r.__dict__.update(zip(small_inputs, near_inputs))
        far_results = args[count_in : count_in + count_out]
        near_results = extra[:count_out]
        leaving = []
        if direct:
            r.__dict__.update(zip(names[count_in : count_in + count_out], near_results))

        def publish(result):
            if direct:
                index = next(index for index, ref in enumerate(near_results) if ref is result)
                copy = pltpu.make_async_copy(result, far_results[index], r.leave_sem.at[index])
                copy.start()
                leaving.append(copy)

        parts_left = [4, 4, 1, 2, 1]

        def finished(group, result):
            parts_left[group] -= 1
            if not parts_left[group]:
                publish(result)

        landing = []
        if direct:
            landings = iter(extra[count_out:])
            landing = [[next(landings) for _ in steps] for steps in ORDERS]
        tower = lax.axis_index("tower")
        row = lax.axis_index("rows")
        partner = (1 - tower, row)
        is_query = tower == 0
        own_rows = model // rows

        barrier = pltpu.get_barrier_semaphore()
        pl.semaphore_signal(barrier, inc=1, device_id=partner, device_id_type=MESH)

        def greet(step, carry):
            peer = (tower, jnp.bitwise_xor(row, step))
            pl.semaphore_signal(barrier, inc=1, device_id=peer, device_id_type=MESH)
            return carry

        lax.fori_loop(1, rows, greet, 0)

        loads = [
            pltpu.make_async_copy(far, near, r.load_sem.at[index])
            for index, (far, near) in enumerate(
                (
                    (r.w_query_key, r.w_query_key_here),
                    (r.w_value, r.w_value_here),
                    (r.w_attn_out, r.w_attn_out_here),
                    (r.w_in, r.w_in_here),
                    (r.w_out, r.w_out_here),
                    (r.w_proj, r.w_proj_here),
                    *zip(far_inputs, near_inputs),
                )
            )
        ]

        def load(index):
            loads[index].start()

        def loaded(index):
            loads[index].wait()

        for index in range(6, len(loads)):
            load(index)
        for index in range(6):
            load(index)
        for index in range(6, len(loads)):
            loaded(index)

        def to_partner(src, dst, index):
            return pltpu.make_async_remote_copy(
                src_ref=src,
                dst_ref=dst,
                send_sem=r.core_send.at[index],
                recv_sem=r.core_recv.at[index],
                device_id=partner,
                device_id_type=MESH,
            )

        coordinate = [jnp.bitwise_and(lax.shift_right_logical(row, 3 - bit), 1) for bit in range(BITS)]

        def piece(unit, step, code):
            place = [slice(None)] * BITS
            for bits in ORDERS[unit][:step]:
                for bit in bits:
                    place[bit] = coordinate[bit]
            for spot, bit in enumerate(ORDERS[unit][step]):
                place[bit] = jnp.bitwise_xor(coordinate[bit], (code >> spot) & 1)
            return place

        def exchange(unit, step, code, half=None):
            place = piece(unit, step, code)
            into = landing[unit][step]
            if len(ORDERS[unit][step]) > 1:
                into = into.at[code - 1]
            elif half is not None:
                pair_step, half_z = half
                place[Z_HALF] = half_z
                if Z_PAIR in ORDERS[unit][step]:
                    into = into.at[half_z]
                else:
                    place[Z_PAIR] = jnp.bitwise_xor(coordinate[Z_PAIR], 1 - pair_step)
                    into = into.at[half_z, place[Z_PAIR]]
            peer = row
            for spot, bit in enumerate(ORDERS[unit][step]):
                peer = jnp.bitwise_xor(peer, ((code >> spot) & 1) << (3 - bit))
            return pltpu.make_async_remote_copy(
                src_ref=r.grads.at[(unit, *place)],
                dst_ref=into,
                send_sem=r.sum_send.at[unit],
                recv_sem=r.sum_recv.at[unit, step],
                device_id=(tower, peer),
                device_id_type=MESH,
            )

        def exchanges(unit, step):
            bits = ORDERS[unit][step]
            if step == 0 and unit < IN_UNIT and bits in ((X,), (Y,), (Z_PAIR,)):
                pair_steps = range(1 if Z_PAIR in bits else 2)
                return [exchange(unit, step, 1, (pair, half_z)) for pair in pair_steps for half_z in range(2)]
            return [exchange(unit, step, code) for code in range(1, 2 ** len(bits))]

        def all_of(ref, send_sem, recv_sem):
            return pltpu.make_async_remote_copy(
                src_ref=ref,
                dst_ref=ref,
                send_sem=send_sem,
                recv_sem=recv_sem,
                device_id=partner,
                device_id_type=MESH,
            )

        def begin(unit):
            if direct:
                for copy in exchanges(unit, 0):
                    copy.start()

        def finish(unit, step):
            if unit == SMALL:
                small_finish(step)
                return
            all_of(landing[unit][step], r.sum_send.at[unit], r.sum_recv.at[unit, step]).wait_recv()
            kept = (unit, *piece(unit, step, 0))
            come = landing[unit][step]
            several = len(ORDERS[unit][step]) > 1
            if step + 1 < len(ORDERS[unit]):
                if several:
                    total = r.grads[kept].astype(FULL)
                    for other in range(3):
                        total = total + come[other].astype(FULL)
                    r.grads[kept] = total.astype(LOW)
                else:
                    r.grads[kept] = r.grads[kept] + come[...]
                for copy in exchanges(unit, step + 1):
                    copy.start()
                return
            total = r.grads[kept].astype(FULL)
            if several:
                for other in range(3):
                    total = total + come[other].astype(FULL)
            else:
                total = total + come[...].astype(FULL)
            if unit < IN_UNIT:
                spot = unit - OUT_UNIT
                r.w_out_grad[spot * own_rows : (spot + 1) * own_rows, :] = total
                finished(0, r.w_out_grad)
            elif unit < ATTN_UNIT:
                spot = unit - IN_UNIT
                r.w_in_grad[:, spot * half : (spot + 1) * half] = total
                finished(1, r.w_in_grad)
            elif unit < QKV_UNIT:
                r.w_attn_out_grad[...] = total
                finished(2, r.w_attn_out_grad)
            elif unit < UNITS - 1:
                spot = unit - QKV_UNIT
                r.w_query_key_grad[:, spot * half : (spot + 1) * half] = total
                finished(3, r.w_query_key_grad)
            else:
                r.w_value_grad[...] = total
                finished(4, r.w_value_grad)

        def small_exchange(step):
            peer = partner if step == row_bits else (tower, jnp.bitwise_xor(row, 1 << step))
            return pltpu.make_async_remote_copy(
                src_ref=r.small.at[step],
                dst_ref=r.small_in.at[step],
                send_sem=r.small_send.at[0],
                recv_sem=r.small_recv.at[step],
                device_id=peer,
                device_id_type=MESH,
            )

        def small_finish(step):
            small_exchange(step).wait_recv()
            r.small[step + 1] = r.small[step] + r.small_in[step]
            if step < row_bits:
                small_exchange(step + 1).start()

        def keep(unit, value):
            value = value.astype(LOW)
            r.grads[unit] = value.reshape(r.grads.shape[1:]) if direct else value

        lane = lax.broadcasted_iota(jnp.int32, (8, width), 1)
        doc_row = jnp.where(lane < r.doc_lengths[0], 0, 1)
        seg_row = jnp.where(is_query, jnp.broadcast_to(r.query_segments[...], (8, width)), doc_row)
        eye = (
            lax.broadcasted_iota(jnp.int32, (width, width), 0)
            == lax.broadcasted_iota(jnp.int32, (width, width), 1)
        ).astype(FULL)
        seg_column = dot_nt(eye.astype(LOW), seg_row.astype(FULL).astype(LOW))[:, 0:1].astype(jnp.int32)
        member = (seg_row == lax.broadcasted_iota(jnp.int32, (8, width), 0)).astype(FULL)
        share = 1.0 / jnp.maximum(jnp.sum(member, axis=-1, keepdims=True), 1.0)

        wide = 2 * width
        table = jnp.concatenate(
            [r.bucket_table[...], jnp.zeros((1, 1), jnp.int32)], axis=1
        )
        turned = (
            lax.broadcasted_iota(jnp.int32, (wide, wide), 0)
            + lax.broadcasted_iota(jnp.int32, (wide, wide), 1)
            == wide - 2
        ).astype(FULL).astype(LOW)
        table_low = jnp.broadcast_to(table.astype(FULL), (8, wide)).astype(LOW)
        table_turned = dot(table_low, turned)[0:1]
        hot = (
            table_turned.astype(jnp.int32) == lax.broadcasted_iota(jnp.int32, (buckets, wide), 0)
        ).astype(FULL)
        r.hot[...] = hot.astype(LOW)
        bias_upper, bias_lower = split(r.rel_bias[...])
        bias_last = (r.rel_bias[...] - bias_upper.astype(FULL) - bias_lower.astype(FULL)).astype(LOW)
        hot_low = hot.astype(LOW)
        r.table[0:heads, :] = dot(bias_upper, hot_low) + dot(bias_lower, hot_low) + dot(bias_last, hot_low)

        allowed = seg_column == seg_row[0:1]

        def spread_bias(head, carry):
            line = jnp.broadcast_to(r.table[pl.ds(head, 1), :], (width, wide))
            bias = pltpu.roll(line, width + 1, 1, stride=1, stride_axis=0)[:, :width]
            r.bias[head] = jnp.where(allowed, bias, MASKED)
            return carry

        lax.fori_loop(0, heads, spread_bias, 0)
        r.small[0] = jnp.zeros((8, half), FULL)

        def note_gain(which, gain_grad):
            r.small[0, 2 * which : 2 * which + 1, :] = gain_grad[:, 0:half]
            r.small[0, 2 * which + 1 : 2 * which + 2, :] = gain_grad[:, half:]
        r.diagonals[...] = jnp.zeros_like(r.diagonals)

        inputs = r.tokens[...].astype(FULL)
        normed = (inputs * inverse_root(inputs) * r.gain_attn[...][None]).astype(LOW)
        r.normed_one[0:width, :] = normed
        loaded(0)
        w_query_key = r.w_query_key_here

        for start in range(0, 2 * model, TILE):
            columns = slice(start, start + TILE)
            r.qkv[:, columns] = dot(normed, w_query_key[:, columns]).astype(LOW)

        loaded(1)
        w_value = r.w_value_here
        r.qkv[:, 2 * model :] = dot(normed, w_value[...]).astype(LOW)

        r.keys_turned[...] = r.qkv[:, model : 2 * model].T
        r.values_turned[...] = r.qkv[:, 2 * model :].T

        place = lax.broadcasted_iota(jnp.int32, (width, 2 * head_size), 1)

        def attend(pair):
            start = pair * 2 * head_size
            query = r.qkv[:, start : start + 2 * head_size]
            key = r.qkv[:, model + start : model + start + 2 * head_size]
            for side in range(2):
                head = 2 * pair + side
                own = (place >= head_size) if side else (place < head_size)
                score = dot_nt(jnp.where(own, key, jnp.zeros_like(key)), query) + r.bias[head]
                weights = jnp.exp(score - jnp.max(score, axis=0, keepdims=True))
                r.probs[head] = (weights * (1.0 / jnp.sum(weights, axis=0, keepdims=True))).astype(LOW)

        def mix(pair):
            for head in (2 * pair, 2 * pair + 1):
                here = slice(head * head_size, (head + 1) * head_size)
                r.mixed_turned[here, :] = dot(r.values_turned[here, :], r.probs[head]).astype(LOW)

        for pair in range(heads // 2):
            attend(pair)
            if pair:
                mix(pair - 1)
        mix(heads // 2 - 1)

        mixed = r.mixed_turned[...].T
        r.mixed[0:width, :] = mixed
        pl.semaphore_wait(barrier, rows)
        send_one = to_partner(r.normed_one.at[0:width], r.normed_one.at[width : 2 * width], 0)
        send_one.start()
        send_mixed = to_partner(r.mixed.at[0:width], r.mixed.at[width : 2 * width], 1)
        send_mixed.start()
        loaded(2)
        w_attn_out = r.w_attn_out_here
        hidden = r.tokens[...].astype(FULL) + dot(mixed, w_attn_out[...])
        r.hidden_one[...] = hidden
        normed_two = (hidden * inverse_root(hidden) * r.gain_ff[...][None]).astype(LOW)
        r.normed_two[0:width, :] = normed_two
        send_two = to_partner(r.normed_two.at[0:width], r.normed_two.at[width : 2 * width], 2)
        send_two.start()

        loaded(3)
        w_in = r.w_in_here
        bend = math.sqrt(2.0 / math.pi)

        for start in range(0, ff, TILE):
            columns = slice(start, start + TILE)
            inner = dot(normed_two, w_in[:, columns])
            curve = jnp.tanh(inner * (bend + (bend * 0.044715) * (inner * inner)))
            r.inner[:, columns] = inner
            r.active[0:width, columns] = (inner * (0.5 + 0.5 * curve)).astype(LOW)

        send_active = to_partner(r.active.at[0:width], r.active.at[width : 2 * width], 3)
        send_active.start()
        loaded(4)
        w_out = r.w_out_here

        hidden = r.hidden_one[...] + dot(r.active[0:width, :], w_out[...])
        r.hidden_two[...] = hidden
        inverse_final = inverse_root(hidden)
        normed_upper, normed_lower = split(hidden * inverse_final * r.gain_final[...][None])
        member_low = member.astype(LOW)
        pooled = (dot(member_low, normed_upper) + dot(member_low, normed_lower)) * share
        pooled = pooled.astype(LOW).astype(FULL)

        own_queries = r.pooled_queries.at[pl.ds(pl.multiple_of(row * query_message, 16), query_message)]
        own_doc = r.pooled_docs.at[pl.ds(pl.multiple_of(row * doc_message, 16), doc_message)]
        r.stage[...] = jnp.zeros_like(r.stage)

        def spread(block, whole):
            for index in range(1, rows):
                pltpu.make_async_remote_copy(
                    src_ref=block,
                    dst_ref=block,
                    send_sem=r.spread_sem.at[0],
                    recv_sem=r.spread_sem.at[1],
                    device_id=(tower, jnp.bitwise_xor(row, rows - index)),
                    device_id_type=MESH,
                ).start()
            others = whole.at[0 : whole.shape[0] // rows * (rows - 1)]
            every = all_of(others, r.spread_sem.at[0], r.spread_sem.at[1])
            every.wait_send()
            every.wait_recv()

        relay_queries = to_partner(r.pooled_queries, r.pooled_queries, 4)
        relay_docs = to_partner(r.pooled_docs, r.pooled_docs, 5)

        @pl.when(is_query)
        def _():
            for part in range(parts):
                r.stage[part * per_row : (part + 1) * per_row, :] = pooled[
                    0:per_row, part * LANES : (part + 1) * LANES
                ]
            own_queries[...] = r.stage[...].astype(LOW)
            spread(own_queries, r.pooled_queries)
            relay_queries.start()
            relay_docs.wait_recv()
            relay_queries.wait_send()

        @pl.when(jnp.logical_not(is_query))
        def _():
            for part in range(parts):
                r.stage[part : part + 1, :] = pooled[0:1, part * LANES : (part + 1) * LANES]
            own_doc[...] = r.stage[0:doc_message, :].astype(LOW)
            spread(own_doc, r.pooled_docs)
            relay_docs.start()
            relay_queries.wait_recv()
            relay_docs.wait_send()

        r.queries_wide[...] = r.pooled_queries[...].astype(FULL)
        r.docs_wide[...] = r.pooled_docs[...].astype(FULL)

        for part in range(parts):
            lanes = slice(part * LANES, (part + 1) * LANES)
            for query in range(per_row):
                r.pooled[query * rows : (query + 1) * rows, lanes] = r.queries_wide[
                    pl.ds(part * per_row + query, rows, stride=query_message), :
                ]
            r.pooled[queries:, lanes] = r.docs_wide[pl.ds(part, rows, stride=doc_message), :]

        loaded(5)
        w_proj = r.w_proj_here
        pooled_low = r.pooled[...].astype(LOW)
        projected = dot(pooled_low, w_proj[...])
        scale = lax.rsqrt(jnp.sum(projected * projected, axis=-1, keepdims=True) + EPSILON)
        embed = (projected * scale).astype(LOW)
        query_embed, doc_embed = embed[:queries], embed[queries:]
        logits = LOGIT_SCALE * dot_nt(query_embed, doc_embed)
        target = jnp.concatenate(
            [
                (
                    jnp.broadcast_to(r.positives[query : query + 1, :].astype(FULL), (rows, rows)).T
                    == lax.broadcasted_iota(jnp.int32, (rows, rows), 1).astype(FULL)
                ).astype(FULL)
                for query in range(per_row)
            ],
            axis=0,
        )
        highest = jnp.max(logits, axis=-1, keepdims=True)
        log_sum = highest + jnp.log(jnp.sum(jnp.exp(logits - highest), axis=-1, keepdims=True))
        missed = log_sum - jnp.sum(logits * target, axis=-1, keepdims=True)
        r.loss[...] = jnp.sum(missed, axis=0, keepdims=True) / queries
        publish(r.loss)
        logits_grad = (jnp.exp(logits - log_sum) - target) * (LOGIT_SCALE / queries)
        grad_upper, grad_lower = split(logits_grad)
        embed_grad = jnp.concatenate(
            [
                dot(grad_upper, doc_embed) + dot(grad_lower, doc_embed),
                dot_tn(grad_upper, query_embed) + dot_tn(grad_lower, query_embed),
            ],
            axis=0,
        )
        along = jnp.sum(embed_grad * projected, axis=-1, keepdims=True)
        proj_grad = (scale * embed_grad - projected * (scale * scale * scale * along)).astype(LOW)
        r.proj_grad[...] = proj_grad.astype(FULL)
        r.own_grad[...] = jnp.zeros_like(r.own_grad)

        @pl.when(is_query)
        def _():
            for query in range(per_row):
                r.own_grad[query : query + 1, :] = r.proj_grad[pl.ds(query * rows + row, 1), :]

        @pl.when(jnp.logical_not(is_query))
        def _():
            r.own_grad[0:1, :] = r.proj_grad[pl.ds(queries + row, 1), :]

        pooled_grad = dot_nt(r.own_grad[...].astype(LOW), w_proj[...])[0:8] * share
        final_grad = jnp.zeros((width, model), FULL)
        for query in range(per_row):
            final_grad = jnp.where(seg_column == query, pooled_grad[query : query + 1, :], final_grad)

        hidden = r.hidden_two[...]
        hidden_grad, gain_grad = norm_backward(
            hidden, inverse_final, r.gain_final[...][None], final_grad
        )
        note_gain(2, gain_grad)
        r.hidden_grad[...] = hidden_grad
        r.branch[...] = hidden_grad.astype(LOW)
        own_half = pl.ds(pl.multiple_of(tower * half, LANES), half)
        other_half = pl.ds(pl.multiple_of((1 - tower) * half, LANES), half)
        send_branch = to_partner(r.branch.at[:, other_half], r.branch_half.at[width : 2 * width], 6)
        send_branch.start()
        r.branch_half[0:width, :] = r.branch[:, own_half]

        per_tile = model * rows // ff
        if direct:
            for half_step in range(2):
                pair = jnp.bitwise_xor(coordinate[Z_PAIR], 1 - half_step)
                spans = [pl.ds(pl.multiple_of((2 * half_z + pair) * model, model), model) for half_z in range(2)]
                if half_step == 0:
                    own_parts = [
                        dot_tn(r.active[0:width, span], r.branch_half[0:width, :]) for span in spans
                    ]
                    send_active.wait()
                    send_branch.wait()

                def tile(half_z):
                    if half_step == 0:
                        value = own_parts[half_z] + dot_tn(
                            r.active[width : 2 * width, spans[half_z]], r.branch_half[width : 2 * width, :]
                        )
                    else:
                        value = dot_tn(r.active[:, spans[half_z]], r.branch_half[...])
                    for unit in range(per_tile):
                        for spot in range(per_tile):
                            start = (spot * per_tile + unit) * own_rows
                            r.grads[unit, half_z, pair, spot // 2, spot % 2] = value[
                                start : start + own_rows, :
                            ].astype(LOW)

                for half_z in range(2):
                    tile(half_z)
                    for unit in range(OUT_UNIT, IN_UNIT):
                        sends = exchanges(unit, 0)
                        at = 2 * half_step + half_z
                        if len(ORDERS[unit][0]) == 1:
                            if at < len(sends):
                                sends[at].start()
                        elif at == 3:
                            for copy in sends:
                                copy.start()
        else:
            send_active.wait()
            send_branch.wait()

            @tiles(ff, model)
            def _(index, columns):
                keep(index, dot_tn(r.active[:, columns], r.branch_half[...]))

        pieces = []

        def then(body):
            pieces.append(body)
            return body

        def inner_back(index):
            columns = pl.ds(index * TILE, TILE)
            active_grad = dot_nt(r.branch[...], w_out[columns, :])
            inner = r.inner[:, columns]
            square = inner * inner
            curve = jnp.tanh(inner * (bend + (bend * 0.044715) * square))
            slope = (0.5 * inner) * (1.0 - curve * curve) * (bend + (bend * 3 * 0.044715) * square)
            r.inner_grad[:, columns] = (active_grad * ((0.5 + 0.5 * curve) + slope)).astype(LOW)

        for index in range(ff // TILE):
            then(functools.partial(inner_back, index))

        own_ff = pl.ds(pl.multiple_of(tower * ff_half, LANES), ff_half)
        other_ff = pl.ds(pl.multiple_of((1 - tower) * ff_half, LANES), ff_half)
        send_inner = to_partner(r.inner_grad.at[:, other_ff], r.inner_half.at[width : 2 * width], 7)
        send_attn = to_partner(r.attn.at[:, other_half], r.attn_half.at[width : 2 * width], 8)

        @then
        def _():
            send_inner.start()
            r.inner_half[0:width, :] = r.inner_grad[:, own_ff]
            r.normed_grad[...] = dot_nt(r.inner_grad[...], w_in[...])

        @then
        def _():
            hidden = r.hidden_one[...]
            through, gain_grad = norm_backward(
                hidden, inverse_root(hidden), r.gain_ff[...][None], r.normed_grad[...]
            )
            note_gain(1, gain_grad)
            hidden_grad = r.hidden_grad[...] + through
            r.hidden_grad[...] = hidden_grad
            r.attn[...] = hidden_grad.astype(LOW)
            send_attn.start()
            r.attn_half[0:width, :] = r.attn[:, own_half]
            send_two.wait()
            send_inner.wait()

        def in_grad(index):
            columns = pl.ds(index * half, half)
            keep(IN_UNIT + index, dot_tn(r.normed_two[...], r.inner_half[:, columns]))
            begin(IN_UNIT + index)

        for index in range(ATTN_UNIT - IN_UNIT):
            then(functools.partial(in_grad, index))

        @then
        def _():
            r.mixed_grad[...] = dot_nt(r.attn[...], w_attn_out[...]).astype(LOW)

        @then
        def _():
            send_mixed.wait()
            send_attn.wait()
            keep(ATTN_UNIT, dot_tn(r.mixed[...], r.attn_half[...]))
            begin(ATTN_UNIT)

        def attention_back(pair):
            columns = pl.ds(pl.multiple_of(pair * 2 * head_size, LANES), 2 * head_size)
            query = r.qkv[:, columns]
            value = r.qkv[:, pl.ds(pl.multiple_of(2 * model + pair * 2 * head_size, LANES), 2 * head_size)]
            mixed_grad = r.mixed_grad[:, columns]
            place = lax.broadcasted_iota(jnp.int32, (width, 2 * head_size), 1)
            key_sides, value_sides = [], []
            for side in range(2):
                head = 2 * pair + side
                own = (place >= head_size) if side else (place < head_size)
                prob_low = r.probs[head]
                prob = prob_low.astype(FULL)
                prob_grad = dot_nt(jnp.where(own, value, jnp.zeros_like(value)), mixed_grad)
                weighted = prob * prob_grad
                score_grad = weighted - prob * jnp.sum(weighted, axis=0, keepdims=True)
                score_low = score_grad.astype(LOW)
                key_sides.append(dot(score_low, query))
                value_sides.append(dot(prob_low, mixed_grad))
                here = pl.ds(pl.multiple_of(head * head_size, head_size), head_size)
                r.queries_turned[here, :] = dot(r.keys_turned[here, :], score_low).astype(LOW)
                r.score_grad[...] = score_grad
                total = jnp.zeros((8, wide), FULL)
                blank = jnp.zeros((8, wide - width), FULL)
                for block in range(width // 8):
                    line = jnp.concatenate([r.score_grad[8 * block : 8 * block + 8, :], blank], axis=1)
                    total = total + pltpu.roll(line, (wide + width - 1 - 8 * block) % wide, 1)
                for line in range(8):
                    r.diagonals[line, pl.ds(head, 1), :] = total[line : line + 1, :]
            after = place >= head_size
            r.qkv_grad[:, pl.ds(pl.multiple_of(model + pair * 2 * head_size, LANES), 2 * head_size)] = (
                jnp.where(after, key_sides[1], key_sides[0]).astype(LOW)
            )
            r.qkv_grad[:, pl.ds(pl.multiple_of(2 * model + pair * 2 * head_size, LANES), 2 * head_size)] = (
                jnp.where(after, value_sides[1], value_sides[0]).astype(LOW)
            )

        for pair in range(heads // 2):
            then(functools.partial(attention_back, pair))

        own_whole = pl.ds(pl.multiple_of(tower * model, LANES), model)
        other_whole = pl.ds(pl.multiple_of((1 - tower) * model, LANES), model)
        own_value = pl.ds(pl.multiple_of(2 * model + tower * half, LANES), half)
        other_value = pl.ds(pl.multiple_of(2 * model + (1 - tower) * half, LANES), half)
        send_qk = to_partner(
            r.qkv_grad.at[:, other_whole], r.qkv_half.at[width : 2 * width, 0:model], 9
        )
        send_value = to_partner(
            r.qkv_grad.at[:, other_value], r.qkv_half.at[width : 2 * width, model:], 10
        )

        @then
        def _():
            r.qkv_grad[:, 0:model] = r.queries_turned[...].T
            send_qk.start()
            send_value.start()
            r.qkv_half[0:width, 0:model] = r.qkv_grad[:, own_whole]
            r.qkv_half[0:width, model:] = r.qkv_grad[:, own_value]
            send_one.wait()
            send_qk.wait()
            send_value.wait()

        def qkv_back(index):
            columns = pl.ds(index * half, half)
            keep(QKV_UNIT + index, dot_tn(r.normed_one[...], r.qkv_half[:, columns]))
            begin(QKV_UNIT + index)

        for index in range(UNITS - QKV_UNIT):
            then(functools.partial(qkv_back, index))

        @then
        def _():
            normed_grad = dot_nt(r.qkv_grad[:, 0 : 2 * model], w_query_key[...])
            r.normed_grad[...] = normed_grad + dot_nt(r.qkv_grad[:, 2 * model :], w_value[...])

        @then
        def _():
            inputs = r.tokens[...].astype(FULL)
            through, gain_grad = norm_backward(
                inputs, inverse_root(inputs), r.gain_attn[...][None], r.normed_grad[...]
            )
            note_gain(0, gain_grad)
            r.tokens_grad[...] = r.hidden_grad[...] + through
            publish(r.tokens_grad)

            offsets = jnp.zeros((16, wide), FULL)
            for line in range(8):
                row_lines = r.diagonals[line]
                offsets = offsets + (pltpu.roll(row_lines, wide - line, 1) if line else row_lines)
            offset_upper, offset_lower = split(offsets)
            hot_low = r.hot[...]
            sums = dot_nt(offset_upper, hot_low) + dot_nt(offset_lower, hot_low)
            for head in range(heads):
                r.small[0, 6:7, head * buckets : (head + 1) * buckets] = sums[head : head + 1]
            small_exchange(0).start()

        @then
        def _():
            r.proj_grad_half[...] = r.proj_grad[:, own_half].astype(LOW)
            r.w_proj_whole[...] = dot_tn(r.pooled[...].astype(LOW), r.proj_grad_half[...])
            if direct:
                r.w_proj_grad[...] = r.w_proj_whole[pl.ds(pl.multiple_of(row * own_rows, 8), own_rows), :]
                publish(r.w_proj_grad)

        for index in range(len(pieces) + 1):
            if index:
                pieces[index - 1]()
            if direct:
                for event in PLAN[index]:
                    finish(*event)

        if not direct:
            for step in range(row_bits + 1):
                small_finish(step)
        total = row_bits + 1
        for which, result in enumerate((r.gain_attn_grad, r.gain_ff_grad, r.gain_final_grad)):
            result[0:half] = r.small[total, 2 * which]
            result[half:model] = r.small[total, 2 * which + 1]
        for head in range(heads):
            r.rel_bias_grad[head : head + 1, :] = r.small[total, 6:7, head * buckets : (head + 1) * buckets]
        for result in (r.gain_attn_grad, r.gain_ff_grad, r.gain_final_grad, r.rel_bias_grad):
            publish(result)
        if direct:
            sent = r.w_proj_whole.at[0 : (rows - 1) * own_rows // 2]
            for unit in range(UNITS):
                all_of(sent, r.sum_send.at[unit], r.sum_recv.at[unit, 0]).wait_send()
        all_of(r.small_in, r.small_send.at[0], r.small_recv.at[0]).wait_send()
        for copy in leaving:
            copy.wait()

    return kernel


def copy_out(*args):
    count = (len(args) - 2) // 3
    here = args[2 * count : 3 * count]
    ways = [
        (
            pltpu.make_async_copy(args[index], here[index], args[-2].at[index]),
            pltpu.make_async_copy(here[index], args[count + index], args[-1].at[index]),
        )
        for index in range(count)
    ]
    for come, _ in ways:
        come.start()
    for come, leave in ways:
        come.wait()
        leave.start()
    for _, leave in ways:
        leave.wait()


def on_device(rows):
    def step(
        tokens,
        query_segments,
        doc_lengths,
        bucket_table,
        positives,
        gain_attn,
        w_query_key,
        w_value,
        w_attn_out,
        rel_bias,
        gain_ff,
        w_in,
        w_out,
        gain_final,
        w_proj,
    ):
        width, model = tokens.shape[1:]
        ff = w_in.shape[1]
        buckets, heads = rel_bias.shape
        per_row = positives.shape[1]
        half = model // 2
        wide = 2 * width
        query_message = -(-per_row * model // LANES // 16) * 16
        queries = rows * per_row
        row_bits = rows.bit_length() - 1
        own_rows = model // rows
        vmem = pl.BlockSpec(memory_space=pltpu.VMEM)
        hbm = pl.BlockSpec(memory_space=pl.ANY)
        direct = in_kernel_sums(rows, model)
        inputs = dict(
            tokens=(tokens[0], pltpu.VMEM),
            query_segments=(query_segments, pltpu.VMEM),
            doc_lengths=(doc_lengths, pltpu.SMEM),
            bucket_table=(bucket_table[None], pltpu.VMEM),
            positives=(positives.T, pltpu.VMEM),
            gain_attn=(gain_attn, pltpu.VMEM),
            w_query_key=(w_query_key, None),
            w_value=(w_value, None),
            w_attn_out=(w_attn_out, None),
            rel_bias=(rel_bias.T, pltpu.VMEM),
            gain_ff=(gain_ff, pltpu.VMEM),
            w_in=(w_in, None),
            w_out=(w_out, None),
            gain_final=(gain_final, pltpu.VMEM),
            w_proj=(w_proj, None),
        )
        outputs = dict(
            loss=((1, 1), FULL),
            tokens_grad=((width, model), FULL),
            gain_attn_grad=((model,), FULL),
            gain_ff_grad=((model,), FULL),
            gain_final_grad=((model,), FULL),
            rel_bias_grad=((heads, buckets), FULL),
        )
        whole = ((model, half), FULL)
        if direct:
            outputs.update(
                w_query_key_grad=((own_rows, model), FULL),
                w_value_grad=((own_rows, half), FULL),
                w_attn_out_grad=((own_rows, half), FULL),
                w_in_grad=((own_rows, ff // 2), FULL),
                w_out_grad=((ff // rows, half), FULL),
                w_proj_grad=((own_rows, half), FULL),
            )
            held = dict(
                w_proj_whole=whole, grads=((UNITS,) + (2,) * row_bits + (own_rows, half), LOW)
            )
            arrived = []
            for steps in ORDERS:
                left = BITS
                for bits in steps:
                    left -= len(bits)
                    several = (3,) if len(bits) > 1 else ()
                    arrived.append(pltpu.VMEM(several + (2,) * left + (own_rows, half), LOW))
        else:
            outputs.update(w_proj_whole=whole, grads=((UNITS, model, half), LOW))
            held = {}
            arrived = []
        scratch = dict(
            w_query_key_here=(w_query_key.shape, LOW),
            w_value_here=(w_value.shape, LOW),
            w_attn_out_here=(w_attn_out.shape, LOW),
            w_in_here=(w_in.shape, LOW),
            w_out_here=(w_out.shape, LOW),
            w_proj_here=(w_proj.shape, LOW),
            hot=((buckets, wide), LOW),
            table=((16, wide), FULL),
            bias=((heads, width, width), FULL),
            normed_one=((2 * width, model), LOW),
            qkv=((width, 3 * model), LOW),
            keys_turned=((model, width), LOW),
            values_turned=((model, width), LOW),
            probs=((heads, width, width), LOW),
            mixed_turned=((model, width), LOW),
            mixed=((2 * width, model), LOW),
            hidden_one=((width, model), FULL),
            normed_two=((2 * width, model), LOW),
            active=((2 * width, ff), LOW),
            inner=((width, ff), FULL),
            hidden_two=((width, model), FULL),
            pooled_queries=((rows * query_message, LANES), LOW),
            pooled_docs=((rows * 16, LANES), LOW),
            queries_wide=((rows * query_message, LANES), FULL),
            docs_wide=((rows * 16, LANES), FULL),
            stage=((query_message, LANES), FULL),
            pooled=((queries + rows, model), FULL),
            proj_grad=((queries + rows, model), FULL),
            proj_grad_half=((queries + rows, half), LOW),
            own_grad=((16, model), FULL),
            hidden_grad=((width, model), FULL),
            branch=((width, model), LOW),
            branch_half=((2 * width, half), LOW),
            inner_grad=((width, ff), LOW),
            inner_half=((2 * width, ff // 2), LOW),
            normed_grad=((width, model), FULL),
            attn=((width, model), LOW),
            attn_half=((2 * width, half), LOW),
            mixed_grad=((width, model), LOW),
            score_grad=((width, width), FULL),
            diagonals=((8, 16, wide), FULL),
            queries_turned=((model, width), LOW),
            qkv_grad=((width, 3 * model), LOW),
            qkv_half=((2 * width, model + half), LOW),
            small=((row_bits + 2, 8, half), FULL),
            small_in=((row_bits + 1, 8, half), FULL),
        )
        scratch.update(held)
        semaphores = dict(
            load_sem=((len(inputs),)),
            core_send=((11,)),
            core_recv=((11,)),
            spread_sem=((2,)),
            small_send=((1,)),
            small_recv=((row_bits + 1,)),
            sum_send=((UNITS,)),
            leave_sem=(len(outputs),),
            sum_recv=((UNITS, BITS)),
        )
        names = [*inputs, *outputs, *scratch, *semaphores]
        small_inputs = [name for name, (_, place) in inputs.items() if place is not None]
        nears = [pltpu.VMEM(shape, kind) for shape, kind in outputs.values()] if direct else []
        sizes = (rows, width, model, ff, heads, buckets, per_row, len(inputs), len(outputs))
        results = pl.pallas_call(
            make_kernel(sizes, names, small_inputs),
            out_shape=[jax.ShapeDtypeStruct(shape, kind) for shape, kind in outputs.values()],
            in_specs=[hbm] * len(inputs),
            out_specs=[hbm if direct else vmem] * len(outputs),
            scratch_shapes=[pltpu.VMEM(shape, kind) for shape, kind in scratch.values()]
            + [pltpu.SemaphoreType.DMA(shape) for shape in semaphores.values()]
            + [inputs[name][1](inputs[name][0].shape, inputs[name][0].dtype) for name in small_inputs]
            + nears
            + arrived,
            compiler_params=pltpu.CompilerParams(
                collective_id=0,
                has_side_effects=True,
                vmem_limit_bytes=VMEM_LIMIT if direct else WIDER_VMEM_LIMIT,
            ),
        )(*[array for array, _ in inputs.values()])
        if direct:
            results = pl.pallas_call(
                copy_out,
                out_shape=[jax.ShapeDtypeStruct(shape, kind) for shape, kind in outputs.values()],
                in_specs=[hbm] * len(outputs),
                out_specs=[hbm] * len(outputs),
                scratch_shapes=nears + [pltpu.SemaphoreType.DMA((len(outputs),))] * 2,
            )(*results)
        r = SimpleNamespace(**dict(zip(outputs, results)))

        if not direct:
            rows_of = dict(scatter_dimension=0, tiled=True)
            r.w_out_grad = lax.psum_scatter(
                r.grads[:IN_UNIT].reshape(ff, half), "rows", **rows_of
            ).astype(FULL)
            others = r.grads[IN_UNIT:].transpose(1, 0, 2).reshape(model, -1)
            others = lax.psum_scatter(others, "rows", **rows_of).astype(FULL)
            r.w_in_grad = others[:, : ff // 2]
            r.w_attn_out_grad = others[:, ff // 2 : ff // 2 + half]
            r.w_query_key_grad = others[:, ff // 2 + half : ff // 2 + half + model]
            r.w_value_grad = others[:, ff // 2 + half + model :]
            r.w_proj_grad = lax.dynamic_slice_in_dim(
                r.w_proj_whole, lax.axis_index("rows") * own_rows, own_rows, 0
            )
        return (
            r.loss[0, 0],
            r.tokens_grad[None],
            r.gain_attn_grad,
            r.w_query_key_grad,
            r.w_value_grad,
            r.w_attn_out_grad,
            r.rel_bias_grad.T,
            r.gain_ff_grad,
            r.w_in_grad,
            r.w_out_grad,
            r.gain_final_grad,
            r.w_proj_grad,
        )

    return step


def solution(mesh):
    return jax.shard_map(
        on_device(mesh.shape["rows"]),
        mesh=mesh,
        in_specs=(P("tower", "rows", None), P("rows", None), P("rows")) + (P(),) * 12,
        out_specs=(
            P(),
            P("tower", "rows", None),
            P(),
            P("rows", "tower"),
            P("rows", "tower"),
            P("rows", "tower"),
            P(),
            P(),
            P("rows", "tower"),
            P("rows", "tower"),
            P(),
            P("rows", "tower"),
        ),
        check_vma=False,
    )
```
